32 devices in a mesh: ka: 2 (over core), fft: 16 (over z, y, x).
Axes of the slice: x: 2, y: 2, z: 4, core: 2. Of those that a mesh axis runs over, the one named last changes fastest.
Arguments:
- orbitals: float32 [2, 1, 2, 128, 128, 128], P('ka', None, None, 'fft'), may hold values from -3 to 3
- costate: float32 [2, 1, 2, 128, 128, 128], P('ka', None, None, 'fft'), may hold values from -6 to 6
- potential: float32 [128, 128, 128], P('fft'), may hold values from -4 to 4
- xc_kernel: float32 [128, 128, 128], P('fft'), may hold values from -1 to -0.1
- vector_potential: float32 [8], replicated, may hold values from -0.6 to 0.6
- kpoint_weight: int32 [2], replicated, may hold values from 1 to 8
- occupation: int32 [1], replicated, may hold values from 100 to 200
Outputs:
- adjoint_out: float32 [2, 1, 2, 128, 128, 128], P('ka', None, None, 'fft')
- cross_potential: float32 [128, 128, 128], P('fft')
The draws below stay inside these ranges and needn't reach their ends.
Inputs may be any that keep to these rules, and one draw needn't show every extreme that they name: `kpoint_weight`: symmetry multiplicities of the k-points.
All inputs are finite; a program needn't handle non-finite values.
Results may differ from the reference program's by a relative error of at most 0.0003.
Values sent between devices are 32-bit elements; how exact they have to be, the bound alone decides.
No kernel may reach another device: no remote copies, remote signals or barrier semaphores. Data moves between devices by JAX's collectives and lax.ppermute only.
A program may use at most 192 MiB of HBM per device.

```python
import math
import jax
import jax.numpy as jnp

N = 128
BANDS = 1
STEPS = 2
SUB = 4
KPTS = 2


def steps_of(key, dims, cuts, least, largest):
    level, own = 1.0, jax.random.fold_in(key, 6)
    for dim, blocks in cuts:
        heights = jnp.exp(jax.random.uniform(jax.random.fold_in(own, dim), (blocks,), jnp.float32, least / len(cuts), largest / len(cuts)))
        level = level * jnp.repeat(heights, dims[dim] // blocks).reshape([-1 if axis == dim else 1 for axis in range(len(dims))])
    return level


def scatter_about(rng, extent, width, limit, split=(), dtype=jnp.bfloat16):
    factor_of = steps_of(rng, extent, split, -0.22, 0.18) if split else 1.0
    entries = jax.random.normal(rng, extent, jnp.float32) * width * factor_of
    return jnp.minimum(jnp.maximum(entries, -limit), limit).astype(dtype)


def setup_inputs(seed: int = 0) -> dict:
    splits = jax.random.split(jax.random.key(seed), 8)
    return {
        "orbitals": scatter_about(splits[0], (KPTS, BANDS, 2, N, N, N), 0.5, 3.0, ((0, 2), (3, 16)), jnp.float32),
        "costate": scatter_about(splits[1], (KPTS, BANDS, 2, N, N, N), 1.0, 6.0, ((0, 2), (3, 16)), jnp.float32),
        "potential": scatter_about(splits[2], (N, N, N), 1.0, 4.0, ((0, 16),), jnp.float32),
        "xc_kernel": jnp.clip(-1.0 + 0.9 * jax.random.uniform(splits[3], (N, N, N), jnp.float32) ** steps_of(splits[3], (N, N, N), ((0, 16),), -0.2, 0.2), -1.0, -0.1),
        "vector_potential": jnp.clip(jax.random.uniform(splits[4], (STEPS * SUB,), jnp.float32, -0.6, 0.6), -0.6, 0.6),
        "kpoint_weight": jax.random.randint(splits[5], (KPTS,), 1, 9).astype(jnp.int32),
        "occupation": jax.random.randint(splits[6], (BANDS,), 100, 201).astype(jnp.int32),
    }


spacing = 0.25
step_time = 0.6


def wave_numbers(grid_size):
    grid_line = jnp.arange(grid_size)
    signed_line = jnp.where(grid_line < grid_size // 2, grid_line, grid_line - grid_size)
    return (2.0 * math.pi / (grid_size * spacing)) * signed_line.astype(jnp.float32)


def substep(field, potential, shift_x, shift_y, shift_z, numbers, push_value, time_sign):
    sub_time = step_time / SUB
    potential_phase = jnp.exp(-1j * time_sign * (0.5 * sub_time) * potential)
    field = field * potential_phase
    spectrum = jnp.fft.fftn(field, axes=(-3, -2, -1))
    along_x = shift_x[:, None, None, None] + numbers[None, :, None, None] + push_value
    along_y = shift_y + numbers[None, None, :, None]
    along_z = shift_z + numbers[None, None, None, :]
    kinetic_angle = (0.5 * sub_time) * (along_x * along_x + along_y * along_y + along_z * along_z)
    spectrum = spectrum * jnp.exp(-1j * time_sign * kinetic_angle)[:, None]
    field = jnp.fft.ifftn(spectrum, axes=(-3, -2, -1))
    return field * potential_phase


def reference(orbitals, costate, potential, xc_kernel, vector_potential, kpoint_weight, occupation):
    lattice_unit = 2.0 * math.pi / (N * spacing)
    k_points = jnp.arange(KPTS).astype(jnp.float32)
    shift_x = lattice_unit * ((k_points + 0.5) / KPTS - 0.5)
    shift_y = lattice_unit * 0.25
    shift_z = -lattice_unit * 0.25
    numbers = wave_numbers(N)
    orbital_field = orbitals[:, :, 0] + 1j * orbitals[:, :, 1]
    history = [orbital_field]
    for step_index in range(STEPS):
        for sub_index in range(SUB):
            orbital_field = substep(orbital_field, potential, shift_x, shift_y, shift_z, numbers,
                                    vector_potential[step_index * SUB + sub_index], 1.0)
        history.append(orbital_field)
    weight = kpoint_weight.astype(jnp.float32) / jnp.sum(kpoint_weight).astype(jnp.float32)
    occupied = occupation.astype(jnp.float32) / 100.0
    band_factor = 2.0 * weight[:, None] * occupied[None, :]
    g_squared = (numbers[:, None, None] * numbers[:, None, None] + numbers[None, :, None] * numbers[None, :, None]
                 + numbers[None, None, :] * numbers[None, None, :])
    coulomb = jnp.where(g_squared > 0, 4.0 * math.pi / jnp.where(g_squared > 0, g_squared, 1.0), 0.0)
    adjoint_field = costate[:, :, 0] + 1j * costate[:, :, 1]
    cross_pot = jnp.zeros_like(potential)
    for step_index in range(STEPS - 1, -1, -1):
        forward_field = history[step_index + 1]
        intersection = jnp.real(adjoint_field) * jnp.real(forward_field) + jnp.imag(adjoint_field) * jnp.imag(forward_field)
        density = jnp.sum(band_factor[:, :, None, None, None] * intersection, axis=(0, 1))
        hartree_pot = jnp.real(jnp.fft.ifftn(coulomb * jnp.fft.fftn(density)))
        cross_pot = hartree_pot + xc_kernel * density
        adjoint_field = adjoint_field - 1j * step_time * cross_pot * forward_field
        for sub_index in range(SUB - 1, -1, -1):
            adjoint_field = substep(adjoint_field, potential, shift_x, shift_y, shift_z, numbers,
                                    vector_potential[step_index * SUB + sub_index], -1.0)
    result_field = jnp.stack([jnp.real(adjoint_field), jnp.imag(adjoint_field)], axis=2)
    return result_field, cross_pot
```

```python
import math

import jax
import jax.numpy as jnp
from jax import lax
from jax.sharding import PartitionSpec as P

STEPS = 2
SUB = 4


spacing = 0.25
step_time = 0.6
sub_time = step_time / SUB
highest = lax.Precision.HIGHEST


def wave_numbers(grid_line, grid_size):
    signed_line = jnp.where(grid_line < grid_size // 2, grid_line, grid_line - grid_size)
    return 2.0 * math.pi / (grid_size * spacing) * signed_line.astype(jnp.float32)


def table_angles(grid_size):
    row_index = lax.broadcasted_iota(jnp.int32, (grid_size, grid_size), 0)
    col_index = lax.broadcasted_iota(jnp.int32, (grid_size, grid_size), 1)
    return 2.0 * math.pi / grid_size * (row_index * col_index % grid_size).astype(jnp.float32)


def line_matrices(shifts, grid_size):
    numbers = wave_numbers(lax.iota(jnp.int32, grid_size), grid_size)
    along = shifts[:, None] + numbers[None, :]
    phase = 0.5 * sub_time * (along * along)
    angles = table_angles(grid_size)
    cosine, sine = jnp.cos(angles), jnp.sin(angles)
    q_real, q_imag = jnp.cos(phase)[:, None, :], -jnp.sin(phase)[:, None, :]
    left_real = (cosine * q_real - sine * q_imag) / grid_size
    left_imag = (cosine * q_imag + sine * q_real) / grid_size
    both = jnp.stack([left_real, left_imag])
    by_cos = jnp.einsum("csam,mb->csab", both, cosine, precision=highest)
    by_sin = jnp.einsum("csam,mb->csab", both, sine, precision=highest)
    return by_cos[0] + by_sin[1], by_cos[1] - by_sin[0]


def real_form(real_part, imag_part):
    upper = jnp.stack([real_part, -imag_part], axis=-2)
    lower = jnp.stack([imag_part, real_part], axis=-2)
    return jnp.stack([upper, lower], axis=-4)


def spin(field, angle):
    cosine, sine = jnp.cos(angle), jnp.sin(angle)
    return jnp.stack(
        [field[0] * cosine + field[1] * sine, field[1] * cosine - field[0] * sine]
    )


def apply(form, matrix, field):
    return jnp.einsum(
        form, matrix, field, precision=lax.Precision.HIGHEST, preferred_element_type=jnp.float32
    )


def plain(orbitals, costate, potential, xc_kernel, vector_potential, kpoint_weight, occupation):
    grid_size = potential.shape[1]
    k_index = lax.axis_index("ka")
    fft_index = lax.axis_index("fft")
    planes = potential.shape[0]
    lattice_unit = 2.0 * math.pi / (grid_size * spacing)
    k_fraction = (k_index.astype(jnp.float32) + 0.5) / lax.axis_size("ka") - 0.5
    shifts = jnp.concatenate(
        [
            lattice_unit * k_fraction + vector_potential,
            jnp.array([lattice_unit * 0.25, -lattice_unit * 0.25], jnp.float32),
        ]
    )
    lines = real_form(*line_matrices(shifts, grid_size))
    back = jnp.transpose(lines, (0, 3, 4, 1, 2))

    def to_columns(field, split, concat):
        return lax.all_to_all(field, "fft", split_axis=split, concat_axis=concat, tiled=True)

    pot_rows = 0.5 * sub_time * potential
    pot_cols = to_columns(pot_rows, 1, 0)

    def propagate(field, step_index, sign):
        table = lines if sign > 0 else back
        order = range(SUB) if sign > 0 else range(SUB - 1, -1, -1)
        mat_y, mat_z = table[STEPS * SUB], table[STEPS * SUB + 1]
        in_rows = True
        field = spin(field, sign * pot_rows)
        for count, sub_index in enumerate(order):
            mat_x = table[step_index * SUB + sub_index]
            last = count == SUB - 1
            turn = sign * (1.0 if last else 2.0)
            field = apply("cadb,dkxyb->ckxya", mat_z, field)
            if in_rows:
                field = apply("cadb,dkxbz->ckxaz", mat_y, field)
                field = to_columns(field, 3, 2)
                field = apply("cadb,dkbyz->ckayz", mat_x, field)
                field = spin(field, turn * pot_cols)
            else:
                field = apply("cadb,dkbyz->ckayz", mat_x, field)
                field = to_columns(field, 2, 3)
                field = apply("cadb,dkxbz->ckxaz", mat_y, field)
                field = spin(field, turn * pot_rows)
            in_rows = not in_rows
        return field

    def parts_first(field):
        bands = field.shape[0] * field.shape[1]
        return jnp.moveaxis(field, 2, 0).reshape((2, bands) + field.shape[3:])

    angles = table_angles(grid_size)
    cas = (jnp.cos(angles) + jnp.sin(angles)) / math.sqrt(grid_size)
    numbers = wave_numbers(lax.iota(jnp.int32, grid_size), grid_size)
    numbers_local = wave_numbers(fft_index * planes + lax.iota(jnp.int32, planes), grid_size)
    g_squared = (
        (numbers * numbers)[:, None, None]
        + (numbers_local * numbers_local)[None, :, None]
        + (numbers * numbers)[None, None, :]
    )
    coulomb = jnp.where(
        g_squared > 0, 4.0 * math.pi / jnp.where(g_squared > 0, g_squared, 1.0), 0.0
    )
    orbital = parts_first(orbitals)
    history = [orbital]
    for step_index in range(STEPS):
        orbital = propagate(orbital, step_index, 1.0)
        history.append(orbital)
    occupied = occupation.astype(jnp.float32) / 100.0
    own_weight = lax.dynamic_slice_in_dim(kpoint_weight, k_index, 1)[0].astype(jnp.float32)
    weight = own_weight / jnp.sum(kpoint_weight).astype(jnp.float32)
    band_factor = 2.0 * weight * occupied
    adjoint = parts_first(costate)
    cross_pot = jnp.zeros_like(potential)
    for step_index in range(STEPS - 1, -1, -1):
        forward = history[step_index + 1]
        density = lax.psum(
            jnp.sum(band_factor[:, None, None, None] * jnp.sum(adjoint * forward, axis=0), axis=0),
            "ka",
        )
        hartree = apply("ab,xyb->xya", cas, density)
        hartree = apply("ab,xbz->xaz", cas, hartree)
        hartree = to_columns(hartree, 1, 0)
        hartree = apply("ab,byz->ayz", cas, hartree)
        hartree = apply("ab,byz->ayz", cas, hartree * coulomb)
        hartree = to_columns(hartree, 0, 1)
        hartree = apply("ab,xbz->xaz", cas, hartree)
        hartree = apply("ab,xyb->xya", cas, hartree)
        cross_pot = hartree + xc_kernel * density
        turned = jnp.stack([forward[1], -forward[0]])
        adjoint = propagate(adjoint + step_time * cross_pot * turned, step_index, -1.0)
    result = jnp.moveaxis(adjoint.reshape((2,) + orbitals.shape[:2] + adjoint.shape[2:]), 0, 2)
    return (result, cross_pot)


def solution(mesh):
    placed = (
        P("ka", None, None, "fft", None, None),
        P("ka", None, None, "fft", None, None),
        P("fft", None, None),
        P("fft", None, None),
        P(),
        P(),
        P(),
    )
    return jax.shard_map(
        plain,
        mesh=mesh,
        in_specs=placed,
        out_specs=(P("ka", None, None, "fft", None, None), P("fft", None, None)),
        check_vma=False,
    )
```

```python
import functools
import math

import jax
import jax.numpy as jnp
from jax import lax
from jax.experimental import pallas as pl
from jax.experimental.pallas import tpu as pltpu
from jax.sharding import PartitionSpec as P

STEPS = 2
SUB = 4


spacing = 0.25
step_time = 0.6
sub_time = step_time / SUB
highest = lax.Precision.HIGHEST


def wave_numbers(grid_line, grid_size):
    signed_line = jnp.where(grid_line < grid_size // 2, grid_line, grid_line - grid_size)
    return 2.0 * math.pi / (grid_size * spacing) * signed_line.astype(jnp.float32)


def table_angles(grid_size):
    row_index = lax.broadcasted_iota(jnp.int32, (grid_size, grid_size), 0)
    col_index = lax.broadcasted_iota(jnp.int32, (grid_size, grid_size), 1)
    return 2.0 * math.pi / grid_size * (row_index * col_index % grid_size).astype(jnp.float32)


def line_matrices(shifts, grid_size):
    numbers = wave_numbers(lax.iota(jnp.int32, grid_size), grid_size)
    along = shifts[:, None] + numbers[None, :]
    phase = 0.5 * sub_time * (along * along)
    angles = table_angles(grid_size)
    cosine, sine = jnp.cos(angles), jnp.sin(angles)
    q_real, q_imag = jnp.cos(phase)[:, None, :], -jnp.sin(phase)[:, None, :]
    left_real = (cosine * q_real - sine * q_imag) / grid_size
    left_imag = (cosine * q_imag + sine * q_real) / grid_size
    both = jnp.stack([left_real, left_imag])
    by_cos = jnp.einsum("csam,mb->csab", both, cosine, precision=highest)
    by_sin = jnp.einsum("csam,mb->csab", both, sine, precision=highest)
    return by_cos[0] + by_sin[1], by_cos[1] - by_sin[0]


def real_form(real_part, imag_part):
    upper = jnp.stack([real_part, -imag_part], axis=-2)
    lower = jnp.stack([imag_part, real_part], axis=-2)
    return jnp.stack([upper, lower], axis=-4)


def spin(field, angle):
    cosine, sine = jnp.cos(angle), jnp.sin(angle)
    return jnp.stack(
        [field[0] * cosine + field[1] * sine, field[1] * cosine - field[0] * sine]
    )


def apply(form, matrix, field):
    return jnp.einsum(
        form, matrix, field, precision=lax.Precision.HIGHEST, preferred_element_type=jnp.float32
    )


def plain(orbitals, costate, potential, xc_kernel, vector_potential, kpoint_weight, occupation):
    grid_size = potential.shape[1]
    k_index = lax.axis_index("ka")
    fft_index = lax.axis_index("fft")
    planes = potential.shape[0]
    lattice_unit = 2.0 * math.pi / (grid_size * spacing)
    k_fraction = (k_index.astype(jnp.float32) + 0.5) / lax.axis_size("ka") - 0.5
    shifts = jnp.concatenate(
        [
            lattice_unit * k_fraction + vector_potential,
            jnp.array([lattice_unit * 0.25, -lattice_unit * 0.25], jnp.float32),
        ]
    )
    lines = real_form(*line_matrices(shifts, grid_size))
    back = jnp.transpose(lines, (0, 3, 4, 1, 2))

    def to_columns(field, split, concat):
        return lax.all_to_all(field, "fft", split_axis=split, concat_axis=concat, tiled=True)

    pot_rows = 0.5 * sub_time * potential
    pot_cols = to_columns(pot_rows, 1, 0)

    def propagate(field, step_index, sign):
        table = lines if sign > 0 else back
        order = range(SUB) if sign > 0 else range(SUB - 1, -1, -1)
        mat_y, mat_z = table[STEPS * SUB], table[STEPS * SUB + 1]
        in_rows = True
        field = spin(field, sign * pot_rows)
        for count, sub_index in enumerate(order):
            mat_x = table[step_index * SUB + sub_index]
            last = count == SUB - 1
            turn = sign * (1.0 if last else 2.0)
            field = apply("cadb,dkxyb->ckxya", mat_z, field)
            if in_rows:
                field = apply("cadb,dkxbz->ckxaz", mat_y, field)
                field = to_columns(field, 3, 2)
                field = apply("cadb,dkbyz->ckayz", mat_x, field)
                field = spin(field, turn * pot_cols)
            else:
                field = apply("cadb,dkbyz->ckayz", mat_x, field)
                field = to_columns(field, 2, 3)
                field = apply("cadb,dkxbz->ckxaz", mat_y, field)
                field = spin(field, turn * pot_rows)
            in_rows = not in_rows
        return field

    def parts_first(field):
        bands = field.shape[0] * field.shape[1]
        return jnp.moveaxis(field, 2, 0).reshape((2, bands) + field.shape[3:])

    angles = table_angles(grid_size)
    cas = (jnp.cos(angles) + jnp.sin(angles)) / math.sqrt(grid_size)
    numbers = wave_numbers(lax.iota(jnp.int32, grid_size), grid_size)
    numbers_local = wave_numbers(fft_index * planes + lax.iota(jnp.int32, planes), grid_size)
    g_squared = (
        (numbers * numbers)[:, None, None]
        + (numbers_local * numbers_local)[None, :, None]
        + (numbers * numbers)[None, None, :]
    )
    coulomb = jnp.where(
        g_squared > 0, 4.0 * math.pi / jnp.where(g_squared > 0, g_squared, 1.0), 0.0
    )
    orbital = parts_first(orbitals)
    history = [orbital]
    for step_index in range(STEPS):
        orbital = propagate(orbital, step_index, 1.0)
        history.append(orbital)
    occupied = occupation.astype(jnp.float32) / 100.0
    own_weight = lax.dynamic_slice_in_dim(kpoint_weight, k_index, 1)[0].astype(jnp.float32)
    weight = own_weight / jnp.sum(kpoint_weight).astype(jnp.float32)
    band_factor = 2.0 * weight * occupied
    adjoint = parts_first(costate)
    cross_pot = jnp.zeros_like(potential)
    for step_index in range(STEPS - 1, -1, -1):
        forward = history[step_index + 1]
        density = lax.psum(
            jnp.sum(band_factor[:, None, None, None] * jnp.sum(adjoint * forward, axis=0), axis=0),
            "ka",
        )
        hartree = apply("ab,xyb->xya", cas, density)
        hartree = apply("ab,xbz->xaz", cas, hartree)
        hartree = to_columns(hartree, 1, 0)
        hartree = apply("ab,byz->ayz", cas, hartree)
        hartree = apply("ab,byz->ayz", cas, hartree * coulomb)
        hartree = to_columns(hartree, 0, 1)
        hartree = apply("ab,xbz->xaz", cas, hartree)
        hartree = apply("ab,xyb->xya", cas, hartree)
        cross_pot = hartree + xc_kernel * density
        turned = jnp.stack([forward[1], -forward[0]])
        adjoint = propagate(adjoint + step_time * cross_pot * turned, step_index, -1.0)
    result = jnp.moveaxis(adjoint.reshape((2,) + orbitals.shape[:2] + adjoint.shape[2:]), 0, 2)
    return (result, cross_pot)


ROWS = 128
PLANES = 8
AXES = ("ka", "fft")


def halves_of(value):
    high = value.astype(jnp.bfloat16)
    return high, (value - high.astype(jnp.float32)).astype(jnp.bfloat16)


def from_left(table, field):
    high, low = halves_of(field)
    return jnp.dot(
        table, jnp.concatenate([high, low, high], axis=0), preferred_element_type=jnp.float32
    )


def from_right(field, table):
    high, low = halves_of(field)
    return jnp.dot(
        jnp.concatenate([high, low, high], axis=1), table, preferred_element_type=jnp.float32
    )


def side_table(matrix, axis):
    high = lax.reduce_precision(matrix, 8, 7)
    low = (matrix - high).astype(jnp.bfloat16)
    high = high.astype(jnp.bfloat16)
    return jnp.concatenate([high, high, low], axis=axis)


def cos_sin(angle):
    square = angle * angle
    cosine, sine = jnp.full_like(angle, 1.0), jnp.full_like(angle, 1.0)
    for order in range(12, 0, -2):
        cosine = 1.0 - cosine * square * (1.0 / (order * (order - 1)))
        sine = 1.0 - sine * square * (1.0 / (order * (order + 1)))
    return cosine, sine * angle


def rotated(real_part, imag_part, cosine, sine):
    return real_part * cosine + imag_part * sine, imag_part * cosine - real_part * sine


def gather_planes(ref):
    blocks = ref.shape[0]
    return jnp.concatenate(
        [
            jnp.concatenate(
                [ref[:, part, plane].reshape(blocks * PLANES, ROWS) for plane in range(PLANES)],
                axis=1,
            )
            for part in range(2)
        ],
        axis=0,
    )


def natural(ref):
    return jnp.concatenate([ref[plane] for plane in range(PLANES)], axis=1)


def lane(value, plane):
    return value[:, plane * ROWS : (plane + 1) * ROWS]


def scatter_planes(real_part, imag_part, right_ref, out_ref):
    rows = jnp.concatenate(
        [
            jnp.concatenate([lane(real_part, plane), lane(imag_part, plane)], axis=1)
            for plane in range(PLANES)
        ],
        axis=0,
    )
    turned = from_right(rows, right_ref[...])
    for plane in range(PLANES):
        for part in range(2):
            piece = turned[plane * ROWS : (plane + 1) * ROWS, part * ROWS : (part + 1) * ROWS]
            for block in range(out_ref.shape[0]):
                out_ref[block, part, pl.ds(plane, PLANES, stride=PLANES), :] = piece[
                    block * PLANES : (block + 1) * PLANES
                ]


def mid_kernel(sign, field_ref, pot_ref, first_ref, second_ref, right_ref, out_ref):
    field = from_left(first_ref[...], gather_planes(field_ref))
    cosine, sine = cos_sin(sign * sub_time * natural(pot_ref))
    real_part, imag_part = rotated(field[:ROWS], field[ROWS:], cosine, sine)
    field = from_left(second_ref[...], jnp.concatenate([real_part, imag_part], axis=0))
    scatter_planes(field[:ROWS], field[ROWS:], right_ref, out_ref)


def store_natural(ref, part, value):
    for plane in range(PLANES):
        ref[part, plane] = lane(value, plane)


def step_kernel(
    sign, field_ref, pot_ref, first_ref, second_ref, right_ref, out_ref, keep_ref
):
    field = from_left(first_ref[...], gather_planes(field_ref))
    cosine, sine = cos_sin(sign * 0.5 * sub_time * natural(pot_ref))
    real_part, imag_part = rotated(field[:ROWS], field[ROWS:], cosine, sine)
    store_natural(keep_ref, 0, real_part)
    store_natural(keep_ref, 1, imag_part)
    real_part, imag_part = rotated(real_part, imag_part, cosine, sine)
    field = from_left(second_ref[...], jnp.concatenate([real_part, imag_part], axis=0))
    scatter_planes(field[:ROWS], field[ROWS:], right_ref, out_ref)


def start_kernel(sign, field_ref, pot_ref, second_ref, right_ref, out_ref):
    cosine, sine = cos_sin(sign * 0.5 * sub_time * natural(pot_ref))
    real_part, imag_part = rotated(
        natural(field_ref.at[0]), natural(field_ref.at[1]), cosine, sine
    )
    field = from_left(second_ref[...], jnp.concatenate([real_part, imag_part], axis=0))
    scatter_planes(field[:ROWS], field[ROWS:], right_ref, out_ref)


def end_kernel(sign, field_ref, pot_ref, first_ref, other_ref, factor_ref, keep_ref, density_ref):
    field = from_left(first_ref[...], gather_planes(field_ref))
    cosine, sine = cos_sin(sign * 0.5 * sub_time * natural(pot_ref))
    real_part, imag_part = rotated(field[:ROWS], field[ROWS:], cosine, sine)
    store_natural(keep_ref, 0, real_part)
    store_natural(keep_ref, 1, imag_part)
    factor = factor_ref[0, 0]
    for plane in range(PLANES):
        density_ref[plane] = factor * (
            lane(real_part, plane) * other_ref[0, plane]
            + lane(imag_part, plane) * other_ref[1, plane]
        )


def final_kernel(sign, field_ref, pot_ref, first_ref, keep_ref):
    field = from_left(first_ref[...], gather_planes(field_ref))
    cosine, sine = cos_sin(sign * 0.5 * sub_time * natural(pot_ref))
    real_part, imag_part = rotated(field[:ROWS], field[ROWS:], cosine, sine)
    store_natural(keep_ref, 0, real_part)
    store_natural(keep_ref, 1, imag_part)


def stack_planes(value):
    return jnp.concatenate([lane(value, plane) for plane in range(PLANES)], axis=0)


def density_kernel(own_ref, other_ref, left_ref, right_ref, density_ref, out_ref):
    density = natural(own_ref) + natural(other_ref)
    for plane in range(PLANES):
        density_ref[plane] = lane(density, plane)
    spectrum = from_right(stack_planes(from_left(left_ref[...], density)), right_ref[...])
    for plane in range(PLANES):
        for block in range(out_ref.shape[0]):
            start = plane * ROWS + block * PLANES
            out_ref[block, pl.ds(plane, PLANES, stride=PLANES), :] = spectrum[
                start : start + PLANES
            ]


def coulomb_kernel(unit, field_ref, square_ref, left_ref, out_ref):
    blocks = field_ref.shape[0]
    rows = jnp.concatenate(
        [field_ref[:, line].reshape(ROWS, ROWS) for line in range(PLANES)], axis=1
    )
    rows = from_left(left_ref[...], rows)
    index = lax.broadcasted_iota(jnp.int32, (ROWS, ROWS), 0)
    number = unit * jnp.where(index < ROWS // 2, index, index - ROWS).astype(jnp.float32)
    along = number * number
    parts = []
    for line in range(PLANES):
        square = along + square_ref[pl.ds(line, 1), :]
        nonzero = square > 0
        parts.append(
            lane(rows, line) * jnp.where(nonzero, 4.0 * math.pi / jnp.where(nonzero, square, 1.0), 0.0)
        )
    rows = from_left(left_ref[...], jnp.concatenate(parts, axis=1))
    for line in range(PLANES):
        out_ref[:, line] = lane(rows, line).reshape(blocks, PLANES, ROWS)


def hartree_kernel(
    sign,
    field_ref,
    density_ref,
    xc_ref,
    orbital_ref,
    adjoint_ref,
    pot_ref,
    cas_left_ref,
    cas_right_ref,
    second_ref,
    right_ref,
    out_ref,
    cross_ref,
):
    blocks = field_ref.shape[0]
    spectrum = jnp.concatenate(
        [
            jnp.concatenate(
                [
                    field_ref[block, pl.ds(plane, PLANES, stride=PLANES), :]
                    for block in range(blocks)
                ],
                axis=0,
            )
            for plane in range(PLANES)
        ],
        axis=1,
    )
    hartree = from_right(
        stack_planes(from_left(cas_left_ref[...], spectrum)), cas_right_ref[...]
    )
    real_parts, imag_parts = [], []
    for plane in range(PLANES):
        cross = hartree[plane * ROWS : (plane + 1) * ROWS] + xc_ref[plane] * density_ref[plane]
        cross_ref[plane] = cross
        real_parts.append(adjoint_ref[0, plane] + step_time * cross * orbital_ref[1, plane])
        imag_parts.append(adjoint_ref[1, plane] - step_time * cross * orbital_ref[0, plane])
    cosine, sine = cos_sin(sign * 0.5 * sub_time * natural(pot_ref))
    real_part, imag_part = rotated(
        jnp.concatenate(real_parts, axis=1), jnp.concatenate(imag_parts, axis=1), cosine, sine
    )
    field = from_left(second_ref[...], jnp.concatenate([real_part, imag_part], axis=0))
    scatter_planes(field[:ROWS], field[ROWS:], right_ref, out_ref)


def run(kernel, outputs, *operands):
    in_specs = [
        pl.BlockSpec(memory_space=pltpu.SMEM if operand.size == 1 else pltpu.VMEM)
        for operand in operands
    ]
    made = pl.pallas_call(
        kernel,
        out_shape=[jax.ShapeDtypeStruct(shape, jnp.float32) for shape in outputs],
        in_specs=in_specs,
        out_specs=[pl.BlockSpec(memory_space=pltpu.VMEM) for _ in outputs],
        compiler_params=pltpu.CompilerParams(vmem_limit_bytes=40 * 2**20),
    )(*operands)
    return made[0] if len(outputs) == 1 else made


def grouped(
    orbitals, costate, potential, xc_kernel, vector_potential, kpoint_weight, occupation
):
    grid_size = potential.shape[1]
    blocks = lax.axis_size("fft")
    half = blocks // 2
    core = lax.axis_index("ka")
    fft_index = lax.axis_index("fft")
    side = fft_index // half
    place = core * half + fft_index % half
    lattice_unit = 2.0 * math.pi / (grid_size * spacing)

    groups = [
        [c * blocks + h * half + j for c in range(2) for j in range(half)] for h in range(2)
    ]
    regroup = []
    for c in range(2):
        for f in range(blocks):
            h, j = f // half, f % half
            regroup.append((c * blocks + f, h * blocks + c * half + j))
    across = [
        (c * blocks + f, c * blocks + (f + half) % blocks) for c in range(2) for f in range(blocks)
    ]

    def exchange(array):
        return lax.all_to_all(array, AXES, 0, 0, axis_index_groups=groups, tiled=True)

    def move(array, pairs):
        return lax.ppermute(array, AXES, pairs)

    block_shape = (blocks, 2, PLANES, PLANES, ROWS)
    sent_shape = (blocks, 2, PLANES * PLANES, ROWS)
    natural_shape = (2, PLANES, ROWS, ROWS)
    real_shape = (PLANES, ROWS, ROWS)

    def swap_field(array):
        return exchange(array.reshape(block_shape))

    own = lax.dynamic_slice_in_dim(potential, core * (PLANES // 2), PLANES // 2, 0)
    own = own.reshape(PLANES // 2, 2, half, PLANES, ROWS).transpose(1, 2, 0, 3, 4)
    own = jnp.broadcast_to(own[:, None], (2, 2) + own.shape[1:]).reshape(
        (2 * blocks, PLANES // 2, PLANES, ROWS)
    )
    got = lax.all_to_all(own, AXES, 0, 0, tiled=True)
    got = got.reshape(2, blocks, PLANES // 2, PLANES, ROWS).transpose(3, 1, 0, 2, 4)
    pot_cols = got.reshape(real_shape)
    pot_rows = move(potential, regroup)

    shift_x = lattice_unit * ((side.astype(jnp.float32) + 0.5) / 2 - 0.5) + vector_potential
    shift_yz = jnp.array([lattice_unit * 0.25, -lattice_unit * 0.25], jnp.float32)
    shifts = jnp.concatenate([shift_x, shift_yz])
    lines = real_form(*line_matrices(shifts, grid_size)).reshape(-1, 2 * grid_size, 2 * grid_size)
    back = jnp.transpose(lines, (0, 2, 1))
    tables = {1.0: side_table(lines, 2), -1.0: side_table(back, 2)}
    count_x = STEPS * SUB
    right_z = {
        1.0: side_table(back[count_x + 1], 0),
        -1.0: side_table(lines[count_x + 1], 0),
    }

    angles = table_angles(grid_size)
    cas = (jnp.cos(angles) + jnp.sin(angles)) / math.sqrt(grid_size)
    cas_left, cas_right = side_table(cas, 1), side_table(cas, 0)
    numbers = wave_numbers(lax.iota(jnp.int32, grid_size), grid_size)
    own_numbers = wave_numbers(place * PLANES + lax.iota(jnp.int32, PLANES), grid_size)
    squares = (own_numbers * own_numbers)[:, None] + (numbers * numbers)[None, :]

    occupied = occupation.astype(jnp.float32) / 100.0
    own_weight = lax.dynamic_slice_in_dim(kpoint_weight, side, 1)[0].astype(jnp.float32)
    weight = own_weight / jnp.sum(kpoint_weight).astype(jnp.float32)
    factor = (2.0 * weight * occupied).reshape(1, 1)

    adjoint = move(costate.reshape(natural_shape), regroup)
    xc_rows = move(xc_kernel, regroup)

    def table_x(sign, count):
        return tables[sign][count if sign > 0 else count_x - 1 - count]

    def table_y(sign):
        return tables[sign][count_x]

    def middle(sign, field, in_rows, count):
        if in_rows:
            tabs = (pot_rows, table_y(sign), table_y(sign))
        else:
            tabs = (pot_cols, table_x(sign, count - 1), table_x(sign, count))
        return run(
            functools.partial(mid_kernel, sign), [sent_shape], field, *tabs, right_z[sign]
        )

    sent = run(
        functools.partial(start_kernel, 1.0),
        [sent_shape],
        orbitals.reshape(natural_shape),
        potential,
        table_y(1.0),
        right_z[1.0],
    )
    sent = move(sent, regroup)
    kept = []
    for count in range(1, count_x):
        field = swap_field(sent)
        in_rows = count % 2 == 0
        if count % SUB == 0:
            sent, orbital = run(
                functools.partial(step_kernel, 1.0),
                [sent_shape, natural_shape],
                field,
                pot_rows,
                table_y(1.0),
                table_y(1.0),
                right_z[1.0],
            )
            kept.append(orbital)
        else:
            sent = middle(1.0, field, in_rows, count)
    orbital, partial = run(
        functools.partial(end_kernel, 1.0),
        [natural_shape, real_shape],
        swap_field(sent),
        pot_rows,
        table_y(1.0),
        adjoint,
        factor,
    )
    kept.append(orbital)

    for step_index in range(STEPS - 1, -1, -1):
        density, sent = run(
            density_kernel,
            [real_shape, (blocks, PLANES * PLANES, ROWS)],
            partial,
            move(partial, across),
            cas_left,
            cas_right,
        )
        field = exchange(sent.reshape(blocks, PLANES, PLANES, ROWS))
        sent = run(
            functools.partial(coulomb_kernel, lattice_unit),
            [(blocks, PLANES, PLANES, ROWS)],
            field,
            squares,
            cas_left,
        )
        field = exchange(sent).reshape(blocks, PLANES * PLANES, ROWS)
        sent, cross = run(
            functools.partial(hartree_kernel, -1.0),
            [sent_shape, real_shape],
            field,
            density,
            xc_rows,
            kept[step_index],
            adjoint,
            pot_rows,
            cas_left,
            cas_right,
            table_y(-1.0),
            right_z[-1.0],
        )
        first = (STEPS - 1 - step_index) * SUB
        for count in range(first + 1, first + SUB):
            sent = middle(-1.0, swap_field(sent), count % 2 == 0, count)
        field = swap_field(sent)
        if step_index > 0:
            adjoint, partial = run(
                functools.partial(end_kernel, -1.0),
                [natural_shape, real_shape],
                field,
                pot_rows,
                table_y(-1.0),
                kept[step_index - 1],
                factor,
            )
        else:
            adjoint = run(
                functools.partial(final_kernel, -1.0),
                [natural_shape],
                field,
                pot_rows,
                table_y(-1.0),
            )
    result = move(adjoint, regroup).reshape(orbitals.shape)
    beside = lax.ppermute(cross, "ka", [(0, 1), (1, 0)])
    return (result, jnp.where(core == side, cross, beside))


def solution(mesh):
    placed = (
        P("ka", None, None, "fft", None, None),
        P("ka", None, None, "fft", None, None),
        P("fft", None, None),
        P("fft", None, None),
        P(),
        P(),
        P(),
    )

    def local(*arguments):
        orbitals, potential = arguments[0], arguments[2]
        fits = (
            mesh.shape["ka"] == 2
            and mesh.shape["fft"] % 2 == 0
            and orbitals.shape[:2] == (1, 1)
            and potential.shape == (PLANES, ROWS, ROWS)
        )
        return grouped(*arguments) if fits else plain(*arguments)

    return jax.shard_map(
        local,
        mesh=mesh,
        in_specs=placed,
        out_specs=(P("ka", None, None, "fft", None, None), P("fft", None, None)),
        check_vma=False,
    )
```

```python
import functools
import math

import jax
import jax.numpy as jnp
import numpy as np
from jax import lax
from jax.experimental import pallas as pl
from jax.experimental.pallas import tpu as pltpu
from jax.sharding import PartitionSpec as P

STEPS = 2
SUB = 4


spacing = 0.25
step_time = 0.6
sub_time = step_time / SUB
highest = lax.Precision.HIGHEST


def wave_numbers(grid_line, grid_size):
    signed_line = jnp.where(grid_line < grid_size // 2, grid_line, grid_line - grid_size)
    return 2.0 * math.pi / (grid_size * spacing) * signed_line.astype(jnp.float32)


def table_angles(grid_size):
    row_index = lax.broadcasted_iota(jnp.int32, (grid_size, grid_size), 0)
    col_index = lax.broadcasted_iota(jnp.int32, (grid_size, grid_size), 1)
    return 2.0 * math.pi / grid_size * (row_index * col_index % grid_size).astype(jnp.float32)


def line_matrices(shifts, grid_size):
    numbers = wave_numbers(lax.iota(jnp.int32, grid_size), grid_size)
    along = shifts[:, None] + numbers[None, :]
    phase = 0.5 * sub_time * (along * along)
    angles = table_angles(grid_size)
    cosine, sine = jnp.cos(angles), jnp.sin(angles)
    q_real, q_imag = jnp.cos(phase)[:, None, :], -jnp.sin(phase)[:, None, :]
    left_real = (cosine * q_real - sine * q_imag) / grid_size
    left_imag = (cosine * q_imag + sine * q_real) / grid_size
    both = jnp.stack([left_real, left_imag])
    by_cos = jnp.einsum("csam,mb->csab", both, cosine, precision=highest)
    by_sin = jnp.einsum("csam,mb->csab", both, sine, precision=highest)
    return by_cos[0] + by_sin[1], by_cos[1] - by_sin[0]


def real_form(real_part, imag_part):
    upper = jnp.stack([real_part, -imag_part], axis=-2)
    lower = jnp.stack([imag_part, real_part], axis=-2)
    return jnp.stack([upper, lower], axis=-4)


def spin(field, angle):
    cosine, sine = jnp.cos(angle), jnp.sin(angle)
    return jnp.stack(
        [field[0] * cosine + field[1] * sine, field[1] * cosine - field[0] * sine]
    )


def apply(form, matrix, field):
    return jnp.einsum(
        form, matrix, field, precision=lax.Precision.HIGHEST, preferred_element_type=jnp.float32
    )


def plain(orbitals, costate, potential, xc_kernel, vector_potential, kpoint_weight, occupation):
    grid_size = potential.shape[1]
    k_index = lax.axis_index("ka")
    fft_index = lax.axis_index("fft")
    planes = potential.shape[0]
    lattice_unit = 2.0 * math.pi / (grid_size * spacing)
    k_fraction = (k_index.astype(jnp.float32) + 0.5) / lax.axis_size("ka") - 0.5
    shifts = jnp.concatenate(
        [
            lattice_unit * k_fraction + vector_potential,
            jnp.array([lattice_unit * 0.25, -lattice_unit * 0.25], jnp.float32),
        ]
    )
    lines = real_form(*line_matrices(shifts, grid_size))
    back = jnp.transpose(lines, (0, 3, 4, 1, 2))

    def to_columns(field, split, concat):
        return lax.all_to_all(field, "fft", split_axis=split, concat_axis=concat, tiled=True)

    pot_rows = 0.5 * sub_time * potential
    pot_cols = to_columns(pot_rows, 1, 0)

    def propagate(field, step_index, sign):
        table = lines if sign > 0 else back
        order = range(SUB) if sign > 0 else range(SUB - 1, -1, -1)
        mat_y, mat_z = table[STEPS * SUB], table[STEPS * SUB + 1]
        in_rows = True
        field = spin(field, sign * pot_rows)
        for count, sub_index in enumerate(order):
            mat_x = table[step_index * SUB + sub_index]
            last = count == SUB - 1
            turn = sign * (1.0 if last else 2.0)
            field = apply("cadb,dkxyb->ckxya", mat_z, field)
            if in_rows:
                field = apply("cadb,dkxbz->ckxaz", mat_y, field)
                field = to_columns(field, 3, 2)
                field = apply("cadb,dkbyz->ckayz", mat_x, field)
                field = spin(field, turn * pot_cols)
            else:
                field = apply("cadb,dkbyz->ckayz", mat_x, field)
                field = to_columns(field, 2, 3)
                field = apply("cadb,dkxbz->ckxaz", mat_y, field)
                field = spin(field, turn * pot_rows)
            in_rows = not in_rows
        return field

    def parts_first(field):
        bands = field.shape[0] * field.shape[1]
        return jnp.moveaxis(field, 2, 0).reshape((2, bands) + field.shape[3:])

    angles = table_angles(grid_size)
    cas = (jnp.cos(angles) + jnp.sin(angles)) / math.sqrt(grid_size)
    numbers = wave_numbers(lax.iota(jnp.int32, grid_size), grid_size)
    numbers_local = wave_numbers(fft_index * planes + lax.iota(jnp.int32, planes), grid_size)
    g_squared = (
        (numbers * numbers)[:, None, None]
        + (numbers_local * numbers_local)[None, :, None]
        + (numbers * numbers)[None, None, :]
    )
    coulomb = jnp.where(
        g_squared > 0, 4.0 * math.pi / jnp.where(g_squared > 0, g_squared, 1.0), 0.0
    )
    orbital = parts_first(orbitals)
    history = [orbital]
    for step_index in range(STEPS):
        orbital = propagate(orbital, step_index, 1.0)
        history.append(orbital)
    occupied = occupation.astype(jnp.float32) / 100.0
    own_weight = lax.dynamic_slice_in_dim(kpoint_weight, k_index, 1)[0].astype(jnp.float32)
    weight = own_weight / jnp.sum(kpoint_weight).astype(jnp.float32)
    band_factor = 2.0 * weight * occupied
    adjoint = parts_first(costate)
    cross_pot = jnp.zeros_like(potential)
    for step_index in range(STEPS - 1, -1, -1):
        forward = history[step_index + 1]
        density = lax.psum(
            jnp.sum(band_factor[:, None, None, None] * jnp.sum(adjoint * forward, axis=0), axis=0),
            "ka",
        )
        hartree = apply("ab,xyb->xya", cas, density)
        hartree = apply("ab,xbz->xaz", cas, hartree)
        hartree = to_columns(hartree, 1, 0)
        hartree = apply("ab,byz->ayz", cas, hartree)
        hartree = apply("ab,byz->ayz", cas, hartree * coulomb)
        hartree = to_columns(hartree, 0, 1)
        hartree = apply("ab,xbz->xaz", cas, hartree)
        hartree = apply("ab,xyb->xya", cas, hartree)
        cross_pot = hartree + xc_kernel * density
        turned = jnp.stack([forward[1], -forward[0]])
        adjoint = propagate(adjoint + step_time * cross_pot * turned, step_index, -1.0)
    result = jnp.moveaxis(adjoint.reshape((2,) + orbitals.shape[:2] + adjoint.shape[2:]), 0, 2)
    return (result, cross_pot)


ROWS = 128
PLANES = 8
AXES = ("ka", "fft")


def halves_of(value):
    high = value.astype(jnp.bfloat16)
    return high, (value - high.astype(jnp.float32)).astype(jnp.bfloat16)


def from_left(table, field):
    size = table.shape[1] // 2
    high, low = halves_of(field)
    return jnp.dot(
        jnp.concatenate([table[:, :size], table], axis=1),
        jnp.concatenate([high, low, high], axis=0),
        preferred_element_type=jnp.float32,
    )


def from_right(field, table):
    size = table.shape[0] // 2
    high, low = halves_of(field)
    return jnp.dot(
        jnp.concatenate([high, low, high], axis=1),
        jnp.concatenate([table[:size], table], axis=0),
        preferred_element_type=jnp.float32,
    )


def side_by_side(matrix, axis):
    return jnp.concatenate(halves_of(matrix), axis=axis)


def circulant(shift, numbers, cosine, sine):
    along = shift + numbers
    phase = 0.5 * sub_time * (along * along)
    q_real, q_imag = jnp.cos(phase), -jnp.sin(phase)
    even = q_real * cosine + q_imag * sine
    odd = q_real * sine - q_imag * cosine
    spectrum = jnp.concatenate(
        [jnp.concatenate([even, odd], axis=1), jnp.concatenate([odd, -even], axis=1)], axis=0
    )
    upper = jnp.dot(
        jnp.concatenate([cosine, sine], axis=1),
        spectrum,
        precision=highest,
        preferred_element_type=jnp.float32,
    ) * (1.0 / ROWS)
    real_part, minus = upper[:, :ROWS], upper[:, ROWS:]
    real_turned, minus_turned = real_part.T, minus.T
    return upper, jnp.concatenate([real_turned, -minus_turned], axis=1)


def whole_matrix(upper):
    real_part, minus = upper[:, :ROWS], upper[:, ROWS:]
    return jnp.concatenate([upper, jnp.concatenate([-minus, real_part], axis=1)], axis=0)


def whole_left(table):
    return jnp.concatenate(
        [whole_matrix(table[:, : 2 * ROWS]), whole_matrix(table[:, 2 * ROWS :])], axis=1
    )


def table_kernel(count_x, shift_ref, numbers_ref, lines_ref, *out_refs):
    numbers, cosine, sine = numbers_ref[...], lines_ref[:, :ROWS], lines_ref[:, ROWS:]
    for line in range(count_x + 1):
        matrix, turned = circulant(shift_ref[line], numbers, cosine, sine)
        out_refs[2 * line][...] = side_by_side(matrix, 1)
        out_refs[2 * line + 1][...] = side_by_side(turned, 1)
    matrix, turned = circulant(shift_ref[count_x + 1], numbers, cosine, sine)
    out_refs[2 * count_x + 2][...] = side_by_side(whole_matrix(turned), 0)
    out_refs[2 * count_x + 3][...] = side_by_side(whole_matrix(matrix), 0)


def cos_sin(angle):
    square = angle * angle
    cosine, sine = jnp.full_like(angle, 1.0), jnp.full_like(angle, 1.0)
    for order in range(12, 0, -2):
        cosine = 1.0 - cosine * square * (1.0 / (order * (order - 1)))
        sine = 1.0 - sine * square * (1.0 / (order * (order + 1)))
    return cosine, sine * angle


def rotated(real_part, imag_part, cosine, sine):
    return real_part * cosine + imag_part * sine, imag_part * cosine - real_part * sine


def gather_planes(ref):
    blocks = ref.shape[0]
    return jnp.concatenate(
        [
            jnp.concatenate(
                [ref[:, part, plane].reshape(blocks * PLANES, ROWS) for plane in range(PLANES)],
                axis=1,
            )
            for part in range(2)
        ],
        axis=0,
    )


def natural(ref):
    return jnp.concatenate([ref[plane] for plane in range(PLANES)], axis=1)


def strided(ref, plane):
    return jnp.concatenate(
        [ref[block, pl.ds(plane, PLANES, stride=PLANES), :] for block in range(ref.shape[0])],
        axis=0,
    )


def angles_of(ref):
    if len(ref.shape) == 3:
        return jnp.concatenate([strided(ref, plane) for plane in range(PLANES)], axis=1)
    if ref.shape[2] == PLANES * PLANES:
        return angles_of(ref.at[:, 2])
    if len(ref.shape) == 5:
        return angles_of(ref.at[:, 2])
    return jnp.concatenate(
        [ref[:, plane].reshape(ROWS, ROWS) for plane in range(PLANES)], axis=1
    )


def lane(value, plane):
    return value[:, plane * ROWS : (plane + 1) * ROWS]


def scatter_planes(real_part, imag_part, table, out_ref):
    rows = jnp.concatenate(
        [
            jnp.concatenate([lane(real_part, plane), lane(imag_part, plane)], axis=1)
            for plane in range(PLANES)
        ],
        axis=0,
    )
    turned = from_right(rows, table)
    for plane in range(PLANES):
        for part in range(2):
            piece = turned[plane * ROWS : (plane + 1) * ROWS, part * ROWS : (part + 1) * ROWS]
            for block in range(out_ref.shape[0]):
                out_ref[block, part, pl.ds(plane, PLANES, stride=PLANES), :] = piece[
                    block * PLANES : (block + 1) * PLANES
                ]


def mid_kernel(sign, field_ref, pot_ref, first_ref, second_ref, right_ref, out_ref):
    field = from_left(whole_left(first_ref[...]), gather_planes(field_ref))
    cosine, sine = cos_sin(sign * sub_time * angles_of(pot_ref))
    real_part, imag_part = rotated(field[:ROWS], field[ROWS:], cosine, sine)
    field = from_left(whole_left(second_ref[...]), jnp.concatenate([real_part, imag_part], axis=0))
    scatter_planes(field[:ROWS], field[ROWS:], right_ref[...], out_ref)


def first_mid_kernel(sign, field_ref, first_ref, second_ref, right_ref, out_ref, pot_ref):
    mid_kernel(sign, field_ref, field_ref, first_ref, second_ref, right_ref, out_ref)
    pot_ref[...] = field_ref[:, 2]


def second_mid_kernel(
    sign, field_ref, pot_field_ref, first_ref, second_ref, right_ref, out_ref, pot_ref
):
    mid_kernel(sign, field_ref, pot_field_ref, first_ref, second_ref, right_ref, out_ref)
    pot_ref[...] = pot_field_ref[:, 2]


def store_natural(ref, value):
    for plane in range(PLANES):
        ref[plane] = lane(value, plane)


def step_kernel(
    sign, field_ref, pot_ref, first_ref, second_ref, right_ref, out_ref, real_ref, imag_ref
):
    field = from_left(whole_left(first_ref[...]), gather_planes(field_ref))
    cosine, sine = cos_sin(sign * 0.5 * sub_time * angles_of(pot_ref))
    real_part, imag_part = rotated(field[:ROWS], field[ROWS:], cosine, sine)
    store_natural(real_ref, real_part)
    store_natural(imag_ref, imag_part)
    real_part, imag_part = rotated(real_part, imag_part, cosine, sine)
    field = from_left(whole_left(second_ref[...]), jnp.concatenate([real_part, imag_part], axis=0))
    scatter_planes(field[:ROWS], field[ROWS:], right_ref[...], out_ref)


def start_kernel(
    unit, field_ref, pot_ref, lines_ref, out_ref, numbers_ref
):
    cosine_line, sine_line = lines_ref[:, :ROWS], lines_ref[:, ROWS:]
    index = lax.broadcasted_iota(jnp.int32, (ROWS, ROWS), 0)
    numbers = wave_numbers(index, ROWS)
    numbers_ref[...] = numbers
    table_y = circulant(0.25 * unit, numbers, cosine_line, sine_line)[0]
    table_z = circulant(-0.25 * unit, numbers, cosine_line, sine_line)[1]
    cosine, sine = cos_sin(0.5 * sub_time * natural(pot_ref))
    real_part, imag_part = rotated(
        natural(field_ref.at[0]), natural(field_ref.at[1]), cosine, sine
    )
    field = from_left(side_by_side(whole_matrix(table_y), 1), jnp.concatenate([real_part, imag_part], axis=0))
    scatter_planes(field[:ROWS], field[ROWS:], side_by_side(whole_matrix(table_z), 0), out_ref)
    for plane in range(PLANES):
        for block in range(out_ref.shape[0]):
            out_ref[block, 2, pl.ds(plane, PLANES, stride=PLANES), :] = pot_ref[
                plane, block * PLANES : (block + 1) * PLANES
            ]


def finish(sign, field_ref, pot_ref, first_ref, real_ref, imag_ref):
    field = from_left(whole_left(first_ref[...]), gather_planes(field_ref))
    cosine, sine = cos_sin(sign * 0.5 * sub_time * angles_of(pot_ref))
    real_part, imag_part = rotated(field[:ROWS], field[ROWS:], cosine, sine)
    store_natural(real_ref, real_part)
    store_natural(imag_ref, imag_part)
    return real_part, imag_part


def end_kernel(
    sign,
    field_ref,
    pot_ref,
    first_ref,
    other_real_ref,
    other_imag_ref,
    factor_ref,
    real_ref,
    imag_ref,
    density_ref,
):
    real_part, imag_part = finish(sign, field_ref, pot_ref, first_ref, real_ref, imag_ref)
    factor = factor_ref[0, 0]
    for plane in range(PLANES):
        density_ref[plane] = factor * (
            lane(real_part, plane) * other_real_ref[plane]
            + lane(imag_part, plane) * other_imag_ref[plane]
        )


def final_kernel(sign, field_ref, pot_ref, first_ref, out_ref):
    finish(
        sign, field_ref, pot_ref, first_ref, out_ref.at[0, 0, 0], out_ref.at[0, 0, 1]
    )


def stack_planes(value):
    return jnp.concatenate([lane(value, plane) for plane in range(PLANES)], axis=0)


def density_kernel(own_ref, other_ref, left_ref, right_ref, density_ref, out_ref):
    density = natural(own_ref) + natural(other_ref)
    for plane in range(PLANES):
        density_ref[plane] = lane(density, plane)
    spectrum = from_right(stack_planes(from_left(left_ref[...], density)), right_ref[...])
    for plane in range(PLANES):
        for block in range(out_ref.shape[0]):
            start = plane * ROWS + block * PLANES
            out_ref[block, pl.ds(plane, PLANES, stride=PLANES), :] = spectrum[
                start : start + PLANES
            ]


def coulomb_kernel(unit, field_ref, square_ref, left_ref, out_ref):
    blocks = field_ref.shape[0]
    rows = jnp.concatenate(
        [field_ref[:, line].reshape(ROWS, ROWS) for line in range(PLANES)], axis=1
    )
    rows = from_left(left_ref[...], rows)
    index = lax.broadcasted_iota(jnp.int32, (ROWS, ROWS), 0)
    number = unit * jnp.where(index < ROWS // 2, index, index - ROWS).astype(jnp.float32)
    along = number * number
    parts = []
    for line in range(PLANES):
        square = along + square_ref[pl.ds(line, 1), :]
        nonzero = square > 0
        parts.append(
            lane(rows, line) * jnp.where(nonzero, 4.0 * math.pi / jnp.where(nonzero, square, 1.0), 0.0)
        )
    rows = from_left(left_ref[...], jnp.concatenate(parts, axis=1))
    for line in range(PLANES):
        out_ref[:, line] = lane(rows, line).reshape(blocks, PLANES, ROWS)


def hartree_kernel(
    sign,
    field_ref,
    density_ref,
    xc_ref,
    orbital_real_ref,
    orbital_imag_ref,
    adjoint_real_ref,
    adjoint_imag_ref,
    pot_ref,
    cas_left_ref,
    cas_right_ref,
    second_ref,
    right_ref,
    out_ref,
    cross_ref,
):
    spectrum = angles_of(field_ref)
    hartree = from_right(
        stack_planes(from_left(cas_left_ref[...], spectrum)), cas_right_ref[...]
    )
    real_parts, imag_parts = [], []
    for plane in range(PLANES):
        cross = hartree[plane * ROWS : (plane + 1) * ROWS] + xc_ref[plane] * density_ref[plane]
        cross_ref[plane] = cross
        real_parts.append(adjoint_real_ref[plane] + step_time * cross * orbital_imag_ref[plane])
        imag_parts.append(adjoint_imag_ref[plane] - step_time * cross * orbital_real_ref[plane])
    cosine, sine = cos_sin(sign * 0.5 * sub_time * angles_of(pot_ref))
    real_part, imag_part = rotated(
        jnp.concatenate(real_parts, axis=1), jnp.concatenate(imag_parts, axis=1), cosine, sine
    )
    field = from_left(whole_left(second_ref[...]), jnp.concatenate([real_part, imag_part], axis=0))
    scatter_planes(field[:ROWS], field[ROWS:], right_ref[...], out_ref)


def run(kernel, outputs, *operands):
    made = pl.pallas_call(
        kernel,
        out_shape=[
            jax.ShapeDtypeStruct(out, jnp.float32) if isinstance(out, tuple) else out
            for out in outputs
        ],
        in_specs=[
            pl.BlockSpec(memory_space=pltpu.SMEM if operand.size < ROWS else pltpu.VMEM)
            for operand in operands
        ],
        out_specs=[pl.BlockSpec(memory_space=pltpu.VMEM) for _ in outputs],
        compiler_params=pltpu.CompilerParams(vmem_limit_bytes=24 * 2**20),
    )(*operands)
    return made[0] if len(outputs) == 1 else made


def grouped(
    orbitals, costate, potential, xc_kernel, vector_potential, kpoint_weight, occupation
):
    grid_size = potential.shape[1]
    blocks = lax.axis_size("fft")
    half = blocks // 2
    core = lax.axis_index("ka")
    fft_index = lax.axis_index("fft")
    side = fft_index // half
    place = core * half + fft_index % half
    lattice_unit = 2.0 * math.pi / (grid_size * spacing)

    groups = [
        [c * blocks + h * half + j for c in range(2) for j in range(half)] for h in range(2)
    ]
    regroup = []
    for c in range(2):
        for f in range(blocks):
            h, j = f // half, f % half
            regroup.append((c * blocks + f, h * blocks + c * half + j))
    across = [
        (c * blocks + f, c * blocks + (f + half) % blocks) for c in range(2) for f in range(blocks)
    ]

    def exchange(array):
        return lax.all_to_all(array, AXES, 0, 0, axis_index_groups=groups, tiled=True)

    def move(array, pairs):
        return lax.ppermute(array, AXES, pairs)

    block_shape = (blocks, 2, PLANES, PLANES, ROWS)
    sent_shape = (blocks, 2, PLANES * PLANES, ROWS)
    natural_shape = (2, PLANES, ROWS, ROWS)
    real_shape = (PLANES, ROWS, ROWS)

    def swap_field(array):
        return exchange(array.reshape(block_shape))

    grid_line = np.arange(grid_size)
    angles = 2.0 * np.pi / grid_size * (np.outer(grid_line, grid_line) % grid_size)
    line_pair = jnp.asarray(
        np.concatenate([np.cos(angles), np.sin(angles)], axis=1).astype(np.float32)
    )
    cas = (np.cos(angles) + np.sin(angles)) / math.sqrt(grid_size)
    cas_high = cas.astype(jnp.bfloat16)
    cas_low = (cas - cas_high.astype(np.float64)).astype(jnp.bfloat16)
    cas_left = jnp.asarray(np.concatenate([cas_high, cas_low], axis=1))
    cas_right = jnp.asarray(np.concatenate([cas_high, cas_low], axis=0))

    shift_x = lattice_unit * ((side.astype(jnp.float32) + 0.5) / 2 - 0.5) + vector_potential
    shift_yz = jnp.array([lattice_unit * 0.25, -lattice_unit * 0.25], jnp.float32)
    count_x = STEPS * SUB

    numbers = wave_numbers(lax.iota(jnp.int32, grid_size), grid_size)
    own_numbers = wave_numbers(place * PLANES + lax.iota(jnp.int32, PLANES), grid_size)
    squares = (own_numbers * own_numbers)[:, None] + (numbers * numbers)[None, :]

    occupied = occupation.astype(jnp.float32) / 100.0
    own_weight = lax.dynamic_slice_in_dim(kpoint_weight, side, 1)[0].astype(jnp.float32)
    weight = own_weight / jnp.sum(kpoint_weight).astype(jnp.float32)
    factor = (2.0 * weight * occupied).reshape(1, 1)

    sent, numbers_full = run(
        functools.partial(start_kernel, lattice_unit),
        [(blocks, 3, PLANES * PLANES, ROWS), (ROWS, ROWS)],
        orbitals.reshape(natural_shape),
        potential,
        line_pair,
    )
    sent = move(sent, regroup)
    left_shape = jax.ShapeDtypeStruct((ROWS, 4 * ROWS), jnp.bfloat16)
    right_shape = jax.ShapeDtypeStruct((4 * ROWS, 2 * ROWS), jnp.bfloat16)
    made = run(
        functools.partial(table_kernel, count_x),
        [left_shape] * (2 * count_x + 2) + [right_shape] * 2,
        jnp.concatenate([shift_x, shift_yz]),
        numbers_full,
        line_pair,
    )
    early = (squares, factor, costate[0, 0, 0], costate[0, 0, 1])
    sent, made, early = lax.optimization_barrier((sent, made, early))
    squares, factor, costate_real, costate_imag = early
    tables = {1.0: made[0 : 2 * count_x + 2 : 2], -1.0: made[1 : 2 * count_x + 2 : 2]}
    right_z = {1.0: made[-2], -1.0: made[-1]}

    def swap_beside(sent, array):
        sent, array = lax.optimization_barrier((sent, array))
        return lax.optimization_barrier((swap_field(sent), move(array, regroup)))

    def table_x(sign, count):
        return tables[sign][count if sign > 0 else count_x - 1 - count]

    def table_y(sign):
        return tables[sign][count_x]

    def middle(sign, field, in_rows, count, pot):
        if in_rows:
            tabs = (pot, table_y(sign), table_y(sign))
        else:
            tabs = (pot, table_x(sign, count - 1), table_x(sign, count))
        return run(
            functools.partial(mid_kernel, sign), [sent_shape], field, *tabs, right_z[sign]
        )

    kept = []
    for count in range(1, count_x):
        if count == 1:
            field = exchange(sent.reshape(blocks, 3, PLANES, PLANES, ROWS))
            pot_sent = sent
            sent, pot_cols = run(
                functools.partial(first_mid_kernel, 1.0),
                [sent_shape, block_shape[:1] + block_shape[2:]],
                field,
                table_x(1.0, 0),
                table_x(1.0, 1),
                right_z[1.0],
            )
            continue
        if count == 2:
            field, adjoint_real = swap_beside(sent, costate_real)
            sent, pot_rows = run(
                functools.partial(second_mid_kernel, 1.0),
                [sent_shape, sent_shape[:1] + sent_shape[2:]],
                field,
                pot_sent,
                table_y(1.0),
                table_y(1.0),
                right_z[1.0],
            )
            continue
        if count == 3:
            field, adjoint_imag = swap_beside(sent, costate_imag)
        elif count == 5:
            field, xc_rows = swap_beside(sent, xc_kernel)
        else:
            field = swap_field(sent)
        in_rows = count % 2 == 0
        if count % SUB == 0:
            sent, *orbital = run(
                functools.partial(step_kernel, 1.0),
                [sent_shape, real_shape, real_shape],
                field,
                pot_rows,
                table_y(1.0),
                table_y(1.0),
                right_z[1.0],
            )
            kept.append(orbital)
        else:
            sent = middle(1.0, field, in_rows, count, pot_rows if in_rows else pot_cols)
    adjoint = [adjoint_real, adjoint_imag]
    *orbital, partial = run(
        functools.partial(end_kernel, 1.0),
        [real_shape] * 3,
        swap_field(sent),
        pot_rows,
        table_y(1.0),
        *adjoint,
        factor,
    )
    kept.append(orbital)

    for step_index in range(STEPS - 1, -1, -1):
        density, sent = run(
            density_kernel,
            [real_shape, (blocks, PLANES * PLANES, ROWS)],
            partial,
            move(partial, across),
            cas_left,
            cas_right,
        )
        field = exchange(sent.reshape(blocks, PLANES, PLANES, ROWS))
        sent = run(
            functools.partial(coulomb_kernel, lattice_unit),
            [(blocks, PLANES, PLANES, ROWS)],
            field,
            squares,
            cas_left,
        )
        field = exchange(sent).reshape(blocks, PLANES * PLANES, ROWS)
        sent, cross = run(
            functools.partial(hartree_kernel, -1.0),
            [sent_shape, real_shape],
            field,
            density,
            xc_rows,
            *kept[step_index],
            *adjoint,
            pot_rows,
            cas_left,
            cas_right,
            table_y(-1.0),
            right_z[-1.0],
        )
        first = (STEPS - 1 - step_index) * SUB
        for count in range(first + 1, first + SUB):
            in_rows = count % 2 == 0
            sent = middle(
                -1.0, swap_field(sent), in_rows, count, pot_rows if in_rows else pot_cols
            )
        field = swap_field(sent)
        if step_index > 0:
            *adjoint, partial = run(
                functools.partial(end_kernel, -1.0),
                [real_shape] * 3,
                field,
                pot_rows,
                table_y(-1.0),
                *kept[step_index - 1],
                factor,
            )
        else:
            adjoint = run(
                functools.partial(final_kernel, -1.0),
                [orbitals.shape],
                field,
                pot_rows,
                table_y(-1.0),
            )
    result = move(adjoint, regroup)
    beside = lax.ppermute(cross, "ka", [(0, 1), (1, 0)])
    return (result, jnp.where(core == side, cross, beside))


def solution(mesh):
    placed = (
        P("ka", None, None, "fft", None, None),
        P("ka", None, None, "fft", None, None),
        P("fft", None, None),
        P("fft", None, None),
        P(),
        P(),
        P(),
    )

    def local(*arguments):
        orbitals, potential = arguments[0], arguments[2]
        fits = (
            mesh.shape["ka"] == 2
            and mesh.shape["fft"] % 2 == 0
            and orbitals.shape[:2] == (1, 1)
            and potential.shape == (PLANES, ROWS, ROWS)
        )
        return grouped(*arguments) if fits else plain(*arguments)

    return jax.shard_map(
        local,
        mesh=mesh,
        in_specs=placed,
        out_specs=(P("ka", None, None, "fft", None, None), P("fft", None, None)),
        check_vma=False,
    )
```

```python
import functools
import math

import jax
import jax.numpy as jnp
import numpy as np
from jax import lax
from jax.experimental import pallas as pl
from jax.experimental.pallas import tpu as pltpu
from jax.sharding import PartitionSpec as P

STEPS = 2
SUB = 4


spacing = 0.25
step_time = 0.6
sub_time = step_time / SUB
highest = lax.Precision.HIGHEST


def wave_numbers(grid_line, grid_size):
    signed_line = jnp.where(grid_line < grid_size // 2, grid_line, grid_line - grid_size)
    return 2.0 * math.pi / (grid_size * spacing) * signed_line.astype(jnp.float32)


def table_angles(grid_size):
    row_index = lax.broadcasted_iota(jnp.int32, (grid_size, grid_size), 0)
    col_index = lax.broadcasted_iota(jnp.int32, (grid_size, grid_size), 1)
    return 2.0 * math.pi / grid_size * (row_index * col_index % grid_size).astype(jnp.float32)


def line_matrices(shifts, grid_size):
    numbers = wave_numbers(lax.iota(jnp.int32, grid_size), grid_size)
    along = shifts[:, None] + numbers[None, :]
    phase = 0.5 * sub_time * (along * along)
    angles = table_angles(grid_size)
    cosine, sine = jnp.cos(angles), jnp.sin(angles)
    q_real, q_imag = jnp.cos(phase)[:, None, :], -jnp.sin(phase)[:, None, :]
    left_real = (cosine * q_real - sine * q_imag) / grid_size
    left_imag = (cosine * q_imag + sine * q_real) / grid_size
    both = jnp.stack([left_real, left_imag])
    by_cos = jnp.einsum("csam,mb->csab", both, cosine, precision=highest)
    by_sin = jnp.einsum("csam,mb->csab", both, sine, precision=highest)
    return by_cos[0] + by_sin[1], by_cos[1] - by_sin[0]


def real_form(real_part, imag_part):
    upper = jnp.stack([real_part, -imag_part], axis=-2)
    lower = jnp.stack([imag_part, real_part], axis=-2)
    return jnp.stack([upper, lower], axis=-4)


def spin(field, angle):
    cosine, sine = jnp.cos(angle), jnp.sin(angle)
    return jnp.stack(
        [field[0] * cosine + field[1] * sine, field[1] * cosine - field[0] * sine]
    )


def apply(form, matrix, field):
    return jnp.einsum(
        form, matrix, field, precision=lax.Precision.HIGHEST, preferred_element_type=jnp.float32
    )


def plain(orbitals, costate, potential, xc_kernel, vector_potential, kpoint_weight, occupation):
    grid_size = potential.shape[1]
    k_index = lax.axis_index("ka")
    fft_index = lax.axis_index("fft")
    planes = potential.shape[0]
    lattice_unit = 2.0 * math.pi / (grid_size * spacing)
    k_fraction = (k_index.astype(jnp.float32) + 0.5) / lax.axis_size("ka") - 0.5
    shifts = jnp.concatenate(
        [
            lattice_unit * k_fraction + vector_potential,
            jnp.array([lattice_unit * 0.25, -lattice_unit * 0.25], jnp.float32),
        ]
    )
    lines = real_form(*line_matrices(shifts, grid_size))
    back = jnp.transpose(lines, (0, 3, 4, 1, 2))

    def to_columns(field, split, concat):
        return lax.all_to_all(field, "fft", split_axis=split, concat_axis=concat, tiled=True)

    pot_rows = 0.5 * sub_time * potential
    pot_cols = to_columns(pot_rows, 1, 0)

    def propagate(field, step_index, sign):
        table = lines if sign > 0 else back
        order = range(SUB) if sign > 0 else range(SUB - 1, -1, -1)
        mat_y, mat_z = table[STEPS * SUB], table[STEPS * SUB + 1]
        in_rows = True
        field = spin(field, sign * pot_rows)
        for count, sub_index in enumerate(order):
            mat_x = table[step_index * SUB + sub_index]
            last = count == SUB - 1
            turn = sign * (1.0 if last else 2.0)
            field = apply("cadb,dkxyb->ckxya", mat_z, field)
            if in_rows:
                field = apply("cadb,dkxbz->ckxaz", mat_y, field)
                field = to_columns(field, 3, 2)
                field = apply("cadb,dkbyz->ckayz", mat_x, field)
                field = spin(field, turn * pot_cols)
            else:
                field = apply("cadb,dkbyz->ckayz", mat_x, field)
                field = to_columns(field, 2, 3)
                field = apply("cadb,dkxbz->ckxaz", mat_y, field)
                field = spin(field, turn * pot_rows)
            in_rows = not in_rows
        return field

    def parts_first(field):
        bands = field.shape[0] * field.shape[1]
        return jnp.moveaxis(field, 2, 0).reshape((2, bands) + field.shape[3:])

    angles = table_angles(grid_size)
    cas = (jnp.cos(angles) + jnp.sin(angles)) / math.sqrt(grid_size)
    numbers = wave_numbers(lax.iota(jnp.int32, grid_size), grid_size)
    numbers_local = wave_numbers(fft_index * planes + lax.iota(jnp.int32, planes), grid_size)
    g_squared = (
        (numbers * numbers)[:, None, None]
        + (numbers_local * numbers_local)[None, :, None]
        + (numbers * numbers)[None, None, :]
    )
    coulomb = jnp.where(
        g_squared > 0, 4.0 * math.pi / jnp.where(g_squared > 0, g_squared, 1.0), 0.0
    )
    orbital = parts_first(orbitals)
    history = [orbital]
    for step_index in range(STEPS):
        orbital = propagate(orbital, step_index, 1.0)
        history.append(orbital)
    occupied = occupation.astype(jnp.float32) / 100.0
    own_weight = lax.dynamic_slice_in_dim(kpoint_weight, k_index, 1)[0].astype(jnp.float32)
    weight = own_weight / jnp.sum(kpoint_weight).astype(jnp.float32)
    band_factor = 2.0 * weight * occupied
    adjoint = parts_first(costate)
    cross_pot = jnp.zeros_like(potential)
    for step_index in range(STEPS - 1, -1, -1):
        forward = history[step_index + 1]
        density = lax.psum(
            jnp.sum(band_factor[:, None, None, None] * jnp.sum(adjoint * forward, axis=0), axis=0),
            "ka",
        )
        hartree = apply("ab,xyb->xya", cas, density)
        hartree = apply("ab,xbz->xaz", cas, hartree)
        hartree = to_columns(hartree, 1, 0)
        hartree = apply("ab,byz->ayz", cas, hartree)
        hartree = apply("ab,byz->ayz", cas, hartree * coulomb)
        hartree = to_columns(hartree, 0, 1)
        hartree = apply("ab,xbz->xaz", cas, hartree)
        hartree = apply("ab,xyb->xya", cas, hartree)
        cross_pot = hartree + xc_kernel * density
        turned = jnp.stack([forward[1], -forward[0]])
        adjoint = propagate(adjoint + step_time * cross_pot * turned, step_index, -1.0)
    result = jnp.moveaxis(adjoint.reshape((2,) + orbitals.shape[:2] + adjoint.shape[2:]), 0, 2)
    return (result, cross_pot)


ROWS = 128
PLANES = 8
QUARTER = 4
AXES = ("ka", "fft")


def halves_of(value):
    high = value.astype(jnp.bfloat16)
    return high, (value - high.astype(jnp.float32)).astype(jnp.bfloat16)


def from_left(table, field):
    size = table.shape[1] // 2
    high, low = halves_of(field)
    return jnp.dot(
        jnp.concatenate([table[:, :size], table], axis=1),
        jnp.concatenate([high, low, high], axis=0),
        preferred_element_type=jnp.float32,
    )


def from_right(field, table):
    size = table.shape[0] // 2
    high, low = halves_of(field)
    return jnp.dot(
        jnp.concatenate([high, low, high], axis=1),
        jnp.concatenate([table[:size], table], axis=0),
        preferred_element_type=jnp.float32,
    )


def side_by_side(matrix, axis):
    return jnp.concatenate(halves_of(matrix), axis=axis)


def circulant(shift, numbers, cosine, sine):
    along = shift + numbers
    phase = 0.5 * sub_time * (along * along)
    q_real, q_imag = jnp.cos(phase), -jnp.sin(phase)
    even = q_real * cosine + q_imag * sine
    odd = q_real * sine - q_imag * cosine
    spectrum = jnp.concatenate(
        [jnp.concatenate([even, odd], axis=1), jnp.concatenate([odd, -even], axis=1)], axis=0
    )
    upper = jnp.dot(
        jnp.concatenate([cosine, sine], axis=1),
        spectrum,
        precision=highest,
        preferred_element_type=jnp.float32,
    ) * (1.0 / ROWS)
    real_part, minus = upper[:, :ROWS], upper[:, ROWS:]
    real_turned, minus_turned = real_part.T, minus.T
    return upper, jnp.concatenate([real_turned, -minus_turned], axis=1)


def whole_matrix(upper):
    real_part, minus = upper[:, :ROWS], upper[:, ROWS:]
    return jnp.concatenate([upper, jnp.concatenate([-minus, real_part], axis=1)], axis=0)


def whole_left(table):
    return jnp.concatenate(
        [whole_matrix(table[:, : 2 * ROWS]), whole_matrix(table[:, 2 * ROWS :])], axis=1
    )


def table_kernel(count_x, shift_ref, numbers_ref, lines_ref, *out_refs):
    numbers, cosine, sine = numbers_ref[...], lines_ref[:, :ROWS], lines_ref[:, ROWS:]
    for line in range(count_x + 1):
        matrix, turned = circulant(shift_ref[line], numbers, cosine, sine)
        out_refs[2 * line][...] = side_by_side(matrix, 1)
        out_refs[2 * line + 1][...] = side_by_side(turned, 1)
    matrix, turned = circulant(shift_ref[count_x + 1], numbers, cosine, sine)
    out_refs[2 * count_x + 2][...] = side_by_side(whole_matrix(turned), 0)
    out_refs[2 * count_x + 3][...] = side_by_side(whole_matrix(matrix), 0)


def cos_sin(angle):
    square = angle * angle
    cosine = sine = 1.0
    for order in range(10, 0, -2):
        cosine = 1.0 - cosine * (square * (1.0 / (order * (order - 1))))
        sine = 1.0 - sine * (square * (1.0 / (order * (order + 1))))
    return cosine, sine * angle


def rotated(sign, real_part, imag_part, cosine, sine):
    if sign > 0:
        return real_part * cosine + imag_part * sine, imag_part * cosine - real_part * sine
    return real_part * cosine - imag_part * sine, imag_part * cosine + real_part * sine


def doubled(cosine, sine):
    return 1.0 - 2.0 * (sine * sine), 2.0 * sine * cosine


def place_of(block, blocks):
    core, rest = divmod(block, blocks // 2)
    return rest // 2 * 4 + core * 2 + rest % 2


def gathered(ref, *index):
    blocks = ref.shape[0]
    return jnp.concatenate(
        [ref[(place_of(block, blocks),) + index] for block in range(blocks)], axis=0
    )


def gather_planes(ref):
    return jnp.concatenate(
        [
            jnp.concatenate([gathered(ref, part, plane) for plane in range(PLANES)], axis=1)
            for part in range(2)
        ],
        axis=0,
    )


def natural(ref):
    return jnp.concatenate([ref[plane] for plane in range(PLANES)], axis=1)


def lane(value, plane):
    return value[:, plane * ROWS : (plane + 1) * ROWS]


def sources_of(blocks):
    half = blocks // 2
    return [
        block // half * blocks + place_of(core * half + block % half, blocks)
        for block in range(blocks)
        for core in range(2)
    ]


def rows_to(out_ref, block, index, plane, piece):
    if not isinstance(out_ref, tuple):
        place = place_of(block, out_ref.shape[0])
        out_ref[(place,) + index + (pl.ds(plane, PLANES, stride=PLANES), slice(None))] = piece
        return
    sources = sources_of(out_ref[0].shape[0] // 2)
    for core in range(2):
        at = (sources[2 * block + core],) + index
        out_ref[0][at + (pl.ds(plane, QUARTER, stride=PLANES), slice(None))] = piece[
            core * QUARTER : (core + 1) * QUARTER
        ]


def turn_z(real_part, imag_part, table):
    rows = jnp.concatenate(
        [
            jnp.concatenate([lane(real_part, plane), lane(imag_part, plane)], axis=1)
            for plane in range(PLANES)
        ],
        axis=0,
    )
    return from_right(rows, table)


def scatter_planes(real_part, imag_part, table, out_ref):
    blocks = ROWS // PLANES
    turned = turn_z(real_part, imag_part, table)
    for plane in range(PLANES):
        for part in range(2):
            piece = turned[plane * ROWS : (plane + 1) * ROWS, part * ROWS : (part + 1) * ROWS]
            for block in range(blocks):
                rows_of = piece[block * PLANES : (block + 1) * PLANES]
                rows_to(out_ref, block, (part,), plane, rows_of)


def between(sign, field, cosine, sine, first_ref, second_ref, right_ref, out_ref):
    field = from_left(whole_left(first_ref[...]), field)
    real_part, imag_part = rotated(sign, field[:ROWS], field[ROWS:], *doubled(cosine, sine))
    field = from_left(
        whole_left(second_ref[...]), jnp.concatenate([real_part, imag_part], axis=0)
    )
    scatter_planes(field[:ROWS], field[ROWS:], right_ref[...], out_ref)


def mid_kernel(
    sign, field_ref, cosine_ref, sine_ref, first_ref, second_ref, right_ref, out_ref
):
    cosine, sine = natural(cosine_ref), natural(sine_ref)
    field = gather_planes(field_ref)
    between(sign, field, cosine, sine, first_ref, second_ref, right_ref, out_ref)


def first_mid_kernel(
    sign, field_ref, first_ref, second_ref, right_ref, out_ref, cosine_ref, sine_ref
):
    blocks = field_ref.shape[0] // 2

    def part_of(part):
        return jnp.concatenate(
            [
                jnp.concatenate(
                    [
                        field_ref[source, part, pl.ds(plane * QUARTER, QUARTER), :]
                        for source in sources_of(blocks)
                    ],
                    axis=0,
                )
                for plane in range(PLANES)
            ],
            axis=1,
        )

    pot = part_of(2)
    for plane in range(PLANES):
        for block in range(blocks):
            rows_of = lane(pot, plane)[block * PLANES : (block + 1) * PLANES]
            rows_to(out_ref, block, (2,), plane, rows_of)
    cosine, sine = cos_sin(0.5 * sub_time * pot)
    store_natural(cosine_ref, cosine)
    store_natural(sine_ref, sine)
    field = jnp.concatenate([part_of(0), part_of(1)], axis=0)
    between(sign, field, cosine, sine, first_ref, second_ref, right_ref, out_ref)


def second_mid_kernel(
    sign, field_ref, first_ref, second_ref, right_ref, out_ref, cosine_ref, sine_ref
):
    pot = jnp.concatenate([gathered(field_ref, 2, plane) for plane in range(PLANES)], axis=1)
    cosine, sine = cos_sin(0.5 * sub_time * pot)
    store_natural(cosine_ref, cosine)
    store_natural(sine_ref, sine)
    field = gather_planes(field_ref)
    between(sign, field, cosine, sine, first_ref, second_ref, right_ref, out_ref)


def last_mid_kernel(
    sign, field_ref, cosine_ref, sine_ref, first_ref, second_ref, right_ref, out_ref
):
    cosine, sine = natural(cosine_ref), natural(sine_ref)
    field = gather_planes(field_ref)
    between(sign, field, cosine, sine, first_ref, second_ref, right_ref, (out_ref,))


def store_natural(ref, value):
    for plane in range(PLANES):
        ref[plane] = lane(value, plane)


def finish(sign, field_ref, cosine, sine, first_ref, real_ref, imag_ref):
    field = from_left(whole_left(first_ref[...]), gather_planes(field_ref))
    real_part, imag_part = rotated(sign, field[:ROWS], field[ROWS:], cosine, sine)
    store_natural(real_ref, real_part)
    store_natural(imag_ref, imag_part)
    return real_part, imag_part


def begin(sign, real_part, imag_part, cosine, sine, second, right, out_ref):
    real_part, imag_part = rotated(sign, real_part, imag_part, cosine, sine)
    field = from_left(second, jnp.concatenate([real_part, imag_part], axis=0))
    scatter_planes(field[:ROWS], field[ROWS:], right, out_ref)


def step_kernel(
    sign,
    field_ref,
    cosine_ref,
    sine_ref,
    first_ref,
    second_ref,
    right_ref,
    out_ref,
    real_ref,
    imag_ref,
):
    cosine, sine = natural(cosine_ref), natural(sine_ref)
    parts = finish(sign, field_ref, cosine, sine, first_ref, real_ref, imag_ref)
    begin(sign, *parts, cosine, sine, whole_left(second_ref[...]), right_ref[...], out_ref)


def plane_order(core):
    return [core * QUARTER + number for number in range(QUARTER)] + [
        (1 - core) * QUARTER + number for number in range(QUARTER)
    ]


def start_kernel(
    unit, field_ref, pot_ref, lines_ref, keep_ref, give_ref, numbers_ref, field, pot, lines, sems
):
    copies = [
        pltpu.make_async_copy(source, target, sems.at[number])
        for number, (source, target) in enumerate(
            ((lines_ref, lines), (pot_ref, pot), (field_ref, field))
        )
    ]
    for copy in copies:
        copy.start()
    order = plane_order(lax.axis_index("ka"))
    index = lax.broadcasted_iota(jnp.int32, (ROWS, ROWS), 0)
    numbers = wave_numbers(index, ROWS)
    numbers_ref[...] = numbers
    copies[0].wait()
    cosine_line, sine_line = lines[:, :ROWS], lines[:, ROWS:]
    table_y = circulant(0.25 * unit, numbers, cosine_line, sine_line)[0]
    table_z = circulant(-0.25 * unit, numbers, cosine_line, sine_line)[1]
    copies[1].wait()
    blocks = ROWS // PLANES

    def put(ref, part, plane, piece):
        for block in range(blocks):
            ref[place_of(block, blocks), part, pl.ds(plane, PLANES, stride=QUARTER), :] = piece[
                block * PLANES : (block + 1) * PLANES
            ]

    for number in range(QUARTER):
        put(keep_ref, 2, number, pot[order[number]])
    cosine, sine = cos_sin(
        0.5 * sub_time * jnp.concatenate([pot[plane] for plane in order], axis=1)
    )
    copies[2].wait()
    real_part, imag_part = rotated(
        1.0,
        jnp.concatenate([field[0, 0, 0, plane] for plane in order], axis=1),
        jnp.concatenate([field[0, 0, 1, plane] for plane in order], axis=1),
        cosine,
        sine,
    )
    turned = from_left(
        side_by_side(whole_matrix(table_y), 1), jnp.concatenate([real_part, imag_part], axis=0)
    )
    turned = turn_z(turned[:ROWS], turned[ROWS:], side_by_side(whole_matrix(table_z), 0))
    for number in range(PLANES):
        ref = keep_ref if number < QUARTER else give_ref
        for part in range(2):
            piece = turned[number * ROWS : (number + 1) * ROWS, part * ROWS : (part + 1) * ROWS]
            put(ref, part, number % QUARTER, piece)


def join_kernel(keep_ref, got_ref, out_ref):
    core = lax.axis_index("ka")
    out_ref[core] = keep_ref[...]
    out_ref[1 - core, :, 0:2] = got_ref[...]
    out_ref[1 - core, :, 2] = keep_ref[:, 2]


def end_kernel(
    sign,
    field_ref,
    cosine_ref,
    sine_ref,
    first_ref,
    other_real_ref,
    other_imag_ref,
    factor_ref,
    real_ref,
    imag_ref,
    density_ref,
):
    cosine, sine = natural(cosine_ref), natural(sine_ref)
    real_part, imag_part = finish(
        sign, field_ref, cosine, sine, first_ref, real_ref, imag_ref
    )
    factor = factor_ref[0, 0]
    for plane in range(PLANES):
        density_ref[plane] = factor * (
            lane(real_part, plane) * other_real_ref[plane]
            + lane(imag_part, plane) * other_imag_ref[plane]
        )


def final_kernel(sign, field_ref, got_ref, pot_ref, first_ref, out_ref):
    core = lax.axis_index("ka")
    order = plane_order(core)
    blocks = got_ref.shape[0]

    def part_of(part):
        planes = []
        for number in range(PLANES):
            at = (part, pl.ds(number % QUARTER * PLANES, PLANES), slice(None))
            rows = [
                field_ref[(core, place_of(block, blocks)) + at]
                if number < QUARTER
                else got_ref[(place_of(block, blocks),) + at]
                for block in range(blocks)
            ]
            planes.append(jnp.concatenate(rows, axis=0))
        return jnp.concatenate(planes, axis=1)

    cosine, sine = cos_sin(
        0.5 * sub_time * jnp.concatenate([pot_ref[plane] for plane in order], axis=1)
    )
    field = from_left(
        whole_left(first_ref[...]), jnp.concatenate([part_of(0), part_of(1)], axis=0)
    )
    real_part, imag_part = rotated(sign, field[:ROWS], field[ROWS:], cosine, sine)
    for number, plane in enumerate(order):
        out_ref[0, 0, 0, plane] = lane(real_part, number)
        out_ref[0, 0, 1, plane] = lane(imag_part, number)


def stack_planes(value):
    return jnp.concatenate([lane(value, plane) for plane in range(PLANES)], axis=0)


def density_kernel(own_ref, other_ref, left_ref, right_ref, density_ref, out_ref):
    density = natural(own_ref) + natural(other_ref)
    store_natural(density_ref, density)
    spectrum = from_right(stack_planes(from_left(left_ref[...], density)), right_ref[...])
    for plane in range(PLANES):
        for block in range(ROWS // PLANES):
            start = plane * ROWS + block * PLANES
            rows_to(out_ref, block, (), plane, spectrum[start : start + PLANES])


def coulomb_kernel(unit, field_ref, square_ref, left_ref, out_ref):
    blocks = field_ref.shape[0]
    rows = jnp.concatenate([gathered(field_ref, line) for line in range(PLANES)], axis=1)
    rows = from_left(left_ref[...], rows)
    index = lax.broadcasted_iota(jnp.int32, (ROWS, ROWS), 0)
    number = unit * jnp.where(index < ROWS // 2, index, index - ROWS).astype(jnp.float32)
    along = number * number
    parts = []
    for line in range(PLANES):
        square = along + square_ref[pl.ds(line, 1), :]
        nonzero = square > 0
        inverse = jnp.where(nonzero, 4.0 * math.pi / jnp.where(nonzero, square, 1.0), 0.0)
        parts.append(lane(rows, line) * inverse)
    rows = from_left(left_ref[...], jnp.concatenate(parts, axis=1))
    for line in range(PLANES):
        for block in range(blocks):
            out_ref[place_of(block, blocks), line] = lane(rows, line)[
                block * PLANES : (block + 1) * PLANES
            ]


def hartree_kernel(
    sign,
    field_ref,
    density_ref,
    xc_ref,
    orbital_real_ref,
    orbital_imag_ref,
    adjoint_real_ref,
    adjoint_imag_ref,
    cosine_ref,
    sine_ref,
    cas_left_ref,
    cas_right_ref,
    second_ref,
    right_ref,
    out_ref,
    cross_ref,
):
    spectrum = jnp.concatenate(
        [gathered(field_ref, pl.ds(plane, PLANES, stride=PLANES)) for plane in range(PLANES)],
        axis=1,
    )
    hartree = from_right(
        stack_planes(from_left(cas_left_ref[...], spectrum)), cas_right_ref[...]
    )
    real_parts, imag_parts = [], []
    for plane in range(PLANES):
        cross = hartree[plane * ROWS : (plane + 1) * ROWS] + xc_ref[plane] * density_ref[plane]
        cross_ref[plane] = cross
        real_parts.append(adjoint_real_ref[plane] + step_time * cross * orbital_imag_ref[plane])
        imag_parts.append(adjoint_imag_ref[plane] - step_time * cross * orbital_real_ref[plane])
    begin(
        sign,
        jnp.concatenate(real_parts, axis=1),
        jnp.concatenate(imag_parts, axis=1),
        natural(cosine_ref),
        natural(sine_ref),
        whole_left(second_ref[...]),
        right_ref[...],
        out_ref,
    )


def run(kernel, outputs, *operands, space=pltpu.VMEM, scratch=()):
    made = pl.pallas_call(
        kernel,
        out_shape=[
            jax.ShapeDtypeStruct(out, jnp.float32) if isinstance(out, tuple) else out
            for out in outputs
        ],
        in_specs=[
            pl.BlockSpec(memory_space=pltpu.SMEM if operand.size < ROWS else space)
            for operand in operands
        ],
        out_specs=[pl.BlockSpec(memory_space=pltpu.VMEM) for _ in outputs],
        scratch_shapes=list(scratch),
        compiler_params=pltpu.CompilerParams(vmem_limit_bytes=24 * 2**20),
    )(*operands)
    return made[0] if len(outputs) == 1 else made


def grouped(
    orbitals, costate, potential, xc_kernel, vector_potential, kpoint_weight, occupation
):
    grid_size = potential.shape[1]
    blocks = lax.axis_size("fft")
    half = blocks // 2
    core = lax.axis_index("ka")
    fft_index = lax.axis_index("fft")
    side = fft_index // half
    place = core * half + fft_index % half
    lattice_unit = 2.0 * math.pi / (grid_size * spacing)

    groups = []
    for h in range(2):
        devices = [c * blocks + h * half + j for c in range(2) for j in range(half)]
        group = [0] * blocks
        for block, device in enumerate(devices):
            group[place_of(block, blocks)] = device
        groups.append(group)
    regroup = []
    for c in range(2):
        for f in range(blocks):
            h, j = f // half, f % half
            regroup.append((c * blocks + f, h * blocks + c * half + j))
    across = [
        (c * blocks + f, c * blocks + (f + half) % blocks) for c in range(2) for f in range(blocks)
    ]

    def exchange(array):
        return lax.all_to_all(array, AXES, 0, 0, axis_index_groups=groups, tiled=True)

    def exchange_all(array):
        return lax.all_to_all(
            array, AXES, 0, 0, axis_index_groups=[groups[0] + groups[1]], tiled=True
        )

    def move(array, pairs):
        return lax.ppermute(array, AXES, pairs)

    block_shape = (blocks, 2, PLANES, PLANES, ROWS)
    sent_shape = (blocks, 2, PLANES * PLANES, ROWS)
    natural_shape = (2, PLANES, ROWS, ROWS)
    real_shape = (PLANES, ROWS, ROWS)

    def swap_field(array):
        return exchange(array.reshape(block_shape))

    grid_line = np.arange(grid_size)
    angles = 2.0 * np.pi / grid_size * (np.outer(grid_line, grid_line) % grid_size)
    line_pair = jnp.asarray(
        np.concatenate([np.cos(angles), np.sin(angles)], axis=1).astype(np.float32)
    )
    cas = (np.cos(angles) + np.sin(angles)) / math.sqrt(grid_size)
    cas_high = cas.astype(jnp.bfloat16)
    cas_low = (cas - cas_high.astype(np.float64)).astype(jnp.bfloat16)
    cas_left = jnp.asarray(np.concatenate([cas_high, cas_low], axis=1))
    cas_right = jnp.asarray(np.concatenate([cas_high, cas_low], axis=0))

    shift_x = lattice_unit * ((side.astype(jnp.float32) + 0.5) / 2 - 0.5) + vector_potential
    shift_yz = jnp.array([lattice_unit * 0.25, -lattice_unit * 0.25], jnp.float32)
    count_x = STEPS * SUB

    numbers = wave_numbers(lax.iota(jnp.int32, grid_size), grid_size)
    own_numbers = wave_numbers(place * PLANES + lax.iota(jnp.int32, PLANES), grid_size)
    squares = (own_numbers * own_numbers)[:, None] + (numbers * numbers)[None, :]

    occupied = occupation.astype(jnp.float32) / 100.0
    own_weight = lax.dynamic_slice_in_dim(kpoint_weight, side, 1)[0].astype(jnp.float32)
    weight = own_weight / jnp.sum(kpoint_weight).astype(jnp.float32)
    factor = (2.0 * weight * occupied).reshape(1, 1)

    keep, give, numbers_full = run(
        functools.partial(start_kernel, lattice_unit),
        [
            (blocks, 3, PLANES * QUARTER, ROWS),
            (blocks, 2, PLANES * QUARTER, ROWS),
            (ROWS, ROWS),
        ],
        orbitals,
        potential,
        line_pair,
        space=pltpu.HBM,
        scratch=[
            pltpu.VMEM(orbitals.shape, jnp.float32),
            pltpu.VMEM(real_shape, jnp.float32),
            pltpu.VMEM((ROWS, 2 * ROWS), jnp.float32),
            pltpu.SemaphoreType.DMA((3,)),
        ],
    )
    cores = [(0, 1), (1, 0)]
    sent = run(
        join_kernel,
        [(2, blocks, 3, PLANES * QUARTER, ROWS)],
        keep,
        lax.ppermute(give, "ka", cores),
    )
    field = exchange_all(sent.reshape(2 * blocks, 3, PLANES * QUARTER, ROWS))
    left_shape = jax.ShapeDtypeStruct((ROWS, 4 * ROWS), jnp.bfloat16)
    right_shape = jax.ShapeDtypeStruct((4 * ROWS, 2 * ROWS), jnp.bfloat16)
    made = run(
        functools.partial(table_kernel, count_x),
        [left_shape] * (2 * count_x + 2) + [right_shape] * 2,
        jnp.concatenate([shift_x, shift_yz]),
        numbers_full,
        line_pair,
    )
    early = (squares, factor, jnp.stack([costate[0, 0, 0], costate[0, 0, 1], xc_kernel]))
    field, made, early = lax.optimization_barrier((field, made, early))
    squares, factor, moving = early
    tables = {1.0: made[0 : 2 * count_x + 2 : 2], -1.0: made[1 : 2 * count_x + 2 : 2]}
    right_z = {1.0: made[-2], -1.0: made[-1]}

    def table_x(sign, count):
        return tables[sign][count if sign > 0 else count_x - 1 - count]

    def table_y(sign):
        return tables[sign][count_x]

    def tables_of(sign, count):
        if count % 2 == 0:
            return table_y(sign), table_y(sign), right_z[sign]
        return table_x(sign, count - 1), table_x(sign, count), right_z[sign]

    def middle(sign, field, count):
        waves = waves_rows if count % 2 == 0 else waves_cols
        return run(
            functools.partial(mid_kernel, sign),
            [sent_shape],
            field,
            *waves,
            *tables_of(sign, count),
        )

    sent, *waves_cols = run(
        functools.partial(first_mid_kernel, 1.0),
        [(blocks, 3) + sent_shape[2:], real_shape, real_shape],
        field,
        *tables_of(1.0, 1),
    )
    sent, moving = lax.optimization_barrier((sent, moving))
    moving = move(moving, regroup)
    sent, *waves_rows = run(
        functools.partial(second_mid_kernel, 1.0),
        [sent_shape, real_shape, real_shape],
        exchange(sent.reshape(blocks, 3, PLANES, PLANES, ROWS)),
        *tables_of(1.0, 2),
    )
    sent = middle(1.0, swap_field(sent), 3)
    sent, moving = lax.optimization_barrier((sent, moving))
    kept = []
    for count in range(4, count_x):
        field = swap_field(sent)
        if count % SUB == 0:
            sent, *orbital = run(
                functools.partial(step_kernel, 1.0),
                [sent_shape, real_shape, real_shape],
                field,
                *waves_rows,
                *tables_of(1.0, count),
            )
            kept.append(orbital)
        else:
            sent = middle(1.0, field, count)
    adjoint, xc_rows = [moving[0], moving[1]], moving[2]
    *orbital, partial = run(
        functools.partial(end_kernel, 1.0),
        [real_shape] * 3,
        swap_field(sent),
        *waves_rows,
        table_y(1.0),
        *adjoint,
        factor,
    )
    kept.append(orbital)

    for step_index in range(STEPS - 1, -1, -1):
        density, sent = run(
            density_kernel,
            [real_shape, (blocks, PLANES * PLANES, ROWS)],
            partial,
            move(partial, across),
            cas_left,
            cas_right,
        )
        field = exchange(sent.reshape(blocks, PLANES, PLANES, ROWS))
        sent = run(
            functools.partial(coulomb_kernel, lattice_unit),
            [(blocks, PLANES, PLANES, ROWS)],
            field,
            squares,
            cas_left,
        )
        field = exchange(sent).reshape(blocks, PLANES * PLANES, ROWS)
        sent, cross = run(
            functools.partial(hartree_kernel, -1.0),
            [sent_shape, real_shape],
            field,
            density,
            xc_rows,
            *kept[step_index],
            *adjoint,
            *waves_rows,
            cas_left,
            cas_right,
            table_y(-1.0),
            right_z[-1.0],
        )
        first = (STEPS - 1 - step_index) * SUB
        for count in range(first + 1, first + SUB - 1):
            sent = middle(-1.0, swap_field(sent), count)
        field = swap_field(sent)
        if step_index > 0:
            sent = middle(-1.0, field, first + SUB - 1)
            *adjoint, partial = run(
                functools.partial(end_kernel, -1.0),
                [real_shape] * 3,
                swap_field(sent),
                *waves_rows,
                table_y(-1.0),
                *kept[step_index - 1],
                factor,
            )
    sent = run(
        functools.partial(last_mid_kernel, -1.0),
        [(2 * blocks, 2, PLANES * QUARTER, ROWS)],
        field,
        *waves_cols,
        *tables_of(-1.0, count_x - 1),
    )
    field = exchange_all(sent).reshape(2, blocks, 2, PLANES * QUARTER, ROWS)
    give = lax.dynamic_index_in_dim(field, 1 - core, 0, keepdims=False)
    result = run(
        functools.partial(final_kernel, -1.0),
        [orbitals.shape],
        field,
        lax.ppermute(give, "ka", cores),
        potential,
        table_y(-1.0),
    )
    beside = lax.ppermute(cross, "ka", [(0, 1), (1, 0)])
    return (result, jnp.where(core == side, cross, beside))


def solution(mesh):
    placed = (
        P("ka", None, None, "fft", None, None),
        P("ka", None, None, "fft", None, None),
        P("fft", None, None),
        P("fft", None, None),
        P(),
        P(),
        P(),
    )

    def local(*arguments):
        orbitals, potential = arguments[0], arguments[2]
        fits = (
            mesh.shape["ka"] == 2
            and mesh.shape["fft"] % 2 == 0
            and orbitals.shape[:2] == (1, 1)
            and potential.shape == (PLANES, ROWS, ROWS)
        )
        return grouped(*arguments) if fits else plain(*arguments)

    return jax.shard_map(
        local,
        mesh=mesh,
        in_specs=placed,
        out_specs=(P("ka", None, None, "fft", None, None), P("fft", None, None)),
        check_vma=False,
    )
```

```python
import functools
import math

import jax
import jax.numpy as jnp
import numpy as np
from jax import lax
from jax.experimental import pallas as pl
from jax.experimental.pallas import tpu as pltpu
from jax.sharding import PartitionSpec as P

STEPS = 2
SUB = 4


spacing = 0.25
step_time = 0.6
sub_time = step_time / SUB
highest = lax.Precision.HIGHEST


def wave_numbers(grid_line, grid_size):
    signed_line = jnp.where(grid_line < grid_size // 2, grid_line, grid_line - grid_size)
    return 2.0 * math.pi / (grid_size * spacing) * signed_line.astype(jnp.float32)


def table_angles(grid_size):
    row_index = lax.broadcasted_iota(jnp.int32, (grid_size, grid_size), 0)
    col_index = lax.broadcasted_iota(jnp.int32, (grid_size, grid_size), 1)
    return 2.0 * math.pi / grid_size * (row_index * col_index % grid_size).astype(jnp.float32)


def line_matrices(shifts, grid_size):
    numbers = wave_numbers(lax.iota(jnp.int32, grid_size), grid_size)
    along = shifts[:, None] + numbers[None, :]
    phase = 0.5 * sub_time * (along * along)
    angles = table_angles(grid_size)
    cosine, sine = jnp.cos(angles), jnp.sin(angles)
    q_real, q_imag = jnp.cos(phase)[:, None, :], -jnp.sin(phase)[:, None, :]
    left_real = (cosine * q_real - sine * q_imag) / grid_size
    left_imag = (cosine * q_imag + sine * q_real) / grid_size
    both = jnp.stack([left_real, left_imag])
    by_cos = jnp.einsum("csam,mb->csab", both, cosine, precision=highest)
    by_sin = jnp.einsum("csam,mb->csab", both, sine, precision=highest)
    return by_cos[0] + by_sin[1], by_cos[1] - by_sin[0]


def real_form(real_part, imag_part):
    upper = jnp.stack([real_part, -imag_part], axis=-2)
    lower = jnp.stack([imag_part, real_part], axis=-2)
    return jnp.stack([upper, lower], axis=-4)


def spin(field, angle):
    cosine, sine = jnp.cos(angle), jnp.sin(angle)
    return jnp.stack(
        [field[0] * cosine + field[1] * sine, field[1] * cosine - field[0] * sine]
    )


def apply(form, matrix, field):
    return jnp.einsum(
        form, matrix, field, precision=lax.Precision.HIGHEST, preferred_element_type=jnp.float32
    )


def plain(orbitals, costate, potential, xc_kernel, vector_potential, kpoint_weight, occupation):
    grid_size = potential.shape[1]
    k_index = lax.axis_index("ka")
    fft_index = lax.axis_index("fft")
    planes = potential.shape[0]
    lattice_unit = 2.0 * math.pi / (grid_size * spacing)
    k_fraction = (k_index.astype(jnp.float32) + 0.5) / lax.axis_size("ka") - 0.5
    shifts = jnp.concatenate(
        [
            lattice_unit * k_fraction + vector_potential,
            jnp.array([lattice_unit * 0.25, -lattice_unit * 0.25], jnp.float32),
        ]
    )
    lines = real_form(*line_matrices(shifts, grid_size))
    back = jnp.transpose(lines, (0, 3, 4, 1, 2))

    def to_columns(field, split, concat):
        return lax.all_to_all(field, "fft", split_axis=split, concat_axis=concat, tiled=True)

    pot_rows = 0.5 * sub_time * potential
    pot_cols = to_columns(pot_rows, 1, 0)

    def propagate(field, step_index, sign):
        table = lines if sign > 0 else back
        order = range(SUB) if sign > 0 else range(SUB - 1, -1, -1)
        mat_y, mat_z = table[STEPS * SUB], table[STEPS * SUB + 1]
        in_rows = True
        field = spin(field, sign * pot_rows)
        for count, sub_index in enumerate(order):
            mat_x = table[step_index * SUB + sub_index]
            last = count == SUB - 1
            turn = sign * (1.0 if last else 2.0)
            field = apply("cadb,dkxyb->ckxya", mat_z, field)
            if in_rows:
                field = apply("cadb,dkxbz->ckxaz", mat_y, field)
                field = to_columns(field, 3, 2)
                field = apply("cadb,dkbyz->ckayz", mat_x, field)
                field = spin(field, turn * pot_cols)
            else:
                field = apply("cadb,dkbyz->ckayz", mat_x, field)
                field = to_columns(field, 2, 3)
                field = apply("cadb,dkxbz->ckxaz", mat_y, field)
                field = spin(field, turn * pot_rows)
            in_rows = not in_rows
        return field

    def parts_first(field):
        bands = field.shape[0] * field.shape[1]
        return jnp.moveaxis(field, 2, 0).reshape((2, bands) + field.shape[3:])

    angles = table_angles(grid_size)
    cas = (jnp.cos(angles) + jnp.sin(angles)) / math.sqrt(grid_size)
    numbers = wave_numbers(lax.iota(jnp.int32, grid_size), grid_size)
    numbers_local = wave_numbers(fft_index * planes + lax.iota(jnp.int32, planes), grid_size)
    g_squared = (
        (numbers * numbers)[:, None, None]
        + (numbers_local * numbers_local)[None, :, None]
        + (numbers * numbers)[None, None, :]
    )
    coulomb = jnp.where(
        g_squared > 0, 4.0 * math.pi / jnp.where(g_squared > 0, g_squared, 1.0), 0.0
    )
    orbital = parts_first(orbitals)
    history = [orbital]
    for step_index in range(STEPS):
        orbital = propagate(orbital, step_index, 1.0)
        history.append(orbital)
    occupied = occupation.astype(jnp.float32) / 100.0
    own_weight = lax.dynamic_slice_in_dim(kpoint_weight, k_index, 1)[0].astype(jnp.float32)
    weight = own_weight / jnp.sum(kpoint_weight).astype(jnp.float32)
    band_factor = 2.0 * weight * occupied
    adjoint = parts_first(costate)
    cross_pot = jnp.zeros_like(potential)
    for step_index in range(STEPS - 1, -1, -1):
        forward = history[step_index + 1]
        density = lax.psum(
            jnp.sum(band_factor[:, None, None, None] * jnp.sum(adjoint * forward, axis=0), axis=0),
            "ka",
        )
        hartree = apply("ab,xyb->xya", cas, density)
        hartree = apply("ab,xbz->xaz", cas, hartree)
        hartree = to_columns(hartree, 1, 0)
        hartree = apply("ab,byz->ayz", cas, hartree)
        hartree = apply("ab,byz->ayz", cas, hartree * coulomb)
        hartree = to_columns(hartree, 0, 1)
        hartree = apply("ab,xbz->xaz", cas, hartree)
        hartree = apply("ab,xyb->xya", cas, hartree)
        cross_pot = hartree + xc_kernel * density
        turned = jnp.stack([forward[1], -forward[0]])
        adjoint = propagate(adjoint + step_time * cross_pot * turned, step_index, -1.0)
    result = jnp.moveaxis(adjoint.reshape((2,) + orbitals.shape[:2] + adjoint.shape[2:]), 0, 2)
    return (result, cross_pot)


ROWS = 128
PLANES = 8
QUARTER = 4
AXES = ("ka", "fft")


def halves_of(value):
    high = value.astype(jnp.bfloat16)
    return high, (value - high.astype(jnp.float32)).astype(jnp.bfloat16)


def from_left(table, field):
    size = table.shape[1] // 2
    high, low = halves_of(field)
    return jnp.dot(
        jnp.concatenate([table[:, :size], table], axis=1),
        jnp.concatenate([high, low, high], axis=0),
        preferred_element_type=jnp.float32,
    )


def from_right(field, table):
    size = table.shape[0] // 2
    high, low = halves_of(field)
    return jnp.dot(
        jnp.concatenate([high, low, high], axis=1),
        jnp.concatenate([table[:size], table], axis=0),
        preferred_element_type=jnp.float32,
    )


def side_by_side(matrix, axis):
    return jnp.concatenate(halves_of(matrix), axis=axis)


def circulant(shift, numbers, cosine, sine):
    along = shift + numbers
    phase = 0.5 * sub_time * (along * along)
    q_real, q_imag = jnp.cos(phase), -jnp.sin(phase)
    even = q_real * cosine + q_imag * sine
    odd = q_real * sine - q_imag * cosine
    spectrum = jnp.concatenate(
        [jnp.concatenate([even, odd], axis=1), jnp.concatenate([odd, -even], axis=1)], axis=0
    )
    upper = jnp.dot(
        jnp.concatenate([cosine, sine], axis=1),
        spectrum,
        precision=highest,
        preferred_element_type=jnp.float32,
    ) * (1.0 / ROWS)
    real_part, minus = upper[:, :ROWS], upper[:, ROWS:]
    real_turned, minus_turned = real_part.T, minus.T
    return upper, jnp.concatenate([real_turned, -minus_turned], axis=1)


def whole_matrix(upper):
    real_part, minus = upper[:, :ROWS], upper[:, ROWS:]
    return jnp.concatenate([upper, jnp.concatenate([-minus, real_part], axis=1)], axis=0)


def whole_left(table):
    return jnp.concatenate(
        [whole_matrix(table[:, : 2 * ROWS]), whole_matrix(table[:, 2 * ROWS :])], axis=1
    )


def table_kernel(count_x, shift_ref, numbers_ref, lines_ref, *out_refs):
    numbers, cosine, sine = numbers_ref[...], lines_ref[:, :ROWS], lines_ref[:, ROWS:]
    for line in range(count_x + 1):
        matrix, turned = circulant(shift_ref[line], numbers, cosine, sine)
        out_refs[2 * line][...] = side_by_side(matrix, 1)
        out_refs[2 * line + 1][...] = side_by_side(turned, 1)
    matrix, turned = circulant(shift_ref[count_x + 1], numbers, cosine, sine)
    out_refs[2 * count_x + 2][...] = side_by_side(whole_matrix(turned), 0)
    out_refs[2 * count_x + 3][...] = side_by_side(whole_matrix(matrix), 0)


def cos_sin(angle):
    square = angle * angle
    cosine = sine = 1.0
    for order in range(10, 0, -2):
        cosine = 1.0 - cosine * (square * (1.0 / (order * (order - 1))))
        sine = 1.0 - sine * (square * (1.0 / (order * (order + 1))))
    return cosine, sine * angle


def rotated(sign, real_part, imag_part, cosine, sine):
    if sign > 0:
        return real_part * cosine + imag_part * sine, imag_part * cosine - real_part * sine
    return real_part * cosine - imag_part * sine, imag_part * cosine + real_part * sine


def doubled(cosine, sine):
    return 1.0 - 2.0 * (sine * sine), 2.0 * sine * cosine


def place_of(block, blocks):
    core, rest = divmod(block, blocks // 2)
    return rest // 2 * 4 + core * 2 + rest % 2


def gathered(ref, *index):
    blocks = ref.shape[0]
    return jnp.concatenate(
        [ref[(place_of(block, blocks),) + index] for block in range(blocks)], axis=0
    )


def gather_planes(ref):
    return jnp.concatenate(
        [
            jnp.concatenate([gathered(ref, part, plane) for plane in range(PLANES)], axis=1)
            for part in range(2)
        ],
        axis=0,
    )


def natural(ref):
    return jnp.concatenate([ref[plane] for plane in range(PLANES)], axis=1)


def lane(value, plane):
    return value[:, plane * ROWS : (plane + 1) * ROWS]


def sources_of(blocks):
    half = blocks // 2
    return [
        block // half * blocks + place_of(core * half + block % half, blocks)
        for block in range(blocks)
        for core in range(2)
    ]


def rows_to(out_ref, block, index, plane, piece):
    if not isinstance(out_ref, tuple):
        place = place_of(block, out_ref.shape[0])
        out_ref[(place,) + index + (pl.ds(plane, PLANES, stride=PLANES), slice(None))] = piece
        return
    sources = sources_of(out_ref[0].shape[0] // 2)
    for core in range(2):
        at = (sources[2 * block + core],) + index
        out_ref[0][at + (pl.ds(plane, QUARTER, stride=PLANES), slice(None))] = piece[
            core * QUARTER : (core + 1) * QUARTER
        ]


def turn_z(real_part, imag_part, table):
    rows = jnp.concatenate(
        [
            jnp.concatenate([lane(real_part, plane), lane(imag_part, plane)], axis=1)
            for plane in range(PLANES)
        ],
        axis=0,
    )
    return from_right(rows, table)


def scatter_planes(real_part, imag_part, table, out_ref):
    blocks = ROWS // PLANES
    turned = turn_z(real_part, imag_part, table)
    for plane in range(PLANES):
        for part in range(2):
            piece = turned[plane * ROWS : (plane + 1) * ROWS, part * ROWS : (part + 1) * ROWS]
            for block in range(blocks):
                rows_of = piece[block * PLANES : (block + 1) * PLANES]
                rows_to(out_ref, block, (part,), plane, rows_of)


def between(sign, field, cosine, sine, first_ref, second_ref, right_ref, out_ref):
    field = from_left(whole_left(first_ref[...]), field)
    real_part, imag_part = rotated(sign, field[:ROWS], field[ROWS:], *doubled(cosine, sine))
    field = from_left(
        whole_left(second_ref[...]), jnp.concatenate([real_part, imag_part], axis=0)
    )
    scatter_planes(field[:ROWS], field[ROWS:], right_ref[...], out_ref)


def mid_kernel(
    sign, field_ref, cosine_ref, sine_ref, first_ref, second_ref, right_ref, out_ref
):
    cosine, sine = natural(cosine_ref), natural(sine_ref)
    field = gather_planes(field_ref)
    between(sign, field, cosine, sine, first_ref, second_ref, right_ref, out_ref)


def gather_all(field_ref, part):
    return jnp.concatenate(
        [
            jnp.concatenate(
                [
                    field_ref[source, part, pl.ds(plane * QUARTER, QUARTER), :]
                    for source in sources_of(field_ref.shape[0] // 2)
                ],
                axis=0,
            )
            for plane in range(PLANES)
        ],
        axis=1,
    )


def first_mid_kernel(
    sign, field_ref, first_ref, second_ref, right_ref, out_ref, cosine_ref, sine_ref
):
    pot = gather_all(field_ref, 2)
    for plane in range(PLANES):
        for block in range(ROWS // PLANES):
            rows_of = lane(pot, plane)[block * PLANES : (block + 1) * PLANES]
            rows_to(out_ref, block, (2,), plane, rows_of)
    cosine, sine = cos_sin(0.5 * sub_time * pot)
    store_natural(cosine_ref, cosine)
    store_natural(sine_ref, sine)
    field = jnp.concatenate([gather_all(field_ref, 0), gather_all(field_ref, 1)], axis=0)
    between(sign, field, cosine, sine, first_ref, second_ref, right_ref, out_ref)


def all_mid_kernel(
    sign, field_ref, cosine_ref, sine_ref, first_ref, second_ref, right_ref, out_ref
):
    cosine, sine = natural(cosine_ref), natural(sine_ref)
    field = jnp.concatenate([gather_all(field_ref, 0), gather_all(field_ref, 1)], axis=0)
    between(sign, field, cosine, sine, first_ref, second_ref, right_ref, out_ref)


def second_mid_kernel(
    sign, field_ref, first_ref, second_ref, right_ref, out_ref, cosine_ref, sine_ref
):
    pot = jnp.concatenate([gathered(field_ref, 2, plane) for plane in range(PLANES)], axis=1)
    cosine, sine = cos_sin(0.5 * sub_time * pot)
    store_natural(cosine_ref, cosine)
    store_natural(sine_ref, sine)
    field = gather_planes(field_ref)
    between(sign, field, cosine, sine, first_ref, second_ref, right_ref, out_ref)


def last_mid_kernel(
    sign, field_ref, cosine_ref, sine_ref, first_ref, second_ref, right_ref, out_ref
):
    cosine, sine = natural(cosine_ref), natural(sine_ref)
    field = gather_planes(field_ref)
    between(sign, field, cosine, sine, first_ref, second_ref, right_ref, (out_ref,))


def store_natural(ref, value):
    for plane in range(PLANES):
        ref[plane] = lane(value, plane)


def finish(sign, field_ref, cosine, sine, first_ref, real_ref, imag_ref):
    field = from_left(whole_left(first_ref[...]), gather_planes(field_ref))
    real_part, imag_part = rotated(sign, field[:ROWS], field[ROWS:], cosine, sine)
    store_natural(real_ref, real_part)
    store_natural(imag_ref, imag_part)
    return real_part, imag_part


def begin(sign, real_part, imag_part, cosine, sine, second, right, out_ref):
    real_part, imag_part = rotated(sign, real_part, imag_part, cosine, sine)
    field = from_left(second, jnp.concatenate([real_part, imag_part], axis=0))
    scatter_planes(field[:ROWS], field[ROWS:], right, out_ref)


def step_kernel(
    sign,
    field_ref,
    cosine_ref,
    sine_ref,
    first_ref,
    second_ref,
    right_ref,
    out_ref,
    real_ref,
    imag_ref,
):
    cosine, sine = natural(cosine_ref), natural(sine_ref)
    parts = finish(sign, field_ref, cosine, sine, first_ref, real_ref, imag_ref)
    begin(sign, *parts, cosine, sine, whole_left(second_ref[...]), right_ref[...], out_ref)


def plane_order(core):
    return [core * QUARTER + number for number in range(QUARTER)] + [
        (1 - core) * QUARTER + number for number in range(QUARTER)
    ]


def put_rows(ref, part, plane, piece):
    blocks = ref.shape[0]
    for block in range(blocks):
        ref[place_of(block, blocks), part, pl.ds(plane, PLANES, stride=QUARTER), :] = piece[
            block * PLANES : (block + 1) * PLANES
        ]


def begin_all(sign, real_part, imag_part, cosine, sine, second, right, keep_ref, give_ref):
    real_part, imag_part = rotated(sign, real_part, imag_part, cosine, sine)
    field = from_left(second, jnp.concatenate([real_part, imag_part], axis=0))
    turned = turn_z(field[:ROWS], field[ROWS:], right)
    for number in range(PLANES):
        ref = keep_ref if number < QUARTER else give_ref
        for part in range(2):
            piece = turned[number * ROWS : (number + 1) * ROWS, part * ROWS : (part + 1) * ROWS]
            put_rows(ref, part, number % QUARTER, piece)


def start_kernel(
    unit, field_ref, pot_ref, lines_ref, keep_ref, give_ref, numbers_ref, field, pot, lines, sems
):
    copies = [
        pltpu.make_async_copy(source, target, sems.at[number])
        for number, (source, target) in enumerate(
            ((lines_ref, lines), (pot_ref, pot), (field_ref, field))
        )
    ]
    for copy in copies:
        copy.start()
    order = plane_order(lax.axis_index("ka"))
    index = lax.broadcasted_iota(jnp.int32, (ROWS, ROWS), 0)
    numbers = wave_numbers(index, ROWS)
    numbers_ref[...] = numbers
    copies[0].wait()
    cosine_line, sine_line = lines[:, :ROWS], lines[:, ROWS:]
    table_y = circulant(0.25 * unit, numbers, cosine_line, sine_line)[0]
    table_z = circulant(-0.25 * unit, numbers, cosine_line, sine_line)[1]
    copies[1].wait()
    for number in range(QUARTER):
        put_rows(keep_ref, 2, number, pot[order[number]])
    cosine, sine = cos_sin(
        0.5 * sub_time * jnp.concatenate([pot[plane] for plane in order], axis=1)
    )
    copies[2].wait()
    begin_all(
        1.0,
        jnp.concatenate([field[0, 0, 0, plane] for plane in order], axis=1),
        jnp.concatenate([field[0, 0, 1, plane] for plane in order], axis=1),
        cosine,
        sine,
        side_by_side(whole_matrix(table_y), 1),
        side_by_side(whole_matrix(table_z), 0),
        keep_ref,
        give_ref,
    )


def join_kernel(keep_ref, got_ref, out_ref):
    core = lax.axis_index("ka")
    out_ref[core] = keep_ref[...]
    out_ref[1 - core, :, 0:2] = got_ref[...]
    if keep_ref.shape[1] > 2:
        out_ref[1 - core, :, 2] = keep_ref[:, 2]


def end_kernel(
    sign,
    field_ref,
    cosine_ref,
    sine_ref,
    first_ref,
    other_real_ref,
    other_imag_ref,
    factor_ref,
    real_ref,
    imag_ref,
    density_ref,
):
    cosine, sine = natural(cosine_ref), natural(sine_ref)
    real_part, imag_part = finish(
        sign, field_ref, cosine, sine, first_ref, real_ref, imag_ref
    )
    factor = factor_ref[0, 0]
    for plane in range(PLANES):
        density_ref[plane] = factor * (
            lane(real_part, plane) * other_real_ref[plane]
            + lane(imag_part, plane) * other_imag_ref[plane]
        )


def finish_all(sign, field_ref, got_ref, pot_ref, first_ref):
    core = lax.axis_index("ka")
    order = plane_order(core)
    blocks = got_ref.shape[0]

    def part_of(part):
        planes = []
        for number in range(PLANES):
            at = (part, pl.ds(number % QUARTER * PLANES, PLANES), slice(None))
            rows = [
                field_ref[(core, place_of(block, blocks)) + at]
                if number < QUARTER
                else got_ref[(place_of(block, blocks),) + at]
                for block in range(blocks)
            ]
            planes.append(jnp.concatenate(rows, axis=0))
        return jnp.concatenate(planes, axis=1)

    cosine, sine = cos_sin(
        0.5 * sub_time * jnp.concatenate([pot_ref[plane] for plane in order], axis=1)
    )
    field = from_left(
        whole_left(first_ref[...]), jnp.concatenate([part_of(0), part_of(1)], axis=0)
    )
    return order, rotated(sign, field[:ROWS], field[ROWS:], cosine, sine)


def final_kernel(sign, field_ref, got_ref, pot_ref, first_ref, out_ref):
    order, (real_part, imag_part) = finish_all(sign, field_ref, got_ref, pot_ref, first_ref)
    for number, plane in enumerate(order):
        out_ref[0, 0, 0, plane] = lane(real_part, number)
        out_ref[0, 0, 1, plane] = lane(imag_part, number)


def end_all_kernel(
    sign,
    field_ref,
    got_ref,
    pot_ref,
    first_ref,
    other_ref,
    factor_ref,
    real_ref,
    imag_ref,
    density_ref,
):
    order, (real_part, imag_part) = finish_all(sign, field_ref, got_ref, pot_ref, first_ref)
    factor = factor_ref[0, 0]
    for number, plane in enumerate(order):
        real_ref[plane] = lane(real_part, number)
        imag_ref[plane] = lane(imag_part, number)
        density_ref[plane] = factor * (
            lane(real_part, number) * other_ref[0, 0, 0, plane]
            + lane(imag_part, number) * other_ref[0, 0, 1, plane]
        )


def density_all_kernel(
    own_ref, other_ref, left_ref, right_ref, density_ref, out_ref, whole_ref
):
    density = natural(own_ref) + natural(other_ref)
    store_natural(density_ref, density)
    spectrum = from_right(stack_planes(from_left(left_ref[...], density)), right_ref[...])
    for plane in range(PLANES):
        for block in range(ROWS // PLANES):
            start = plane * ROWS + block * PLANES
            whole_ref[block, pl.ds(plane, PLANES, stride=PLANES), :] = spectrum[
                start : start + PLANES
            ]
    size = QUARTER * PLANES
    start = pl.multiple_of(lax.axis_index("ka") * size, size)
    out_ref[...] = whole_ref[:, pl.ds(start, size), :]


def hartree_all_kernel(
    sign,
    field_ref,
    got_ref,
    density_ref,
    xc_ref,
    orbital_real_ref,
    orbital_imag_ref,
    adjoint_ref,
    pot_ref,
    cas_left_ref,
    cas_right_ref,
    second_ref,
    right_ref,
    keep_ref,
    give_ref,
    rows_ref,
):
    core = lax.axis_index("ka")
    rows_ref[core] = field_ref[...]
    rows_ref[1 - core] = got_ref[...]
    spectrum = jnp.concatenate(
        [
            jnp.concatenate(
                [
                    rows_ref[number, block, pl.ds(plane, QUARTER, stride=PLANES), :]
                    for block in range(field_ref.shape[0])
                    for number in range(2)
                ],
                axis=0,
            )
            for plane in range(PLANES)
        ],
        axis=1,
    )
    hartree = from_right(
        stack_planes(from_left(cas_left_ref[...], spectrum)), cas_right_ref[...]
    )
    for plane in range(PLANES):
        rows_ref[plane // QUARTER, pl.ds(plane % QUARTER * QUARTER, QUARTER)] = (
            hartree[plane * ROWS : (plane + 1) * ROWS]
        ).reshape(QUARTER, QUARTER * PLANES, ROWS)
    order = plane_order(core)
    real_parts, imag_parts = [], []
    for number, plane in enumerate(order):
        at = core if number < QUARTER else 1 - core
        own = rows_ref[at, pl.ds(number % QUARTER * QUARTER, QUARTER)].reshape(ROWS, ROWS)
        cross = own + xc_ref[plane] * density_ref[plane]
        real_parts.append(
            adjoint_ref[0, 0, 0, plane] + step_time * cross * orbital_imag_ref[plane]
        )
        imag_parts.append(
            adjoint_ref[0, 0, 1, plane] - step_time * cross * orbital_real_ref[plane]
        )
    cosine, sine = cos_sin(
        0.5 * sub_time * jnp.concatenate([pot_ref[plane] for plane in order], axis=1)
    )
    begin_all(
        sign,
        jnp.concatenate(real_parts, axis=1),
        jnp.concatenate(imag_parts, axis=1),
        cosine,
        sine,
        whole_left(second_ref[...]),
        right_ref[...],
        keep_ref,
        give_ref,
    )


def stack_planes(value):
    return jnp.concatenate([lane(value, plane) for plane in range(PLANES)], axis=0)


def density_kernel(own_ref, other_ref, left_ref, right_ref, density_ref, out_ref):
    density = natural(own_ref) + natural(other_ref)
    store_natural(density_ref, density)
    spectrum = from_right(stack_planes(from_left(left_ref[...], density)), right_ref[...])
    for plane in range(PLANES):
        for block in range(ROWS // PLANES):
            start = plane * ROWS + block * PLANES
            rows_to(out_ref, block, (), plane, spectrum[start : start + PLANES])


def coulomb_kernel(unit, placed, field_ref, square_ref, left_ref, out_ref):
    blocks, lines = field_ref.shape[:2]
    places = [place_of(block, blocks) if placed else block for block in range(blocks)]
    rows = jnp.concatenate(
        [
            jnp.concatenate([field_ref[place, line] for place in places], axis=0)
            for line in range(lines)
        ],
        axis=1,
    )
    rows = from_left(left_ref[...], rows)
    index = lax.broadcasted_iota(jnp.int32, (ROWS, ROWS), 0)
    number = unit * jnp.where(index < ROWS // 2, index, index - ROWS).astype(jnp.float32)
    along = number * number
    parts = []
    for line in range(lines):
        square = along + square_ref[pl.ds(line, 1), :]
        nonzero = square > 0
        inverse = jnp.where(nonzero, 4.0 * math.pi / jnp.where(nonzero, square, 1.0), 0.0)
        parts.append(lane(rows, line) * inverse)
    rows = from_left(left_ref[...], jnp.concatenate(parts, axis=1))
    for line in range(lines):
        for block, place in enumerate(places):
            out_ref[place, line] = lane(rows, line)[block * PLANES : (block + 1) * PLANES]


def hartree_kernel(
    sign,
    field_ref,
    density_ref,
    xc_ref,
    orbital_real_ref,
    orbital_imag_ref,
    adjoint_real_ref,
    adjoint_imag_ref,
    cosine_ref,
    sine_ref,
    cas_left_ref,
    cas_right_ref,
    second_ref,
    right_ref,
    out_ref,
    cross_ref,
):
    spectrum = jnp.concatenate(
        [gathered(field_ref, pl.ds(plane, PLANES, stride=PLANES)) for plane in range(PLANES)],
        axis=1,
    )
    hartree = from_right(
        stack_planes(from_left(cas_left_ref[...], spectrum)), cas_right_ref[...]
    )
    real_parts, imag_parts = [], []
    for plane in range(PLANES):
        cross = hartree[plane * ROWS : (plane + 1) * ROWS] + xc_ref[plane] * density_ref[plane]
        cross_ref[plane] = cross
        real_parts.append(adjoint_real_ref[plane] + step_time * cross * orbital_imag_ref[plane])
        imag_parts.append(adjoint_imag_ref[plane] - step_time * cross * orbital_real_ref[plane])
    begin(
        sign,
        jnp.concatenate(real_parts, axis=1),
        jnp.concatenate(imag_parts, axis=1),
        natural(cosine_ref),
        natural(sine_ref),
        whole_left(second_ref[...]),
        right_ref[...],
        out_ref,
    )


def run(kernel, outputs, *operands, space=pltpu.VMEM, scratch=()):
    made = pl.pallas_call(
        kernel,
        out_shape=[
            jax.ShapeDtypeStruct(out, jnp.float32) if isinstance(out, tuple) else out
            for out in outputs
        ],
        in_specs=[
            pl.BlockSpec(memory_space=pltpu.SMEM if operand.size < ROWS else space)
            for operand in operands
        ],
        out_specs=[pl.BlockSpec(memory_space=pltpu.VMEM) for _ in outputs],
        scratch_shapes=list(scratch),
        compiler_params=pltpu.CompilerParams(vmem_limit_bytes=24 * 2**20),
    )(*operands)
    return made[0] if len(outputs) == 1 else made


def grouped(
    orbitals, costate, potential, xc_kernel, vector_potential, kpoint_weight, occupation
):
    grid_size = potential.shape[1]
    blocks = lax.axis_size("fft")
    half = blocks // 2
    core = lax.axis_index("ka")
    fft_index = lax.axis_index("fft")
    side = fft_index // half
    place = core * half + fft_index % half
    lattice_unit = 2.0 * math.pi / (grid_size * spacing)

    groups = []
    for h in range(2):
        devices = [c * blocks + h * half + j for c in range(2) for j in range(half)]
        group = [0] * blocks
        for block, device in enumerate(devices):
            group[place_of(block, blocks)] = device
        groups.append(group)
    regroup = []
    for c in range(2):
        for f in range(blocks):
            h, j = f // half, f % half
            regroup.append((c * blocks + f, h * blocks + c * half + j))
    across = [
        (c * blocks + f, c * blocks + (f + half) % blocks) for c in range(2) for f in range(blocks)
    ]

    def exchange(array):
        return lax.all_to_all(array, AXES, 0, 0, axis_index_groups=groups, tiled=True)

    def exchange_whole(array):
        return lax.all_to_all(array, "fft", 0, 0, tiled=True)

    def exchange_all(array):
        return lax.all_to_all(
            array, AXES, 0, 0, axis_index_groups=[groups[0] + groups[1]], tiled=True
        )

    def other_core(array):
        return lax.ppermute(array, "ka", [(0, 1), (1, 0)])

    def to_halves(keep, give):
        sent = run(join_kernel, [(2,) + keep.shape], keep, other_core(give))
        return exchange_all(sent.reshape((2 * blocks,) + keep.shape[1:]))

    def from_halves(sent):
        field = exchange_all(sent).reshape(2, blocks, 2, PLANES * QUARTER, ROWS)
        give = lax.dynamic_index_in_dim(field, 1 - core, 0, keepdims=False)
        return field, other_core(give)

    def move(array, pairs):
        return lax.ppermute(array, AXES, pairs)

    block_shape = (blocks, 2, PLANES, PLANES, ROWS)
    sent_shape = (blocks, 2, PLANES * PLANES, ROWS)
    natural_shape = (2, PLANES, ROWS, ROWS)
    real_shape = (PLANES, ROWS, ROWS)

    def swap_field(array):
        return exchange(array.reshape(block_shape))

    grid_line = np.arange(grid_size)
    angles = 2.0 * np.pi / grid_size * (np.outer(grid_line, grid_line) % grid_size)
    line_pair = jnp.asarray(
        np.concatenate([np.cos(angles), np.sin(angles)], axis=1).astype(np.float32)
    )
    cas = (np.cos(angles) + np.sin(angles)) / math.sqrt(grid_size)
    cas_high = cas.astype(jnp.bfloat16)
    cas_low = (cas - cas_high.astype(np.float64)).astype(jnp.bfloat16)
    cas_left = jnp.asarray(np.concatenate([cas_high, cas_low], axis=1))
    cas_right = jnp.asarray(np.concatenate([cas_high, cas_low], axis=0))

    shift_x = lattice_unit * ((side.astype(jnp.float32) + 0.5) / 2 - 0.5) + vector_potential
    shift_yz = jnp.array([lattice_unit * 0.25, -lattice_unit * 0.25], jnp.float32)
    count_x = STEPS * SUB

    numbers = wave_numbers(lax.iota(jnp.int32, grid_size), grid_size)
    def squares_of(first, count):
        own = wave_numbers(first + lax.iota(jnp.int32, count), grid_size)
        return (own * own)[:, None] + (numbers * numbers)[None, :]

    squares = squares_of(place * PLANES, PLANES)
    squares_all = squares_of(fft_index * PLANES + core * QUARTER, QUARTER)

    def factor_of(k_index):
        own_weight = lax.dynamic_slice_in_dim(kpoint_weight, k_index, 1)[0].astype(jnp.float32)
        weight = own_weight / jnp.sum(kpoint_weight).astype(jnp.float32)
        return (2.0 * weight * occupation.astype(jnp.float32) / 100.0).reshape(1, 1)

    factor, factor_all = factor_of(side), factor_of(core)

    keep, give, numbers_full = run(
        functools.partial(start_kernel, lattice_unit),
        [
            (blocks, 3, PLANES * QUARTER, ROWS),
            (blocks, 2, PLANES * QUARTER, ROWS),
            (ROWS, ROWS),
        ],
        orbitals,
        potential,
        line_pair,
        space=pltpu.HBM,
        scratch=[
            pltpu.VMEM(orbitals.shape, jnp.float32),
            pltpu.VMEM(real_shape, jnp.float32),
            pltpu.VMEM((ROWS, 2 * ROWS), jnp.float32),
            pltpu.SemaphoreType.DMA((3,)),
        ],
    )
    field = to_halves(keep, give)
    left_shape = jax.ShapeDtypeStruct((ROWS, 4 * ROWS), jnp.bfloat16)
    right_shape = jax.ShapeDtypeStruct((4 * ROWS, 2 * ROWS), jnp.bfloat16)
    made = run(
        functools.partial(table_kernel, count_x),
        [left_shape] * (2 * count_x + 2) + [right_shape] * 2,
        jnp.concatenate([shift_x, shift_yz]),
        numbers_full,
        line_pair,
    )
    early = (squares, squares_all, factor, factor_all)
    made, early = lax.optimization_barrier((made, early))
    squares, squares_all, factor, factor_all = early
    tables = {1.0: made[0 : 2 * count_x + 2 : 2], -1.0: made[1 : 2 * count_x + 2 : 2]}
    right_z = {1.0: made[-2], -1.0: made[-1]}

    def table_x(sign, count):
        return tables[sign][count if sign > 0 else count_x - 1 - count]

    def table_y(sign):
        return tables[sign][count_x]

    def tables_of(sign, count):
        if count % 2 == 0:
            return table_y(sign), table_y(sign), right_z[sign]
        return table_x(sign, count - 1), table_x(sign, count), right_z[sign]

    def middle(sign, field, count):
        waves = waves_rows if count % 2 == 0 else waves_cols
        return run(
            functools.partial(mid_kernel, sign),
            [sent_shape],
            field,
            *waves,
            *tables_of(sign, count),
        )

    sent, *waves_cols = run(
        functools.partial(first_mid_kernel, 1.0),
        [(blocks, 3) + sent_shape[2:], real_shape, real_shape],
        field,
        *tables_of(1.0, 1),
    )
    sent, *waves_rows = run(
        functools.partial(second_mid_kernel, 1.0),
        [sent_shape, real_shape, real_shape],
        exchange(sent.reshape(blocks, 3, PLANES, PLANES, ROWS)),
        *tables_of(1.0, 2),
    )
    sent = middle(1.0, swap_field(sent), 3)
    kept = []
    all_shape = (2 * blocks, 2, PLANES * QUARTER, ROWS)
    keep_shape = (blocks, 2, PLANES * QUARTER, ROWS)
    for count in range(4, count_x - 1):
        field = swap_field(sent)
        if count % SUB == 0:
            sent, *orbital = run(
                functools.partial(step_kernel, 1.0),
                [sent_shape, real_shape, real_shape],
                field,
                *waves_rows,
                *tables_of(1.0, count),
            )
            kept.append(orbital)
        else:
            sent = middle(1.0, field, count)
    sent = run(
        functools.partial(last_mid_kernel, 1.0),
        [all_shape],
        swap_field(sent),
        *waves_cols,
        *tables_of(1.0, count_x - 1),
    )
    *orbital, partial = run(
        functools.partial(end_all_kernel, 1.0),
        [real_shape] * 3,
        *from_halves(sent),
        potential,
        table_y(1.0),
        costate,
        factor_all,
    )

    density, sent = run(
        density_all_kernel,
        [real_shape, (blocks, QUARTER * PLANES, ROWS)],
        partial,
        other_core(partial),
        cas_left,
        cas_right,
        scratch=[pltpu.VMEM((blocks, PLANES * PLANES, ROWS), jnp.float32)],
    )
    field = exchange_whole(sent.reshape(blocks, QUARTER, PLANES, ROWS))
    sent = run(
        functools.partial(coulomb_kernel, lattice_unit, False),
        [(blocks, QUARTER, PLANES, ROWS)],
        field,
        squares_all,
        cas_left,
    )
    field = exchange_whole(sent)
    field = field.reshape(blocks, QUARTER * PLANES, ROWS)
    keep, give = run(
        functools.partial(hartree_all_kernel, -1.0),
        [keep_shape, keep_shape],
        field,
        other_core(field),
        density,
        xc_kernel,
        *orbital,
        costate,
        potential,
        cas_left,
        cas_right,
        table_y(-1.0),
        right_z[-1.0],
        scratch=[pltpu.VMEM((2, blocks, QUARTER * PLANES, ROWS), jnp.float32)],
    )
    sent = run(
        functools.partial(all_mid_kernel, -1.0),
        [sent_shape],
        to_halves(keep, give),
        *waves_cols,
        *tables_of(-1.0, 1),
    )
    for step_index in range(STEPS - 1, -1, -1):
        first = (STEPS - 1 - step_index) * SUB
        if step_index < STEPS - 1:
            density, sent = run(
                density_kernel,
                [real_shape, (blocks, PLANES * PLANES, ROWS)],
                partial,
                move(partial, across),
                cas_left,
                cas_right,
            )
            field = exchange(sent.reshape(blocks, PLANES, PLANES, ROWS))
            sent = run(
                functools.partial(coulomb_kernel, lattice_unit, True),
                [(blocks, PLANES, PLANES, ROWS)],
                field,
                squares,
                cas_left,
            )
            field = exchange(sent).reshape(blocks, PLANES * PLANES, ROWS)
            sent, cross = run(
                functools.partial(hartree_kernel, -1.0),
                [sent_shape, real_shape],
                field,
                density,
                xc_rows,
                *kept[step_index],
                *adjoint,
                *waves_rows,
                cas_left,
                cas_right,
                table_y(-1.0),
                right_z[-1.0],
            )
            sent = middle(-1.0, swap_field(sent), first + 1)
            field = swap_field(sent)
        else:
            sent, xc_rows = lax.optimization_barrier((sent, xc_kernel))
            field = swap_field(sent)
            field, xc_rows = lax.optimization_barrier((field, move(xc_rows, regroup)))
        sent = middle(-1.0, field, first + 2)
        field = swap_field(sent)
        if step_index > 0:
            sent = middle(-1.0, field, first + SUB - 1)
            *adjoint, partial = run(
                functools.partial(end_kernel, -1.0),
                [real_shape] * 3,
                swap_field(sent),
                *waves_rows,
                table_y(-1.0),
                *kept[step_index - 1],
                factor,
            )
    sent = run(
        functools.partial(last_mid_kernel, -1.0),
        [all_shape],
        field,
        *waves_cols,
        *tables_of(-1.0, count_x - 1),
    )
    result = run(
        functools.partial(final_kernel, -1.0),
        [orbitals.shape],
        *from_halves(sent),
        potential,
        table_y(-1.0),
    )
    return (result, jnp.where(core == side, cross, other_core(cross)))


def solution(mesh):
    placed = (
        P("ka", None, None, "fft", None, None),
        P("ka", None, None, "fft", None, None),
        P("fft", None, None),
        P("fft", None, None),
        P(),
        P(),
        P(),
    )

    def local(*arguments):
        orbitals, potential = arguments[0], arguments[2]
        fits = (
            mesh.shape["ka"] == 2
            and mesh.shape["fft"] % 2 == 0
            and orbitals.shape[:2] == (1, 1)
            and potential.shape == (PLANES, ROWS, ROWS)
        )
        return grouped(*arguments) if fits else plain(*arguments)

    return jax.shard_map(
        local,
        mesh=mesh,
        in_specs=placed,
        out_specs=(P("ka", None, None, "fft", None, None), P("fft", None, None)),
        check_vma=False,
    )
```

```python
import functools
import math

import jax
import jax.numpy as jnp
import numpy as np
from jax import lax
from jax.experimental import pallas as pl
from jax.experimental.pallas import tpu as pltpu
from jax.sharding import PartitionSpec as P

STEPS = 2
SUB = 4


spacing = 0.25
step_time = 0.6
sub_time = step_time / SUB
highest = lax.Precision.HIGHEST


def wave_numbers(grid_line, grid_size):
    signed_line = jnp.where(grid_line < grid_size // 2, grid_line, grid_line - grid_size)
    return 2.0 * math.pi / (grid_size * spacing) * signed_line.astype(jnp.float32)


def table_angles(grid_size):
    row_index = lax.broadcasted_iota(jnp.int32, (grid_size, grid_size), 0)
    col_index = lax.broadcasted_iota(jnp.int32, (grid_size, grid_size), 1)
    return 2.0 * math.pi / grid_size * (row_index * col_index % grid_size).astype(jnp.float32)


def line_matrices(shifts, grid_size):
    numbers = wave_numbers(lax.iota(jnp.int32, grid_size), grid_size)
    along = shifts[:, None] + numbers[None, :]
    phase = 0.5 * sub_time * (along * along)
    angles = table_angles(grid_size)
    cosine, sine = jnp.cos(angles), jnp.sin(angles)
    q_real, q_imag = jnp.cos(phase)[:, None, :], -jnp.sin(phase)[:, None, :]
    left_real = (cosine * q_real - sine * q_imag) / grid_size
    left_imag = (cosine * q_imag + sine * q_real) / grid_size
    both = jnp.stack([left_real, left_imag])
    by_cos = jnp.einsum("csam,mb->csab", both, cosine, precision=highest)
    by_sin = jnp.einsum("csam,mb->csab", both, sine, precision=highest)
    return by_cos[0] + by_sin[1], by_cos[1] - by_sin[0]


def real_form(real_part, imag_part):
    upper = jnp.stack([real_part, -imag_part], axis=-2)
    lower = jnp.stack([imag_part, real_part], axis=-2)
    return jnp.stack([upper, lower], axis=-4)


def spin(field, angle):
    cosine, sine = jnp.cos(angle), jnp.sin(angle)
    return jnp.stack(
        [field[0] * cosine + field[1] * sine, field[1] * cosine - field[0] * sine]
    )


def apply(form, matrix, field):
    return jnp.einsum(
        form, matrix, field, precision=lax.Precision.HIGHEST, preferred_element_type=jnp.float32
    )


def plain(orbitals, costate, potential, xc_kernel, vector_potential, kpoint_weight, occupation):
    grid_size = potential.shape[1]
    k_index = lax.axis_index("ka")
    fft_index = lax.axis_index("fft")
    planes = potential.shape[0]
    lattice_unit = 2.0 * math.pi / (grid_size * spacing)
    k_fraction = (k_index.astype(jnp.float32) + 0.5) / lax.axis_size("ka") - 0.5
    shifts = jnp.concatenate(
        [
            lattice_unit * k_fraction + vector_potential,
            jnp.array([lattice_unit * 0.25, -lattice_unit * 0.25], jnp.float32),
        ]
    )
    lines = real_form(*line_matrices(shifts, grid_size))
    back = jnp.transpose(lines, (0, 3, 4, 1, 2))

    def to_columns(field, split, concat):
        return lax.all_to_all(field, "fft", split_axis=split, concat_axis=concat, tiled=True)

    pot_rows = 0.5 * sub_time * potential
    pot_cols = to_columns(pot_rows, 1, 0)

    def propagate(field, step_index, sign):
        table = lines if sign > 0 else back
        order = range(SUB) if sign > 0 else range(SUB - 1, -1, -1)
        mat_y, mat_z = table[STEPS * SUB], table[STEPS * SUB + 1]
        in_rows = True
        field = spin(field, sign * pot_rows)
        for count, sub_index in enumerate(order):
            mat_x = table[step_index * SUB + sub_index]
            last = count == SUB - 1
            turn = sign * (1.0 if last else 2.0)
            field = apply("cadb,dkxyb->ckxya", mat_z, field)
            if in_rows:
                field = apply("cadb,dkxbz->ckxaz", mat_y, field)
                field = to_columns(field, 3, 2)
                field = apply("cadb,dkbyz->ckayz", mat_x, field)
                field = spin(field, turn * pot_cols)
            else:
                field = apply("cadb,dkbyz->ckayz", mat_x, field)
                field = to_columns(field, 2, 3)
                field = apply("cadb,dkxbz->ckxaz", mat_y, field)
                field = spin(field, turn * pot_rows)
            in_rows = not in_rows
        return field

    def parts_first(field):
        bands = field.shape[0] * field.shape[1]
        return jnp.moveaxis(field, 2, 0).reshape((2, bands) + field.shape[3:])

    angles = table_angles(grid_size)
    cas = (jnp.cos(angles) + jnp.sin(angles)) / math.sqrt(grid_size)
    numbers = wave_numbers(lax.iota(jnp.int32, grid_size), grid_size)
    numbers_local = wave_numbers(fft_index * planes + lax.iota(jnp.int32, planes), grid_size)
    g_squared = (
        (numbers * numbers)[:, None, None]
        + (numbers_local * numbers_local)[None, :, None]
        + (numbers * numbers)[None, None, :]
    )
    coulomb = jnp.where(
        g_squared > 0, 4.0 * math.pi / jnp.where(g_squared > 0, g_squared, 1.0), 0.0
    )
    orbital = parts_first(orbitals)
    history = [orbital]
    for step_index in range(STEPS):
        orbital = propagate(orbital, step_index, 1.0)
        history.append(orbital)
    occupied = occupation.astype(jnp.float32) / 100.0
    own_weight = lax.dynamic_slice_in_dim(kpoint_weight, k_index, 1)[0].astype(jnp.float32)
    weight = own_weight / jnp.sum(kpoint_weight).astype(jnp.float32)
    band_factor = 2.0 * weight * occupied
    adjoint = parts_first(costate)
    cross_pot = jnp.zeros_like(potential)
    for step_index in range(STEPS - 1, -1, -1):
        forward = history[step_index + 1]
        density = lax.psum(
            jnp.sum(band_factor[:, None, None, None] * jnp.sum(adjoint * forward, axis=0), axis=0),
            "ka",
        )
        hartree = apply("ab,xyb->xya", cas, density)
        hartree = apply("ab,xbz->xaz", cas, hartree)
        hartree = to_columns(hartree, 1, 0)
        hartree = apply("ab,byz->ayz", cas, hartree)
        hartree = apply("ab,byz->ayz", cas, hartree * coulomb)
        hartree = to_columns(hartree, 0, 1)
        hartree = apply("ab,xbz->xaz", cas, hartree)
        hartree = apply("ab,xyb->xya", cas, hartree)
        cross_pot = hartree + xc_kernel * density
        turned = jnp.stack([forward[1], -forward[0]])
        adjoint = propagate(adjoint + step_time * cross_pot * turned, step_index, -1.0)
    result = jnp.moveaxis(adjoint.reshape((2,) + orbitals.shape[:2] + adjoint.shape[2:]), 0, 2)
    return (result, cross_pot)


ROWS = 128
PLANES = 8
QUARTER = 4
AXES = ("ka", "fft")


def halves_of(value):
    high = value.astype(jnp.bfloat16)
    return high, (value - high.astype(jnp.float32)).astype(jnp.bfloat16)


def from_left(table, field):
    size = table.shape[1] // 2
    high, low = halves_of(field)
    return jnp.dot(
        jnp.concatenate([table[:, :size], table], axis=1),
        jnp.concatenate([high, low, high], axis=0),
        preferred_element_type=jnp.float32,
    )


def from_right(field, table):
    size = table.shape[0] // 2
    high, low = halves_of(field)
    return jnp.dot(
        jnp.concatenate([high, low, high], axis=1),
        jnp.concatenate([table[:size], table], axis=0),
        preferred_element_type=jnp.float32,
    )


def side_by_side(matrix, axis):
    return jnp.concatenate(halves_of(matrix), axis=axis)


def circulant(shift, numbers, cosine, sine):
    along = shift + numbers
    phase = 0.5 * sub_time * (along * along)
    q_real, q_imag = jnp.cos(phase), -jnp.sin(phase)
    even = q_real * cosine + q_imag * sine
    odd = q_real * sine - q_imag * cosine
    spectrum = jnp.concatenate(
        [jnp.concatenate([even, odd], axis=1), jnp.concatenate([odd, -even], axis=1)], axis=0
    )
    upper = jnp.dot(
        jnp.concatenate([cosine, sine], axis=1),
        spectrum,
        precision=highest,
        preferred_element_type=jnp.float32,
    ) * (1.0 / ROWS)
    real_part, minus = upper[:, :ROWS], upper[:, ROWS:]
    real_turned, minus_turned = real_part.T, minus.T
    return upper, jnp.concatenate([real_turned, -minus_turned], axis=1)


def whole_matrix(upper):
    real_part, minus = upper[:, :ROWS], upper[:, ROWS:]
    return jnp.concatenate([upper, jnp.concatenate([-minus, real_part], axis=1)], axis=0)


def whole_left(table):
    return jnp.concatenate(
        [whole_matrix(table[:, : 2 * ROWS]), whole_matrix(table[:, 2 * ROWS :])], axis=1
    )


def table_kernel(shift_ref, lines_ref, *out_refs):
    numbers = wave_numbers(lax.broadcasted_iota(jnp.int32, (ROWS, ROWS), 0), ROWS)
    cosine, sine = lines_ref[:, :ROWS], lines_ref[:, ROWS:]
    for line in range(len(out_refs) // 2):
        matrix, turned = circulant(shift_ref[line], numbers, cosine, sine)
        out_refs[2 * line][...] = side_by_side(matrix, 1)
        out_refs[2 * line + 1][...] = side_by_side(turned, 1)


def constant_circulant(shift, grid_size):
    grid_line = np.arange(grid_size)
    signed_line = np.where(grid_line < grid_size // 2, grid_line, grid_line - grid_size)
    along = shift + 2.0 * math.pi / (grid_size * spacing) * signed_line
    waves = np.exp(2j * np.pi / grid_size * (np.outer(grid_line, grid_line) % grid_size))
    line = (waves * np.exp(-0.5j * sub_time * along * along)) @ waves.conj() / grid_size
    whole = np.block([[line.real, -line.imag], [line.imag, line.real]])
    return whole, whole.T


def constant_table(matrix, axis):
    high = matrix.astype(jnp.bfloat16)
    low = (matrix - high.astype(np.float64)).astype(jnp.bfloat16)
    return jnp.asarray(np.concatenate([high, low], axis=axis))


def cos_sin(angle):
    square = angle * angle
    cosine = sine = 1.0
    for order in range(10, 0, -2):
        cosine = 1.0 - cosine * (square * (1.0 / (order * (order - 1))))
        sine = 1.0 - sine * (square * (1.0 / (order * (order + 1))))
    return cosine, sine * angle


def rotated(sign, real_part, imag_part, cosine, sine):
    if sign > 0:
        return real_part * cosine + imag_part * sine, imag_part * cosine - real_part * sine
    return real_part * cosine - imag_part * sine, imag_part * cosine + real_part * sine


def doubled(cosine, sine):
    return 1.0 - 2.0 * (sine * sine), 2.0 * sine * cosine


def place_of(block, blocks):
    core, rest = divmod(block, blocks // 2)
    return rest // 2 * 4 + core * 2 + rest % 2


def gathered(ref, *index):
    blocks = ref.shape[0]
    return jnp.concatenate(
        [ref[(place_of(block, blocks),) + index] for block in range(blocks)], axis=0
    )


def gather_planes(ref):
    return jnp.concatenate(
        [
            jnp.concatenate([gathered(ref, part, plane) for plane in range(PLANES)], axis=1)
            for part in range(2)
        ],
        axis=0,
    )


def natural(ref):
    return jnp.concatenate([ref[plane] for plane in range(PLANES)], axis=1)


def lane(value, plane):
    return value[:, plane * ROWS : (plane + 1) * ROWS]


def core_place(block, blocks):
    core, chip = divmod(block, blocks // 2)
    bits = (blocks // 2).bit_length() - 1
    return core, sum((chip >> bit & 1) << (bits - 1 - bit) for bit in range(bits))


def sources_of(blocks):
    half = blocks // 2
    return [
        (core * 2 + block // half) * half + core_place(block % half, blocks)[1]
        for block in range(blocks)
        for core in range(2)
    ]


def rows_to(out_ref, block, index, plane, piece):
    if not isinstance(out_ref, tuple):
        place = place_of(block, out_ref.shape[0])
        out_ref[(place,) + index + (pl.ds(plane, PLANES, stride=PLANES), slice(None))] = piece
        return
    sources = sources_of(out_ref[0].shape[0] // 2)
    for core in range(2):
        at = (sources[2 * block + core],) + index
        out_ref[0][at + (pl.ds(plane, QUARTER, stride=PLANES), slice(None))] = piece[
            core * QUARTER : (core + 1) * QUARTER
        ]


def turn_z(real_part, imag_part, table):
    rows = jnp.concatenate(
        [
            jnp.concatenate([lane(real_part, plane), lane(imag_part, plane)], axis=1)
            for plane in range(real_part.shape[1] // ROWS)
        ],
        axis=0,
    )
    return from_right(rows, table)


def scatter_planes(real_part, imag_part, table, out_ref):
    blocks = ROWS // PLANES
    turned = turn_z(real_part, imag_part, table)
    for plane in range(PLANES):
        for part in range(2):
            piece = turned[plane * ROWS : (plane + 1) * ROWS, part * ROWS : (part + 1) * ROWS]
            for block in range(blocks):
                rows_of = piece[block * PLANES : (block + 1) * PLANES]
                rows_to(out_ref, block, (part,), plane, rows_of)


def between(sign, field, cosine, sine, first_ref, second_ref, right_ref, out_ref):
    field = from_left(whole_left(first_ref[...]), field)
    real_part, imag_part = rotated(sign, field[:ROWS], field[ROWS:], *doubled(cosine, sine))
    field = from_left(
        whole_left(second_ref[...]), jnp.concatenate([real_part, imag_part], axis=0)
    )
    scatter_planes(field[:ROWS], field[ROWS:], right_ref[...], out_ref)


def mid_kernel(
    sign, field_ref, cosine_ref, sine_ref, first_ref, second_ref, right_ref, out_ref
):
    cosine, sine = natural(cosine_ref), natural(sine_ref)
    field = gather_planes(field_ref)
    between(sign, field, cosine, sine, first_ref, second_ref, right_ref, out_ref)


def gather_all(field_ref, part):
    return jnp.concatenate(
        [
            jnp.concatenate(
                [
                    field_ref[source, part, pl.ds(plane * QUARTER, QUARTER), :]
                    for source in sources_of(field_ref.shape[0] // 2)
                ],
                axis=0,
            )
            for plane in range(PLANES)
        ],
        axis=1,
    )


def first_mid_kernel(
    sign, field_ref, first_ref, second_ref, right_ref, out_ref, cosine_ref, sine_ref
):
    pot = gather_all(field_ref, 2)
    for plane in range(PLANES):
        for block in range(ROWS // PLANES):
            rows_of = lane(pot, plane)[block * PLANES : (block + 1) * PLANES]
            rows_to(out_ref, block, (2,), plane, rows_of)
    cosine, sine = cos_sin(0.5 * sub_time * pot)
    store_natural(cosine_ref, cosine)
    store_natural(sine_ref, sine)
    field = jnp.concatenate([gather_all(field_ref, 0), gather_all(field_ref, 1)], axis=0)
    between(sign, field, cosine, sine, first_ref, second_ref, right_ref, out_ref)


def all_mid_kernel(
    sign, field_ref, cosine_ref, sine_ref, first_ref, second_ref, right_ref, out_ref
):
    cosine, sine = natural(cosine_ref), natural(sine_ref)
    field = jnp.concatenate([gather_all(field_ref, 0), gather_all(field_ref, 1)], axis=0)
    between(sign, field, cosine, sine, first_ref, second_ref, right_ref, out_ref)


def second_mid_kernel(
    sign, field_ref, first_ref, second_ref, right_ref, out_ref, cosine_ref, sine_ref
):
    pot = jnp.concatenate([gathered(field_ref, 2, plane) for plane in range(PLANES)], axis=1)
    cosine, sine = cos_sin(0.5 * sub_time * pot)
    store_natural(cosine_ref, cosine)
    store_natural(sine_ref, sine)
    field = gather_planes(field_ref)
    between(sign, field, cosine, sine, first_ref, second_ref, right_ref, out_ref)


def last_mid_kernel(
    sign, field_ref, cosine_ref, sine_ref, first_ref, second_ref, right_ref, out_ref
):
    cosine, sine = natural(cosine_ref), natural(sine_ref)
    field = gather_planes(field_ref)
    between(sign, field, cosine, sine, first_ref, second_ref, right_ref, (out_ref,))


def store_natural(ref, value):
    for plane in range(PLANES):
        ref[plane] = lane(value, plane)


def finish(sign, field_ref, cosine, sine, first_ref, real_ref, imag_ref):
    field = from_left(whole_left(first_ref[...]), gather_planes(field_ref))
    real_part, imag_part = rotated(sign, field[:ROWS], field[ROWS:], cosine, sine)
    store_natural(real_ref, real_part)
    store_natural(imag_ref, imag_part)
    return real_part, imag_part


def begin(sign, real_part, imag_part, cosine, sine, second, right, out_ref):
    real_part, imag_part = rotated(sign, real_part, imag_part, cosine, sine)
    field = from_left(second, jnp.concatenate([real_part, imag_part], axis=0))
    scatter_planes(field[:ROWS], field[ROWS:], right, out_ref)


def step_kernel(
    sign,
    field_ref,
    cosine_ref,
    sine_ref,
    first_ref,
    second_ref,
    right_ref,
    out_ref,
    real_ref,
    imag_ref,
):
    cosine, sine = natural(cosine_ref), natural(sine_ref)
    parts = finish(sign, field_ref, cosine, sine, first_ref, real_ref, imag_ref)
    begin(sign, *parts, cosine, sine, whole_left(second_ref[...]), right_ref[...], out_ref)


def plane_order(core):
    return [core * QUARTER + number for number in range(QUARTER)] + [
        (1 - core) * QUARTER + number for number in range(QUARTER)
    ]


def begin_some(sign, real_part, imag_part, cosine, sine, second, right, out_ref):
    real_part, imag_part = rotated(sign, real_part, imag_part, cosine, sine)
    field = from_left(second, jnp.concatenate([real_part, imag_part], axis=0))
    turned = turn_z(field[:ROWS], field[ROWS:], right)
    for number in range(QUARTER):
        for part in range(2):
            piece = turned[number * ROWS : (number + 1) * ROWS, part * ROWS : (part + 1) * ROWS]
            put_rows(out_ref, (part,), number, piece)


def put_rows(ref, index, number, piece):
    blocks = ROWS // PLANES
    for block in range(blocks):
        at = core_place(block, blocks) + index
        ref[at + (pl.ds(number, PLANES, stride=QUARTER), slice(None))] = piece[
            block * PLANES : (block + 1) * PLANES
        ]


def start_kernel(
    given, field_ref, pot_ref, second_ref, right_ref, out_ref, field, pot, second, right, sems
):
    copies = [
        pltpu.make_async_copy(source, target, sems.at[number])
        for number, (source, target) in enumerate(
            ((pot_ref, pot), (field_ref, field), (second_ref, second), (right_ref, right))
        )
    ]
    for copy in copies:
        copy.start()
    order = plane_order(lax.axis_index("ka"))[given * QUARTER : (given + 1) * QUARTER]
    copies[0].wait()
    if out_ref.shape[2] > 2:
        for number, plane in enumerate(order):
            put_rows(out_ref, (2,), number, pot[plane])
    cosine, sine = cos_sin(
        0.5 * sub_time * jnp.concatenate([pot[plane] for plane in order], axis=1)
    )
    for copy in copies[1:]:
        copy.wait()
    begin_some(
        1.0,
        jnp.concatenate([field[0, 0, 0, plane] for plane in order], axis=1),
        jnp.concatenate([field[0, 0, 1, plane] for plane in order], axis=1),
        cosine,
        sine,
        whole_left(second[...]),
        right[...],
        out_ref,
    )


def join_kernel(keep_ref, got_ref, out_ref):
    core = lax.axis_index("ka")
    parts = got_ref.shape[2]
    for to in range(2):
        out_ref[to, core] = keep_ref[to]
        out_ref[to, 1 - core, :, 0:parts] = got_ref[to]
        if keep_ref.shape[2] > parts:
            out_ref[to, 1 - core, :, parts] = keep_ref[to, :, parts]


def end_kernel(
    sign,
    field_ref,
    cosine_ref,
    sine_ref,
    first_ref,
    other_real_ref,
    other_imag_ref,
    factor_ref,
    real_ref,
    imag_ref,
    density_ref,
):
    cosine, sine = natural(cosine_ref), natural(sine_ref)
    real_part, imag_part = finish(
        sign, field_ref, cosine, sine, first_ref, real_ref, imag_ref
    )
    factor = factor_ref[0, 0]
    for plane in range(PLANES):
        density_ref[plane] = factor * (
            lane(real_part, plane) * other_real_ref[plane]
            + lane(imag_part, plane) * other_imag_ref[plane]
        )


def finish_all(sign, field_ref, got_ref, pot_ref, first_ref):
    core = lax.axis_index("ka")
    order = plane_order(core)
    blocks = ROWS // PLANES

    def part_of(part):
        planes = []
        for number in range(PLANES):
            at = (part, pl.ds(number % QUARTER * PLANES, PLANES), slice(None))
            rows = [
                field_ref[(to, core, chip) + at] if number < QUARTER else got_ref[(to, chip) + at]
                for to, chip in (core_place(block, blocks) for block in range(blocks))
            ]
            planes.append(jnp.concatenate(rows, axis=0))
        return jnp.concatenate(planes, axis=1)

    cosine, sine = cos_sin(
        0.5 * sub_time * jnp.concatenate([pot_ref[plane] for plane in order], axis=1)
    )
    field = from_left(
        whole_left(first_ref[...]), jnp.concatenate([part_of(0), part_of(1)], axis=0)
    )
    return order, rotated(sign, field[:ROWS], field[ROWS:], cosine, sine)


def final_kernel(sign, field_ref, got_ref, pot_ref, first_ref, out_ref):
    order, (real_part, imag_part) = finish_all(sign, field_ref, got_ref, pot_ref, first_ref)
    for number, plane in enumerate(order):
        out_ref[0, 0, 0, plane] = lane(real_part, number)
        out_ref[0, 0, 1, plane] = lane(imag_part, number)


def end_all_kernel(
    sign,
    field_ref,
    got_ref,
    pot_ref,
    first_ref,
    other_ref,
    factor_ref,
    real_ref,
    imag_ref,
    density_ref,
):
    order, (real_part, imag_part) = finish_all(sign, field_ref, got_ref, pot_ref, first_ref)
    factor = factor_ref[0, 0]
    for number, plane in enumerate(order):
        real_ref[plane] = lane(real_part, number)
        imag_ref[plane] = lane(imag_part, number)
        density_ref[plane] = factor * (
            lane(real_part, number) * other_ref[0, 0, 0, plane]
            + lane(imag_part, number) * other_ref[0, 0, 1, plane]
        )


def density_all_kernel(
    own_ref, other_ref, left_ref, right_ref, density_ref, out_ref, whole_ref
):
    density = natural(own_ref) + natural(other_ref)
    store_natural(density_ref, density)
    spectrum = from_right(stack_planes(from_left(left_ref[...], density)), right_ref[...])
    for plane in range(PLANES):
        for block in range(ROWS // PLANES):
            start = plane * ROWS + block * PLANES
            whole_ref[block, pl.ds(plane, PLANES, stride=PLANES), :] = spectrum[
                start : start + PLANES
            ]
    size = QUARTER * PLANES
    start = pl.multiple_of(lax.axis_index("ka") * size, size)
    out_ref[...] = whole_ref[:, pl.ds(start, size), :]


def hartree_all_kernel(
    sign,
    given,
    field_ref,
    got_ref,
    density_ref,
    xc_ref,
    orbital_real_ref,
    orbital_imag_ref,
    adjoint_ref,
    pot_ref,
    cas_left_ref,
    cas_right_ref,
    second_ref,
    right_ref,
    out_ref,
    rows_ref,
):
    core = lax.axis_index("ka")
    order = plane_order(core)[given * QUARTER : (given + 1) * QUARTER]
    rows_ref[core] = field_ref[...]
    rows_ref[1 - core] = got_ref[...]
    spectrum = jnp.concatenate(
        [
            jnp.concatenate(
                [
                    rows_ref[number, block, pl.ds(plane, QUARTER, stride=PLANES), :]
                    for block in range(field_ref.shape[0])
                    for number in range(2)
                ],
                axis=0,
            )
            for plane in order
        ],
        axis=1,
    )
    hartree = from_right(
        stack_planes(from_left(cas_left_ref[...], spectrum)), cas_right_ref[...]
    )
    real_parts, imag_parts = [], []
    for number, plane in enumerate(order):
        cross = (
            hartree[number * ROWS : (number + 1) * ROWS] + xc_ref[plane] * density_ref[plane]
        )
        real_parts.append(
            adjoint_ref[0, 0, 0, plane] + step_time * cross * orbital_imag_ref[plane]
        )
        imag_parts.append(
            adjoint_ref[0, 0, 1, plane] - step_time * cross * orbital_real_ref[plane]
        )
    cosine, sine = cos_sin(
        0.5 * sub_time * jnp.concatenate([pot_ref[plane] for plane in order], axis=1)
    )
    begin_some(
        sign,
        jnp.concatenate(real_parts, axis=1),
        jnp.concatenate(imag_parts, axis=1),
        cosine,
        sine,
        whole_left(second_ref[...]),
        right_ref[...],
        out_ref,
    )


def stack_planes(value):
    planes = value.shape[1] // ROWS
    return jnp.concatenate([lane(value, plane) for plane in range(planes)], axis=0)


def density_kernel(own_ref, other_ref, left_ref, right_ref, density_ref, out_ref):
    density = natural(own_ref) + natural(other_ref)
    store_natural(density_ref, density)
    spectrum = from_right(stack_planes(from_left(left_ref[...], density)), right_ref[...])
    for plane in range(PLANES):
        for block in range(ROWS // PLANES):
            start = plane * ROWS + block * PLANES
            rows_to(out_ref, block, (), plane, spectrum[start : start + PLANES])


def coulomb_kernel(unit, placed, field_ref, square_ref, left_ref, out_ref):
    blocks, lines = field_ref.shape[:2]
    places = [place_of(block, blocks) if placed else block for block in range(blocks)]
    rows = jnp.concatenate(
        [
            jnp.concatenate([field_ref[place, line] for place in places], axis=0)
            for line in range(lines)
        ],
        axis=1,
    )
    rows = from_left(left_ref[...], rows)
    index = lax.broadcasted_iota(jnp.int32, (ROWS, ROWS), 0)
    number = unit * jnp.where(index < ROWS // 2, index, index - ROWS).astype(jnp.float32)
    along = number * number
    parts = []
    for line in range(lines):
        square = along + square_ref[pl.ds(line, 1), :]
        nonzero = square > 0
        inverse = jnp.where(nonzero, 4.0 * math.pi / jnp.where(nonzero, square, 1.0), 0.0)
        parts.append(lane(rows, line) * inverse)
    rows = from_left(left_ref[...], jnp.concatenate(parts, axis=1))
    for line in range(lines):
        for block, place in enumerate(places):
            out_ref[place, line] = lane(rows, line)[block * PLANES : (block + 1) * PLANES]


def hartree_kernel(
    sign,
    field_ref,
    density_ref,
    xc_ref,
    orbital_real_ref,
    orbital_imag_ref,
    adjoint_real_ref,
    adjoint_imag_ref,
    cosine_ref,
    sine_ref,
    cas_left_ref,
    cas_right_ref,
    second_ref,
    right_ref,
    out_ref,
    cross_ref,
):
    spectrum = jnp.concatenate(
        [gathered(field_ref, pl.ds(plane, PLANES, stride=PLANES)) for plane in range(PLANES)],
        axis=1,
    )
    hartree = from_right(
        stack_planes(from_left(cas_left_ref[...], spectrum)), cas_right_ref[...]
    )
    real_parts, imag_parts = [], []
    for plane in range(PLANES):
        cross = hartree[plane * ROWS : (plane + 1) * ROWS] + xc_ref[plane] * density_ref[plane]
        cross_ref[plane] = cross
        real_parts.append(adjoint_real_ref[plane] + step_time * cross * orbital_imag_ref[plane])
        imag_parts.append(adjoint_imag_ref[plane] - step_time * cross * orbital_real_ref[plane])
    begin(
        sign,
        jnp.concatenate(real_parts, axis=1),
        jnp.concatenate(imag_parts, axis=1),
        natural(cosine_ref),
        natural(sine_ref),
        whole_left(second_ref[...]),
        right_ref[...],
        out_ref,
    )


def run(kernel, outputs, *operands, space=pltpu.VMEM, scratch=()):
    made = pl.pallas_call(
        kernel,
        out_shape=[
            jax.ShapeDtypeStruct(out, jnp.float32) if isinstance(out, tuple) else out
            for out in outputs
        ],
        in_specs=[
            pl.BlockSpec(memory_space=pltpu.SMEM if operand.size < ROWS else space)
            for operand in operands
        ],
        out_specs=[pl.BlockSpec(memory_space=pltpu.VMEM) for _ in outputs],
        scratch_shapes=list(scratch),
        compiler_params=pltpu.CompilerParams(vmem_limit_bytes=24 * 2**20),
    )(*operands)
    return made[0] if len(outputs) == 1 else made


def grouped(
    orbitals, costate, potential, xc_kernel, vector_potential, kpoint_weight, occupation
):
    grid_size = potential.shape[1]
    blocks = lax.axis_size("fft")
    half = blocks // 2
    core = lax.axis_index("ka")
    fft_index = lax.axis_index("fft")
    side = fft_index // half
    place = core * half + fft_index % half
    lattice_unit = 2.0 * math.pi / (grid_size * spacing)

    groups = []
    for h in range(2):
        devices = [c * blocks + h * half + j for c in range(2) for j in range(half)]
        group = [0] * blocks
        for block, device in enumerate(devices):
            group[place_of(block, blocks)] = device
        groups.append(group)
    everyone = [0] * (2 * blocks)
    for number, source in enumerate(sources_of(blocks)):
        everyone[source] = number % 2 * blocks + number // 2
    regroup = []
    for c in range(2):
        for f in range(blocks):
            h, j = f // half, f % half
            regroup.append((c * blocks + f, h * blocks + c * half + j))
    across = [
        (c * blocks + f, c * blocks + (f + half) % blocks) for c in range(2) for f in range(blocks)
    ]

    def exchange(array):
        return lax.all_to_all(array, AXES, 0, 0, axis_index_groups=groups, tiled=True)

    def exchange_whole(array):
        return lax.all_to_all(array, "fft", 0, 0, tiled=True)

    def exchange_all(array):
        return lax.all_to_all(
            array, AXES, 0, 0, axis_index_groups=[everyone], tiled=True
        )

    def other_core(array):
        return lax.ppermute(array, "ka", [(0, 1), (1, 0)])

    def joined(keep, give):
        return run(join_kernel, [(2,) + keep.shape], keep, other_core(give))

    def to_halves(sent):
        return exchange_all(sent.reshape((2 * blocks,) + sent.shape[3:]))

    def from_halves(sent):
        field = exchange_all(sent).reshape(2, 2, half, 2, PLANES * QUARTER, ROWS)
        give = lax.dynamic_index_in_dim(field, 1 - core, 1, keepdims=False)
        return field, other_core(give)

    def move(array, pairs):
        return lax.ppermute(array, AXES, pairs)

    block_shape = (blocks, 2, PLANES, PLANES, ROWS)
    sent_shape = (blocks, 2, PLANES * PLANES, ROWS)
    natural_shape = (2, PLANES, ROWS, ROWS)
    real_shape = (PLANES, ROWS, ROWS)

    def swap_field(array):
        return exchange(array.reshape(block_shape))

    grid_line = np.arange(grid_size)
    angles = 2.0 * np.pi / grid_size * (np.outer(grid_line, grid_line) % grid_size)
    line_pair = jnp.asarray(
        np.concatenate([np.cos(angles), np.sin(angles)], axis=1).astype(np.float32)
    )
    cas = (np.cos(angles) + np.sin(angles)) / math.sqrt(grid_size)
    cas_left, cas_right = constant_table(cas, 1), constant_table(cas, 0)
    line_y = constant_circulant(0.25 * lattice_unit, grid_size)
    line_z = constant_circulant(-0.25 * lattice_unit, grid_size)
    tables_y = {1.0: constant_table(line_y[0][:ROWS], 1), -1.0: constant_table(line_y[1][:ROWS], 1)}
    right_z = {1.0: constant_table(line_z[1], 0), -1.0: constant_table(line_z[0], 0)}

    shift_x = lattice_unit * ((side.astype(jnp.float32) + 0.5) / 2 - 0.5) + vector_potential
    count_x = STEPS * SUB

    numbers = wave_numbers(lax.iota(jnp.int32, grid_size), grid_size)
    def squares_of(first, count):
        own = wave_numbers(first + lax.iota(jnp.int32, count), grid_size)
        return (own * own)[:, None] + (numbers * numbers)[None, :]

    squares = squares_of(place * PLANES, PLANES)
    squares_all = squares_of(fft_index * PLANES + core * QUARTER, QUARTER)

    def factor_of(k_index):
        own_weight = lax.dynamic_slice_in_dim(kpoint_weight, k_index, 1)[0].astype(jnp.float32)
        weight = own_weight / jnp.sum(kpoint_weight).astype(jnp.float32)
        return (2.0 * weight * occupation.astype(jnp.float32) / 100.0).reshape(1, 1)

    factor, factor_all = factor_of(side), factor_of(core)

    def start(given, parts):
        return run(
            functools.partial(start_kernel, given),
            [(2, half, parts, PLANES * QUARTER, ROWS)],
            orbitals,
            potential,
            tables_y[1.0],
            right_z[1.0],
            space=pltpu.HBM,
            scratch=[
                pltpu.VMEM(orbitals.shape, jnp.float32),
                pltpu.VMEM(real_shape, jnp.float32),
                pltpu.VMEM(tables_y[1.0].shape, jnp.bfloat16),
                pltpu.VMEM(right_z[1.0].shape, jnp.bfloat16),
                pltpu.SemaphoreType.DMA((4,)),
            ],
        )

    give = start(1, 2)
    sent = joined(start(0, 3), give)
    sent, shift_x = lax.optimization_barrier((sent, shift_x))
    field = to_halves(sent)
    made = run(
        table_kernel,
        [jax.ShapeDtypeStruct((ROWS, 4 * ROWS), jnp.bfloat16)] * (2 * count_x),
        shift_x,
        line_pair,
    )
    early = (squares, squares_all, factor, factor_all)
    made, early = lax.optimization_barrier((made, early))
    squares, squares_all, factor, factor_all = early
    tables_x = {1.0: made[::2], -1.0: made[1::2]}

    def table_x(sign, count):
        return tables_x[sign][count if sign > 0 else count_x - 1 - count]

    def table_y(sign):
        return tables_y[sign]

    def tables_of(sign, count):
        if count % 2 == 0:
            return table_y(sign), table_y(sign), right_z[sign]
        return table_x(sign, count - 1), table_x(sign, count), right_z[sign]

    def middle(sign, field, count):
        waves = waves_rows if count % 2 == 0 else waves_cols
        return run(
            functools.partial(mid_kernel, sign),
            [sent_shape],
            field,
            *waves,
            *tables_of(sign, count),
        )

    sent, *waves_cols = run(
        functools.partial(first_mid_kernel, 1.0),
        [(blocks, 3) + sent_shape[2:], real_shape, real_shape],
        field,
        *tables_of(1.0, 1),
    )
    sent, *waves_rows = run(
        functools.partial(second_mid_kernel, 1.0),
        [sent_shape, real_shape, real_shape],
        exchange(sent.reshape(blocks, 3, PLANES, PLANES, ROWS)),
        *tables_of(1.0, 2),
    )
    sent = middle(1.0, swap_field(sent), 3)
    kept = []
    all_shape = (2 * blocks, 2, PLANES * QUARTER, ROWS)
    for count in range(4, count_x - 1):
        field = swap_field(sent)
        if count % SUB == 0:
            sent, *orbital = run(
                functools.partial(step_kernel, 1.0),
                [sent_shape, real_shape, real_shape],
                field,
                *waves_rows,
                *tables_of(1.0, count),
            )
            kept.append(orbital)
        else:
            sent = middle(1.0, field, count)
    sent = run(
        functools.partial(last_mid_kernel, 1.0),
        [all_shape],
        swap_field(sent),
        *waves_cols,
        *tables_of(1.0, count_x - 1),
    )
    *orbital, partial = run(
        functools.partial(end_all_kernel, 1.0),
        [real_shape] * 3,
        *from_halves(sent),
        potential,
        table_y(1.0),
        costate,
        factor_all,
    )

    density, sent = run(
        density_all_kernel,
        [real_shape, (blocks, QUARTER * PLANES, ROWS)],
        partial,
        other_core(partial),
        cas_left,
        cas_right,
        scratch=[pltpu.VMEM((blocks, PLANES * PLANES, ROWS), jnp.float32)],
    )
    field = exchange_whole(sent.reshape(blocks, QUARTER, PLANES, ROWS))
    sent = run(
        functools.partial(coulomb_kernel, lattice_unit, False),
        [(blocks, QUARTER, PLANES, ROWS)],
        field,
        squares_all,
        cas_left,
    )
    field = exchange_whole(sent)
    field = field.reshape(blocks, QUARTER * PLANES, ROWS)
    got = other_core(field)

    def restart(given):
        return run(
            functools.partial(hartree_all_kernel, -1.0, given),
            [(2, half, 2, PLANES * QUARTER, ROWS)],
            field,
            got,
            density,
            xc_kernel,
            *orbital,
            costate,
            potential,
            cas_left,
            cas_right,
            table_y(-1.0),
            right_z[-1.0],
            scratch=[pltpu.VMEM((2, blocks, QUARTER * PLANES, ROWS), jnp.float32)],
        )

    give = restart(1)
    sent = run(
        functools.partial(all_mid_kernel, -1.0),
        [sent_shape],
        to_halves(joined(restart(0), give)),
        *waves_cols,
        *tables_of(-1.0, 1),
    )
    for step_index in range(STEPS - 1, -1, -1):
        first = (STEPS - 1 - step_index) * SUB
        if step_index < STEPS - 1:
            density, sent = run(
                density_kernel,
                [real_shape, (blocks, PLANES * PLANES, ROWS)],
                partial,
                move(partial, across),
                cas_left,
                cas_right,
            )
            field = exchange(sent.reshape(blocks, PLANES, PLANES, ROWS))
            sent = run(
                functools.partial(coulomb_kernel, lattice_unit, True),
                [(blocks, PLANES, PLANES, ROWS)],
                field,
                squares,
                cas_left,
            )
            field = exchange(sent).reshape(blocks, PLANES * PLANES, ROWS)
            sent, cross = run(
                functools.partial(hartree_kernel, -1.0),
                [sent_shape, real_shape],
                field,
                density,
                xc_rows,
                *kept[step_index],
                *adjoint,
                *waves_rows,
                cas_left,
                cas_right,
                table_y(-1.0),
                right_z[-1.0],
            )
            sent = middle(-1.0, swap_field(sent), first + 1)
            field = swap_field(sent)
        else:
            sent, xc_rows = lax.optimization_barrier((sent, xc_kernel))
            field = swap_field(sent)
            field, xc_rows = lax.optimization_barrier((field, move(xc_rows, regroup)))
        sent = middle(-1.0, field, first + 2)
        field = swap_field(sent)
        if step_index > 0:
            sent = middle(-1.0, field, first + SUB - 1)
            *adjoint, partial = run(
                functools.partial(end_kernel, -1.0),
                [real_shape] * 3,
                swap_field(sent),
                *waves_rows,
                table_y(-1.0),
                *kept[step_index - 1],
                factor,
            )
    sent = run(
        functools.partial(last_mid_kernel, -1.0),
        [all_shape],
        field,
        *waves_cols,
        *tables_of(-1.0, count_x - 1),
    )
    result = run(
        functools.partial(final_kernel, -1.0),
        [orbitals.shape],
        *from_halves(sent),
        potential,
        table_y(-1.0),
    )
    return (result, jnp.where(core == side, cross, other_core(cross)))


def solution(mesh):
    placed = (
        P("ka", None, None, "fft", None, None),
        P("ka", None, None, "fft", None, None),
        P("fft", None, None),
        P("fft", None, None),
        P(),
        P(),
        P(),
    )

    def local(*arguments):
        orbitals, potential = arguments[0], arguments[2]
        fits = (
            mesh.shape["ka"] == 2
            and mesh.shape["fft"] % 2 == 0
            and orbitals.shape[:2] == (1, 1)
            and potential.shape == (PLANES, ROWS, ROWS)
        )
        return grouped(*arguments) if fits else plain(*arguments)

    return jax.shard_map(
        local,
        mesh=mesh,
        in_specs=placed,
        out_specs=(P("ka", None, None, "fft", None, None), P("fft", None, None)),
        check_vma=False,
    )
```

```python
import functools
import math

import jax
import jax.numpy as jnp
import numpy as np
from jax import lax
from jax.experimental import pallas as pl
from jax.experimental.pallas import tpu as pltpu
from jax.sharding import PartitionSpec as P

STEPS = 2
SUB = 4


spacing = 0.25
step_time = 0.6
sub_time = step_time / SUB
highest = lax.Precision.HIGHEST


def wave_numbers(grid_line, grid_size):
    signed_line = jnp.where(grid_line < grid_size // 2, grid_line, grid_line - grid_size)
    return 2.0 * math.pi / (grid_size * spacing) * signed_line.astype(jnp.float32)


def table_angles(grid_size):
    row_index = lax.broadcasted_iota(jnp.int32, (grid_size, grid_size), 0)
    col_index = lax.broadcasted_iota(jnp.int32, (grid_size, grid_size), 1)
    return 2.0 * math.pi / grid_size * (row_index * col_index % grid_size).astype(jnp.float32)


def line_matrices(shifts, grid_size):
    numbers = wave_numbers(lax.iota(jnp.int32, grid_size), grid_size)
    along = shifts[:, None] + numbers[None, :]
    phase = 0.5 * sub_time * (along * along)
    angles = table_angles(grid_size)
    cosine, sine = jnp.cos(angles), jnp.sin(angles)
    q_real, q_imag = jnp.cos(phase)[:, None, :], -jnp.sin(phase)[:, None, :]
    left_real = (cosine * q_real - sine * q_imag) / grid_size
    left_imag = (cosine * q_imag + sine * q_real) / grid_size
    both = jnp.stack([left_real, left_imag])
    by_cos = jnp.einsum("csam,mb->csab", both, cosine, precision=highest)
    by_sin = jnp.einsum("csam,mb->csab", both, sine, precision=highest)
    return by_cos[0] + by_sin[1], by_cos[1] - by_sin[0]


def real_form(real_part, imag_part):
    upper = jnp.stack([real_part, -imag_part], axis=-2)
    lower = jnp.stack([imag_part, real_part], axis=-2)
    return jnp.stack([upper, lower], axis=-4)


def spin(field, angle):
    cosine, sine = jnp.cos(angle), jnp.sin(angle)
    return jnp.stack(
        [field[0] * cosine + field[1] * sine, field[1] * cosine - field[0] * sine]
    )


def apply(form, matrix, field):
    return jnp.einsum(
        form, matrix, field, precision=lax.Precision.HIGHEST, preferred_element_type=jnp.float32
    )


def plain(orbitals, costate, potential, xc_kernel, vector_potential, kpoint_weight, occupation):
    grid_size = potential.shape[1]
    k_index = lax.axis_index("ka")
    fft_index = lax.axis_index("fft")
    planes = potential.shape[0]
    lattice_unit = 2.0 * math.pi / (grid_size * spacing)
    k_fraction = (k_index.astype(jnp.float32) + 0.5) / lax.axis_size("ka") - 0.5
    shifts = jnp.concatenate(
        [
            lattice_unit * k_fraction + vector_potential,
            jnp.array([lattice_unit * 0.25, -lattice_unit * 0.25], jnp.float32),
        ]
    )
    lines = real_form(*line_matrices(shifts, grid_size))
    back = jnp.transpose(lines, (0, 3, 4, 1, 2))

    def to_columns(field, split, concat):
        return lax.all_to_all(field, "fft", split_axis=split, concat_axis=concat, tiled=True)

    pot_rows = 0.5 * sub_time * potential
    pot_cols = to_columns(pot_rows, 1, 0)

    def propagate(field, step_index, sign):
        table = lines if sign > 0 else back
        order = range(SUB) if sign > 0 else range(SUB - 1, -1, -1)
        mat_y, mat_z = table[STEPS * SUB], table[STEPS * SUB + 1]
        in_rows = True
        field = spin(field, sign * pot_rows)
        for count, sub_index in enumerate(order):
            mat_x = table[step_index * SUB + sub_index]
            last = count == SUB - 1
            turn = sign * (1.0 if last else 2.0)
            field = apply("cadb,dkxyb->ckxya", mat_z, field)
            if in_rows:
                field = apply("cadb,dkxbz->ckxaz", mat_y, field)
                field = to_columns(field, 3, 2)
                field = apply("cadb,dkbyz->ckayz", mat_x, field)
                field = spin(field, turn * pot_cols)
            else:
                field = apply("cadb,dkbyz->ckayz", mat_x, field)
                field = to_columns(field, 2, 3)
                field = apply("cadb,dkxbz->ckxaz", mat_y, field)
                field = spin(field, turn * pot_rows)
            in_rows = not in_rows
        return field

    def parts_first(field):
        bands = field.shape[0] * field.shape[1]
        return jnp.moveaxis(field, 2, 0).reshape((2, bands) + field.shape[3:])

    angles = table_angles(grid_size)
    cas = (jnp.cos(angles) + jnp.sin(angles)) / math.sqrt(grid_size)
    numbers = wave_numbers(lax.iota(jnp.int32, grid_size), grid_size)
    numbers_local = wave_numbers(fft_index * planes + lax.iota(jnp.int32, planes), grid_size)
    g_squared = (
        (numbers * numbers)[:, None, None]
        + (numbers_local * numbers_local)[None, :, None]
        + (numbers * numbers)[None, None, :]
    )
    coulomb = jnp.where(
        g_squared > 0, 4.0 * math.pi / jnp.where(g_squared > 0, g_squared, 1.0), 0.0
    )
    orbital = parts_first(orbitals)
    history = [orbital]
    for step_index in range(STEPS):
        orbital = propagate(orbital, step_index, 1.0)
        history.append(orbital)
    occupied = occupation.astype(jnp.float32) / 100.0
    own_weight = lax.dynamic_slice_in_dim(kpoint_weight, k_index, 1)[0].astype(jnp.float32)
    weight = own_weight / jnp.sum(kpoint_weight).astype(jnp.float32)
    band_factor = 2.0 * weight * occupied
    adjoint = parts_first(costate)
    cross_pot = jnp.zeros_like(potential)
    for step_index in range(STEPS - 1, -1, -1):
        forward = history[step_index + 1]
        density = lax.psum(
            jnp.sum(band_factor[:, None, None, None] * jnp.sum(adjoint * forward, axis=0), axis=0),
            "ka",
        )
        hartree = apply("ab,xyb->xya", cas, density)
        hartree = apply("ab,xbz->xaz", cas, hartree)
        hartree = to_columns(hartree, 1, 0)
        hartree = apply("ab,byz->ayz", cas, hartree)
        hartree = apply("ab,byz->ayz", cas, hartree * coulomb)
        hartree = to_columns(hartree, 0, 1)
        hartree = apply("ab,xbz->xaz", cas, hartree)
        hartree = apply("ab,xyb->xya", cas, hartree)
        cross_pot = hartree + xc_kernel * density
        turned = jnp.stack([forward[1], -forward[0]])
        adjoint = propagate(adjoint + step_time * cross_pot * turned, step_index, -1.0)
    result = jnp.moveaxis(adjoint.reshape((2,) + orbitals.shape[:2] + adjoint.shape[2:]), 0, 2)
    return (result, cross_pot)


ROWS = 128
PLANES = 8
QUARTER = 4
AXES = ("ka", "fft")


def halves_of(value):
    high = value.astype(jnp.bfloat16)
    return high, (value - high.astype(jnp.float32)).astype(jnp.bfloat16)


def from_left(table, field):
    size = table.shape[1] // 2
    high, low = halves_of(field)
    return jnp.dot(
        jnp.concatenate([table[:, :size], table], axis=1),
        jnp.concatenate([high, low, high], axis=0),
        preferred_element_type=jnp.float32,
    )


def from_right(field, table):
    size = table.shape[0] // 2
    high, low = halves_of(field)
    return jnp.dot(
        jnp.concatenate([high, low, high], axis=1),
        jnp.concatenate([table[:size], table], axis=0),
        preferred_element_type=jnp.float32,
    )


def side_by_side(matrix, axis):
    return jnp.concatenate(halves_of(matrix), axis=axis)


def own_shift(count):
    side = lax.axis_index("fft") // (count // 2)
    return 0.5 * (jnp.full((ROWS, ROWS), side, jnp.int32).astype(jnp.float32) + 0.5) - 0.5


def circulant(shift, numbers, cosine, sine):
    along = shift + numbers
    phase = 0.5 * sub_time * (along * along)
    q_real, q_imag = jnp.cos(phase), -jnp.sin(phase)
    even = q_real * cosine + q_imag * sine
    odd = q_real * sine - q_imag * cosine
    spectrum = jnp.concatenate(
        [jnp.concatenate([even, odd], axis=1), jnp.concatenate([odd, -even], axis=1)], axis=0
    )
    upper = jnp.dot(
        jnp.concatenate([cosine, sine], axis=1),
        spectrum,
        precision=highest,
        preferred_element_type=jnp.float32,
    ) * (1.0 / ROWS)
    real_part, minus = upper[:, :ROWS], upper[:, ROWS:]
    real_turned, minus_turned = real_part.T, minus.T
    return upper, jnp.concatenate([real_turned, -minus_turned], axis=1)


def whole_matrix(upper):
    real_part, minus = upper[:, :ROWS], upper[:, ROWS:]
    return jnp.concatenate([upper, jnp.concatenate([-minus, real_part], axis=1)], axis=0)


def whole_left(table):
    return jnp.concatenate(
        [whole_matrix(table[:, : 2 * ROWS]), whole_matrix(table[:, 2 * ROWS :])], axis=1
    )


def table_kernel(unit, push_ref, lines_ref, *out_refs):
    numbers = wave_numbers(lax.broadcasted_iota(jnp.int32, (ROWS, ROWS), 0), ROWS)
    numbers = numbers + unit * own_shift(ROWS // PLANES)
    cosine, sine = lines_ref[:, :ROWS], lines_ref[:, ROWS:]
    pairs = (len(out_refs) + 1) // 2
    for line in range(2 * pairs):
        pair, which = divmod(line, 2)
        matrix, turned = circulant(push_ref[line], numbers, cosine, sine)
        if pair > 0:
            out_refs[pair - 1][which] = side_by_side(matrix, 1)
        out_refs[2 * pairs - 2 - pair][1 - which] = side_by_side(turned, 1)


def constant_circulant(shift, grid_size):
    grid_line = np.arange(grid_size)
    signed_line = np.where(grid_line < grid_size // 2, grid_line, grid_line - grid_size)
    along = shift + 2.0 * math.pi / (grid_size * spacing) * signed_line
    waves = np.exp(2j * np.pi / grid_size * (np.outer(grid_line, grid_line) % grid_size))
    line = (waves * np.exp(-0.5j * sub_time * along * along)) @ waves.conj() / grid_size
    whole = np.block([[line.real, -line.imag], [line.imag, line.real]])
    return whole, whole.T


def constant_table(matrix, axis):
    high = matrix.astype(jnp.bfloat16)
    low = (matrix - high.astype(np.float64)).astype(jnp.bfloat16)
    return jnp.asarray(np.concatenate([high, low], axis=axis))


def cos_sin(angle):
    square = angle * angle
    cosine = sine = 1.0
    for order in range(10, 0, -2):
        cosine = 1.0 - cosine * (square * (1.0 / (order * (order - 1))))
        sine = 1.0 - sine * (square * (1.0 / (order * (order + 1))))
    return cosine, sine * angle


def rotated(sign, real_part, imag_part, cosine, sine):
    if sign > 0:
        return real_part * cosine + imag_part * sine, imag_part * cosine - real_part * sine
    return real_part * cosine - imag_part * sine, imag_part * cosine + real_part * sine


def doubled(cosine, sine):
    return 1.0 - 2.0 * (sine * sine), 2.0 * sine * cosine


def place_of(block, blocks):
    core, rest = divmod(block, blocks // 2)
    return rest // 2 * 4 + core * 2 + rest % 2


def gathered(ref, *index):
    blocks = ref.shape[0]
    return jnp.concatenate(
        [ref[(place_of(block, blocks),) + index] for block in range(blocks)], axis=0
    )


def gather_planes(ref):
    return jnp.concatenate(
        [
            jnp.concatenate([gathered(ref, part, plane) for plane in range(PLANES)], axis=1)
            for part in range(2)
        ],
        axis=0,
    )


def natural(ref):
    return jnp.concatenate([ref[plane] for plane in range(PLANES)], axis=1)


def lane(value, plane):
    return value[:, plane * ROWS : (plane + 1) * ROWS]


def core_place(block, blocks):
    core, chip = divmod(block, blocks // 2)
    bits = (blocks // 2).bit_length() - 1
    return core, sum((chip >> bit & 1) << (bits - 1 - bit) for bit in range(bits))


def sources_of(blocks):
    half = blocks // 2
    return [
        (core * 2 + block // half) * half + core_place(block % half, blocks)[1]
        for block in range(blocks)
        for core in range(2)
    ]


def rows_to(out_ref, block, index, plane, piece):
    if not isinstance(out_ref, tuple):
        place = place_of(block, out_ref.shape[0])
        out_ref[(place,) + index + (pl.ds(plane, PLANES, stride=PLANES), slice(None))] = piece
        return
    sources = sources_of(out_ref[0].shape[0] // 2)
    for core in range(2):
        at = (sources[2 * block + core],) + index
        out_ref[0][at + (pl.ds(plane, QUARTER, stride=PLANES), slice(None))] = piece[
            core * QUARTER : (core + 1) * QUARTER
        ]


def turn_z(real_part, imag_part, table):
    rows = jnp.concatenate(
        [
            jnp.concatenate([lane(real_part, plane), lane(imag_part, plane)], axis=1)
            for plane in range(real_part.shape[1] // ROWS)
        ],
        axis=0,
    )
    return from_right(rows, table)


def scatter_planes(real_part, imag_part, table, out_ref):
    blocks = ROWS // PLANES
    turned = turn_z(real_part, imag_part, table)
    for plane in range(PLANES):
        for part in range(2):
            piece = turned[plane * ROWS : (plane + 1) * ROWS, part * ROWS : (part + 1) * ROWS]
            for block in range(blocks):
                rows_of = piece[block * PLANES : (block + 1) * PLANES]
                rows_to(out_ref, block, (part,), plane, rows_of)


def between(sign, field, cosine, sine, first, second, right, out_ref):
    field = from_left(whole_left(first), field)
    real_part, imag_part = rotated(sign, field[:ROWS], field[ROWS:], *doubled(cosine, sine))
    field = from_left(
        whole_left(second), jnp.concatenate([real_part, imag_part], axis=0)
    )
    scatter_planes(field[:ROWS], field[ROWS:], right, out_ref)


def mid_kernel(
    sign, field_ref, cosine_ref, sine_ref, first_ref, second_ref, right_ref, out_ref
):
    cosine, sine = natural(cosine_ref), natural(sine_ref)
    field = gather_planes(field_ref)
    between(
        sign, field, cosine, sine, first_ref[...], second_ref[...], right_ref[...], out_ref
    )


def gather_all(field_ref, part):
    return jnp.concatenate(
        [
            jnp.concatenate(
                [
                    field_ref[source, part, pl.ds(plane * QUARTER, QUARTER), :]
                    for source in sources_of(field_ref.shape[0] // 2)
                ],
                axis=0,
            )
            for plane in range(PLANES)
        ],
        axis=1,
    )


def first_mid_kernel(
    sign, unit, field_ref, push_ref, lines_ref, right_ref, out_ref, cosine_ref, sine_ref
):
    numbers = wave_numbers(lax.broadcasted_iota(jnp.int32, (ROWS, ROWS), 0), ROWS)
    numbers = numbers + unit * own_shift(ROWS // PLANES)
    first, second = (
        side_by_side(
            circulant(push_ref[line], numbers, lines_ref[:, :ROWS], lines_ref[:, ROWS:])[0], 1
        )
        for line in range(2)
    )
    pot = gather_all(field_ref, 2)
    for plane in range(PLANES):
        for block in range(ROWS // PLANES):
            rows_of = lane(pot, plane)[block * PLANES : (block + 1) * PLANES]
            rows_to(out_ref, block, (2,), plane, rows_of)
    cosine, sine = cos_sin(0.5 * sub_time * pot)
    store_natural(cosine_ref, cosine)
    store_natural(sine_ref, sine)
    field = jnp.concatenate([gather_all(field_ref, 0), gather_all(field_ref, 1)], axis=0)
    between(sign, field, cosine, sine, first, second, right_ref[...], out_ref)


def all_mid_kernel(
    sign, field_ref, cosine_ref, sine_ref, first_ref, second_ref, right_ref, out_ref
):
    cosine, sine = natural(cosine_ref), natural(sine_ref)
    field = jnp.concatenate([gather_all(field_ref, 0), gather_all(field_ref, 1)], axis=0)
    between(
        sign, field, cosine, sine, first_ref[...], second_ref[...], right_ref[...], out_ref
    )


def second_mid_kernel(
    sign, field_ref, first_ref, second_ref, right_ref, out_ref, cosine_ref, sine_ref
):
    pot = jnp.concatenate([gathered(field_ref, 2, plane) for plane in range(PLANES)], axis=1)
    cosine, sine = cos_sin(0.5 * sub_time * pot)
    store_natural(cosine_ref, cosine)
    store_natural(sine_ref, sine)
    field = gather_planes(field_ref)
    between(
        sign, field, cosine, sine, first_ref[...], second_ref[...], right_ref[...], out_ref
    )


def last_mid_kernel(
    sign, field_ref, cosine_ref, sine_ref, first_ref, second_ref, right_ref, out_ref
):
    cosine, sine = natural(cosine_ref), natural(sine_ref)
    field = gather_planes(field_ref)
    between(
        sign, field, cosine, sine, first_ref[...], second_ref[...], right_ref[...], (out_ref,)
    )


def store_natural(ref, value):
    for plane in range(PLANES):
        ref[plane] = lane(value, plane)


def density_factor(weight_ref, occupation_ref, k_index):
    def row(value):
        return jnp.full((1, ROWS), value, jnp.int32).astype(jnp.float32)

    total = row(weight_ref[0] + weight_ref[1])
    return 2.0 * (row(weight_ref[k_index]) / total) * (row(occupation_ref[0]) / 100.0)


def finish(sign, field_ref, cosine, sine, first_ref, real_ref, imag_ref):
    field = from_left(whole_left(first_ref[...]), gather_planes(field_ref))
    real_part, imag_part = rotated(sign, field[:ROWS], field[ROWS:], cosine, sine)
    store_natural(real_ref, real_part)
    store_natural(imag_ref, imag_part)
    return real_part, imag_part


def begin(sign, real_part, imag_part, cosine, sine, second, right, out_ref):
    real_part, imag_part = rotated(sign, real_part, imag_part, cosine, sine)
    field = from_left(second, jnp.concatenate([real_part, imag_part], axis=0))
    scatter_planes(field[:ROWS], field[ROWS:], right, out_ref)


def step_kernel(
    sign,
    field_ref,
    cosine_ref,
    sine_ref,
    first_ref,
    second_ref,
    right_ref,
    out_ref,
    real_ref,
    imag_ref,
):
    cosine, sine = natural(cosine_ref), natural(sine_ref)
    parts = finish(sign, field_ref, cosine, sine, first_ref, real_ref, imag_ref)
    begin(sign, *parts, cosine, sine, whole_left(second_ref[...]), right_ref[...], out_ref)


def plane_order(core):
    return [core * QUARTER + number for number in range(QUARTER)] + [
        (1 - core) * QUARTER + number for number in range(QUARTER)
    ]


def begin_some(sign, real_part, imag_part, cosine, sine, second, right, out_ref):
    real_part, imag_part = rotated(sign, real_part, imag_part, cosine, sine)
    field = from_left(second, jnp.concatenate([real_part, imag_part], axis=0))
    turned = turn_z(field[:ROWS], field[ROWS:], right)
    for number in range(QUARTER):
        for part in range(2):
            piece = turned[number * ROWS : (number + 1) * ROWS, part * ROWS : (part + 1) * ROWS]
            put_rows(out_ref, (part,), number, piece)


def put_rows(ref, index, number, piece):
    blocks = ROWS // PLANES
    for block in range(blocks):
        at = core_place(block, blocks) + index
        ref[at + (pl.ds(number, PLANES, stride=QUARTER), slice(None))] = piece[
            block * PLANES : (block + 1) * PLANES
        ]


def start_kernel(
    given, field_ref, pot_ref, second_ref, right_ref, out_ref, field, pot, second, right, sems
):
    start = plane_order(lax.axis_index("ka"))[given * QUARTER]
    copies = [
        pltpu.make_async_copy(source, target, sems.at[number])
        for number, (source, target) in enumerate(
            (
                (pot_ref.at[pl.ds(start, QUARTER)], pot),
                (field_ref.at[0, 0, :, pl.ds(start, QUARTER)], field),
                (second_ref, second),
                (right_ref, right),
            )
        )
    ]
    for copy in copies:
        copy.start()
    copies[0].wait()
    if out_ref.shape[2] > 2:
        for number in range(QUARTER):
            put_rows(out_ref, (2,), number, pot[number])
    planes = range(QUARTER)
    cosine, sine = cos_sin(
        0.5 * sub_time * jnp.concatenate([pot[plane] for plane in planes], axis=1)
    )
    for copy in copies[1:]:
        copy.wait()
    begin_some(
        1.0,
        jnp.concatenate([field[0, plane] for plane in planes], axis=1),
        jnp.concatenate([field[1, plane] for plane in planes], axis=1),
        cosine,
        sine,
        whole_left(second[...]),
        right[...],
        out_ref,
    )


def join_kernel(keep_ref, got_ref, out_ref):
    core = lax.axis_index("ka")
    parts = got_ref.shape[2]
    for to in range(2):
        out_ref[to, core] = keep_ref[to]
        out_ref[to, 1 - core, :, 0:parts] = got_ref[to]
        if keep_ref.shape[2] > parts:
            out_ref[to, 1 - core, :, parts] = keep_ref[to, :, parts]


def end_kernel(
    sign,
    field_ref,
    cosine_ref,
    sine_ref,
    first_ref,
    other_real_ref,
    other_imag_ref,
    weight_ref,
    occupation_ref,
    real_ref,
    imag_ref,
    density_ref,
):
    cosine, sine = natural(cosine_ref), natural(sine_ref)
    real_part, imag_part = finish(
        sign, field_ref, cosine, sine, first_ref, real_ref, imag_ref
    )
    side = lax.axis_index("fft") // (field_ref.shape[0] // 2)
    factor = density_factor(weight_ref, occupation_ref, side)
    for plane in range(PLANES):
        density_ref[plane] = factor * (
            lane(real_part, plane) * other_real_ref[plane]
            + lane(imag_part, plane) * other_imag_ref[plane]
        )


def finish_all(sign, field_ref, got_ref, pot_ref, first_ref):
    core = lax.axis_index("ka")
    order = plane_order(core)
    blocks = ROWS // PLANES

    def part_of(part):
        planes = []
        for number in range(PLANES):
            at = (part, pl.ds(number % QUARTER * PLANES, PLANES), slice(None))
            rows = [
                field_ref[(to, core, chip) + at] if number < QUARTER else got_ref[(to, chip) + at]
                for to, chip in (core_place(block, blocks) for block in range(blocks))
            ]
            planes.append(jnp.concatenate(rows, axis=0))
        return jnp.concatenate(planes, axis=1)

    cosine, sine = cos_sin(
        0.5 * sub_time * jnp.concatenate([pot_ref[plane] for plane in order], axis=1)
    )
    field = from_left(
        whole_left(first_ref[...]), jnp.concatenate([part_of(0), part_of(1)], axis=0)
    )
    return order, rotated(sign, field[:ROWS], field[ROWS:], cosine, sine)


def final_kernel(
    sign,
    field_ref,
    got_ref,
    pot_ref,
    first_ref,
    cross_ref,
    beside_ref,
    out_ref,
    cross_out_ref,
):
    blocks = ROWS // PLANES
    here = lax.axis_index("ka") == lax.axis_index("fft") // (blocks // 2)
    for plane in range(PLANES):
        cross_out_ref[plane] = jnp.where(here, cross_ref[plane], beside_ref[plane])
    order, (real_part, imag_part) = finish_all(sign, field_ref, got_ref, pot_ref, first_ref)
    for number, plane in enumerate(order):
        out_ref[0, 0, 0, plane] = lane(real_part, number)
        out_ref[0, 0, 1, plane] = lane(imag_part, number)


def end_all_kernel(
    sign,
    field_ref,
    got_ref,
    pot_ref,
    first_ref,
    other_ref,
    weight_ref,
    occupation_ref,
    real_ref,
    imag_ref,
    density_ref,
):
    order, (real_part, imag_part) = finish_all(sign, field_ref, got_ref, pot_ref, first_ref)
    factor = density_factor(weight_ref, occupation_ref, lax.axis_index("ka"))
    for number, plane in enumerate(order):
        real_ref[plane] = lane(real_part, number)
        imag_ref[plane] = lane(imag_part, number)
        density_ref[plane] = factor * (
            lane(real_part, number) * other_ref[0, 0, 0, plane]
            + lane(imag_part, number) * other_ref[0, 0, 1, plane]
        )


def density_all_kernel(
    own_ref, other_ref, left_ref, right_ref, density_ref, out_ref, whole_ref
):
    density = natural(own_ref) + natural(other_ref)
    store_natural(density_ref, density)
    spectrum = from_right(stack_planes(from_left(left_ref[...], density)), right_ref[...])
    for plane in range(PLANES):
        for block in range(ROWS // PLANES):
            start = plane * ROWS + block * PLANES
            whole_ref[block, pl.ds(plane, PLANES, stride=PLANES), :] = spectrum[
                start : start + PLANES
            ]
    size = QUARTER * PLANES
    start = pl.multiple_of(lax.axis_index("ka") * size, size)
    out_ref[...] = whole_ref[:, pl.ds(start, size), :]


def hartree_all_kernel(
    sign,
    given,
    field_ref,
    got_ref,
    density_ref,
    xc_ref,
    orbital_real_ref,
    orbital_imag_ref,
    adjoint_ref,
    pot_ref,
    cas_left_ref,
    cas_right_ref,
    second_ref,
    right_ref,
    out_ref,
    rows_ref,
):
    core = lax.axis_index("ka")
    order = plane_order(core)[given * QUARTER : (given + 1) * QUARTER]
    rows_ref[core] = field_ref[...]
    rows_ref[1 - core] = got_ref[...]
    spectrum = jnp.concatenate(
        [
            jnp.concatenate(
                [
                    rows_ref[number, block, pl.ds(plane, QUARTER, stride=PLANES), :]
                    for block in range(field_ref.shape[0])
                    for number in range(2)
                ],
                axis=0,
            )
            for plane in order
        ],
        axis=1,
    )
    hartree = from_right(
        stack_planes(from_left(cas_left_ref[...], spectrum)), cas_right_ref[...]
    )
    real_parts, imag_parts = [], []
    for number, plane in enumerate(order):
        cross = (
            hartree[number * ROWS : (number + 1) * ROWS] + xc_ref[plane] * density_ref[plane]
        )
        real_parts.append(
            adjoint_ref[0, 0, 0, plane] + step_time * cross * orbital_imag_ref[plane]
        )
        imag_parts.append(
            adjoint_ref[0, 0, 1, plane] - step_time * cross * orbital_real_ref[plane]
        )
    cosine, sine = cos_sin(
        0.5 * sub_time * jnp.concatenate([pot_ref[plane] for plane in order], axis=1)
    )
    begin_some(
        sign,
        jnp.concatenate(real_parts, axis=1),
        jnp.concatenate(imag_parts, axis=1),
        cosine,
        sine,
        whole_left(second_ref[...]),
        right_ref[...],
        out_ref,
    )


def stack_planes(value):
    planes = value.shape[1] // ROWS
    return jnp.concatenate([lane(value, plane) for plane in range(planes)], axis=0)


def density_kernel(own_ref, other_ref, left_ref, right_ref, density_ref, out_ref):
    density = natural(own_ref) + natural(other_ref)
    store_natural(density_ref, density)
    spectrum = from_right(stack_planes(from_left(left_ref[...], density)), right_ref[...])
    for plane in range(PLANES):
        for block in range(ROWS // PLANES):
            start = plane * ROWS + block * PLANES
            rows_to(out_ref, block, (), plane, spectrum[start : start + PLANES])


def coulomb_kernel(unit, placed, field_ref, left_ref, out_ref):
    blocks, lines = field_ref.shape[:2]
    core, chip = lax.axis_index("ka"), lax.axis_index("fft")
    if placed:
        first = (core * (blocks // 2) + chip % (blocks // 2)) * PLANES
    else:
        first = chip * PLANES + core * QUARTER
    places = [place_of(block, blocks) if placed else block for block in range(blocks)]
    rows = jnp.concatenate(
        [
            jnp.concatenate([field_ref[place, line] for place in places], axis=0)
            for line in range(lines)
        ],
        axis=1,
    )
    rows = from_left(left_ref[...], rows)

    def squared(index):
        number = unit * jnp.where(index < ROWS // 2, index, index - ROWS).astype(jnp.float32)
        return number * number

    along = squared(lax.broadcasted_iota(jnp.int32, (ROWS, ROWS), 0)) + squared(
        lax.broadcasted_iota(jnp.int32, (ROWS, ROWS), 1)
    )
    parts = []
    for line in range(lines):
        square = along + squared(jnp.full((1, ROWS), first + line, jnp.int32))
        nonzero = square > 0
        inverse = jnp.where(nonzero, 4.0 * math.pi / jnp.where(nonzero, square, 1.0), 0.0)
        parts.append(lane(rows, line) * inverse)
    rows = from_left(left_ref[...], jnp.concatenate(parts, axis=1))
    for line in range(lines):
        for block, place in enumerate(places):
            out_ref[place, line] = lane(rows, line)[block * PLANES : (block + 1) * PLANES]


def hartree_kernel(
    sign,
    field_ref,
    density_ref,
    xc_ref,
    orbital_real_ref,
    orbital_imag_ref,
    adjoint_real_ref,
    adjoint_imag_ref,
    cosine_ref,
    sine_ref,
    cas_left_ref,
    cas_right_ref,
    second_ref,
    right_ref,
    out_ref,
    cross_ref,
):
    spectrum = jnp.concatenate(
        [gathered(field_ref, pl.ds(plane, PLANES, stride=PLANES)) for plane in range(PLANES)],
        axis=1,
    )
    hartree = from_right(
        stack_planes(from_left(cas_left_ref[...], spectrum)), cas_right_ref[...]
    )
    real_parts, imag_parts = [], []
    for plane in range(PLANES):
        cross = hartree[plane * ROWS : (plane + 1) * ROWS] + xc_ref[plane] * density_ref[plane]
        cross_ref[plane] = cross
        real_parts.append(adjoint_real_ref[plane] + step_time * cross * orbital_imag_ref[plane])
        imag_parts.append(adjoint_imag_ref[plane] - step_time * cross * orbital_real_ref[plane])
    begin(
        sign,
        jnp.concatenate(real_parts, axis=1),
        jnp.concatenate(imag_parts, axis=1),
        natural(cosine_ref),
        natural(sine_ref),
        whole_left(second_ref[...]),
        right_ref[...],
        out_ref,
    )


def run(kernel, outputs, *operands, space=pltpu.VMEM, scratch=(), grant=24):
    arrays, views = [], []
    for operand in operands:
        array, index = operand if isinstance(operand, tuple) else (operand, None)
        known = [number for number, other in enumerate(arrays) if other is array]
        if not known:
            arrays.append(array)
        views.append((known[0] if known else len(arrays) - 1, index))

    def body(*refs):
        seen = [
            refs[number] if index is None else refs[number].at[index] for number, index in views
        ]
        kernel(*seen, *refs[len(arrays) :])

    made = pl.pallas_call(
        body,
        out_shape=[
            jax.ShapeDtypeStruct(out, jnp.float32) if isinstance(out, tuple) else out
            for out in outputs
        ],
        in_specs=[
            pl.BlockSpec(memory_space=pltpu.SMEM if array.size < ROWS else space)
            for array in arrays
        ],
        out_specs=[pl.BlockSpec(memory_space=pltpu.VMEM) for _ in outputs],
        scratch_shapes=list(scratch),
        compiler_params=pltpu.CompilerParams(vmem_limit_bytes=grant * 2**20),
    )(*arrays)
    return made[0] if len(outputs) == 1 else made


def grouped(
    orbitals, costate, potential, xc_kernel, vector_potential, kpoint_weight, occupation
):
    grid_size = potential.shape[1]
    blocks = lax.axis_size("fft")
    half = blocks // 2
    core = lax.axis_index("ka")
    fft_index = lax.axis_index("fft")
    side = fft_index // half
    place = core * half + fft_index % half
    lattice_unit = 2.0 * math.pi / (grid_size * spacing)

    groups = []
    for h in range(2):
        devices = [c * blocks + h * half + j for c in range(2) for j in range(half)]
        group = [0] * blocks
        for block, device in enumerate(devices):
            group[place_of(block, blocks)] = device
        groups.append(group)
    everyone = [0] * (2 * blocks)
    for number, source in enumerate(sources_of(blocks)):
        everyone[source] = number % 2 * blocks + number // 2
    regroup = []
    for c in range(2):
        for f in range(blocks):
            h, j = f // half, f % half
            regroup.append((c * blocks + f, h * blocks + c * half + j))
    across = [
        (c * blocks + f, c * blocks + (f + half) % blocks) for c in range(2) for f in range(blocks)
    ]

    def exchange(array):
        return lax.all_to_all(array, AXES, 0, 0, axis_index_groups=groups, tiled=True)

    def exchange_whole(array):
        return lax.all_to_all(array, "fft", 0, 0, tiled=True)

    def exchange_all(array):
        return lax.all_to_all(
            array, AXES, 0, 0, axis_index_groups=[everyone], tiled=True
        )

    def other_core(array):
        return lax.ppermute(array, "ka", [(0, 1), (1, 0)])

    def joined(keep, give):
        return run(join_kernel, [(2,) + keep.shape], keep, other_core(give))

    def to_halves(sent):
        return exchange_all(sent.reshape((2 * blocks,) + sent.shape[3:]))

    def from_halves(sent):
        field = exchange_all(sent).reshape(2, 2, half, 2, PLANES * QUARTER, ROWS)
        zero = np.uint32(0)
        give = lax.dynamic_slice(
            field, (zero, other, zero, zero, zero, zero), (2, 1) + field.shape[2:]
        )
        return field, other_core(give.reshape((2,) + field.shape[2:]))

    def move(array, pairs):
        return lax.ppermute(array, AXES, pairs)

    block_shape = (blocks, 2, PLANES, PLANES, ROWS)
    sent_shape = (blocks, 2, PLANES * PLANES, ROWS)
    natural_shape = (2, PLANES, ROWS, ROWS)
    real_shape = (PLANES, ROWS, ROWS)

    def swap_field(array):
        return exchange(array.reshape(block_shape))

    grid_line = np.arange(grid_size)
    angles = 2.0 * np.pi / grid_size * (np.outer(grid_line, grid_line) % grid_size)
    line_pair = jnp.asarray(
        np.concatenate([np.cos(angles), np.sin(angles)], axis=1).astype(np.float32)
    )
    cas = (np.cos(angles) + np.sin(angles)) / math.sqrt(grid_size)
    cas_left, cas_right = constant_table(cas, 1), constant_table(cas, 0)
    line_y = constant_circulant(0.25 * lattice_unit, grid_size)
    line_z = constant_circulant(-0.25 * lattice_unit, grid_size)
    tables_y = {1.0: constant_table(line_y[0][:ROWS], 1), -1.0: constant_table(line_y[1][:ROWS], 1)}
    right_z = {1.0: constant_table(line_z[1], 0), -1.0: constant_table(line_z[0], 0)}

    count_x = STEPS * SUB

    def start(given, parts):
        return run(
            functools.partial(start_kernel, given),
            [(2, half, parts, PLANES * QUARTER, ROWS)],
            orbitals,
            potential,
            tables_y[1.0],
            right_z[1.0],
            space=pltpu.HBM,
            grant=56,
            scratch=[
                pltpu.VMEM((2, QUARTER, ROWS, ROWS), jnp.float32),
                pltpu.VMEM((QUARTER, ROWS, ROWS), jnp.float32),
                pltpu.VMEM(tables_y[1.0].shape, jnp.bfloat16),
                pltpu.VMEM(right_z[1.0].shape, jnp.bfloat16),
                pltpu.SemaphoreType.DMA((4,)),
            ],
        )

    give = start(1, 2)
    sent = joined(start(0, 3), give)
    sent, other = lax.optimization_barrier((sent, (1 - core).astype(jnp.uint32)))
    field = to_halves(sent)

    def table_y(sign):
        return tables_y[sign]

    def tables_of(sign, count):
        if count % 2 == 0:
            return table_y(sign), table_y(sign), right_z[sign]
        pair = tables_x[sign][count // 2]
        return (pair, 0), (pair, 1), right_z[sign]

    def middle(sign, field, count):
        waves = waves_rows if count % 2 == 0 else waves_cols
        return run(
            functools.partial(mid_kernel, sign),
            [sent_shape],
            field,
            *waves,
            *tables_of(sign, count),
        )

    sent, *waves_cols = run(
        functools.partial(first_mid_kernel, 1.0, lattice_unit),
        [(blocks, 3) + sent_shape[2:], real_shape, real_shape],
        field,
        vector_potential,
        line_pair,
        right_z[1.0],
    )
    sent, *waves_rows = run(
        functools.partial(second_mid_kernel, 1.0),
        [sent_shape, real_shape, real_shape],
        exchange(sent.reshape(blocks, 3, PLANES, PLANES, ROWS)),
        table_y(1.0),
        table_y(1.0),
        right_z[1.0],
    )
    sent, push, xc_rows = lax.optimization_barrier((sent, vector_potential, xc_kernel))
    xc_rows = move(xc_rows, regroup)
    field = swap_field(sent)
    made = run(
        functools.partial(table_kernel, lattice_unit),
        [jax.ShapeDtypeStruct((2, ROWS, 4 * ROWS), jnp.bfloat16)] * (count_x - 1),
        push,
        line_pair,
    )
    field, xc_rows, made = lax.optimization_barrier((field, xc_rows, made))
    tables_x = {1.0: [None, *made[: count_x // 2 - 1]], -1.0: made[count_x // 2 - 1 :]}
    sent = middle(1.0, field, 3)
    kept = []
    all_shape = (2 * blocks, 2, PLANES * QUARTER, ROWS)
    for count in range(4, count_x - 1):
        field = swap_field(sent)
        if count % SUB == 0:
            sent, *orbital = run(
                functools.partial(step_kernel, 1.0),
                [sent_shape, real_shape, real_shape],
                field,
                *waves_rows,
                *tables_of(1.0, count),
            )
            kept.append(orbital)
        else:
            sent = middle(1.0, field, count)
    sent = run(
        functools.partial(last_mid_kernel, 1.0),
        [all_shape],
        swap_field(sent),
        *waves_cols,
        *tables_of(1.0, count_x - 1),
    )
    *orbital, partial = run(
        functools.partial(end_all_kernel, 1.0),
        [real_shape] * 3,
        *from_halves(sent),
        potential,
        table_y(1.0),
        costate,
        kpoint_weight,
        occupation,
    )

    density, sent = run(
        density_all_kernel,
        [real_shape, (blocks, QUARTER * PLANES, ROWS)],
        partial,
        other_core(partial),
        cas_left,
        cas_right,
        scratch=[pltpu.VMEM((blocks, PLANES * PLANES, ROWS), jnp.float32)],
    )
    field = exchange_whole(sent.reshape(blocks, QUARTER, PLANES, ROWS))
    sent = run(
        functools.partial(coulomb_kernel, lattice_unit, False),
        [(blocks, QUARTER, PLANES, ROWS)],
        field,
        cas_left,
    )
    field = exchange_whole(sent)
    field = field.reshape(blocks, QUARTER * PLANES, ROWS)
    got = other_core(field)

    def restart(given):
        return run(
            functools.partial(hartree_all_kernel, -1.0, given),
            [(2, half, 2, PLANES * QUARTER, ROWS)],
            field,
            got,
            density,
            xc_kernel,
            *orbital,
            costate,
            potential,
            cas_left,
            cas_right,
            table_y(-1.0),
            right_z[-1.0],
            scratch=[pltpu.VMEM((2, blocks, QUARTER * PLANES, ROWS), jnp.float32)],
        )

    give = restart(1)
    sent = run(
        functools.partial(all_mid_kernel, -1.0),
        [sent_shape],
        to_halves(joined(restart(0), give)),
        *waves_cols,
        *tables_of(-1.0, 1),
    )
    for step_index in range(STEPS - 1, -1, -1):
        first = (STEPS - 1 - step_index) * SUB
        if step_index < STEPS - 1:
            density, sent = run(
                density_kernel,
                [real_shape, (blocks, PLANES * PLANES, ROWS)],
                partial,
                move(partial, across),
                cas_left,
                cas_right,
            )
            field = exchange(sent.reshape(blocks, PLANES, PLANES, ROWS))
            sent = run(
                functools.partial(coulomb_kernel, lattice_unit, True),
                [(blocks, PLANES, PLANES, ROWS)],
                field,
                cas_left,
            )
            field = exchange(sent).reshape(blocks, PLANES * PLANES, ROWS)
            sent, cross = run(
                functools.partial(hartree_kernel, -1.0),
                [sent_shape, real_shape],
                field,
                density,
                xc_rows,
                *kept[step_index],
                *adjoint,
                *waves_rows,
                cas_left,
                cas_right,
                table_y(-1.0),
                right_z[-1.0],
            )
            sent = middle(-1.0, swap_field(sent), first + 1)
        field = swap_field(sent)
        sent = middle(-1.0, field, first + 2)
        field = swap_field(sent)
        if step_index > 0:
            sent = middle(-1.0, field, first + SUB - 1)
            *adjoint, partial = run(
                functools.partial(end_kernel, -1.0),
                [real_shape] * 3,
                swap_field(sent),
                *waves_rows,
                table_y(-1.0),
                *kept[step_index - 1],
                kpoint_weight,
                occupation,
            )
    sent = run(
        functools.partial(last_mid_kernel, -1.0),
        [all_shape],
        field,
        *waves_cols,
        *tables_of(-1.0, count_x - 1),
    )
    field, got = from_halves(sent)
    field, cross = lax.optimization_barrier((field, cross))
    return run(
        functools.partial(final_kernel, -1.0),
        [orbitals.shape, real_shape],
        field,
        got,
        potential,
        table_y(-1.0),
        cross,
        other_core(cross),
    )


def solution(mesh):
    placed = (
        P("ka", None, None, "fft", None, None),
        P("ka", None, None, "fft", None, None),
        P("fft", None, None),
        P("fft", None, None),
        P(),
        P(),
        P(),
    )

    def local(*arguments):
        orbitals, potential = arguments[0], arguments[2]
        fits = (
            mesh.shape["ka"] == 2
            and mesh.shape["fft"] % 2 == 0
            and orbitals.shape[:2] == (1, 1)
            and potential.shape == (PLANES, ROWS, ROWS)
        )
        return grouped(*arguments) if fits else plain(*arguments)

    return jax.shard_map(
        local,
        mesh=mesh,
        in_specs=placed,
        out_specs=(P("ka", None, None, "fft", None, None), P("fft", None, None)),
        check_vma=False,
    )
```

```python
import functools
import math

import jax
import jax.numpy as jnp
import numpy as np
from jax import lax
from jax.experimental import pallas as pl
from jax.experimental.pallas import tpu as pltpu
from jax.sharding import PartitionSpec as P

STEPS = 2
SUB = 4


spacing = 0.25
step_time = 0.6
sub_time = step_time / SUB
highest = lax.Precision.HIGHEST


def wave_numbers(grid_line, grid_size):
    signed_line = jnp.where(grid_line < grid_size // 2, grid_line, grid_line - grid_size)
    return 2.0 * math.pi / (grid_size * spacing) * signed_line.astype(jnp.float32)


def table_angles(grid_size):
    row_index = lax.broadcasted_iota(jnp.int32, (grid_size, grid_size), 0)
    col_index = lax.broadcasted_iota(jnp.int32, (grid_size, grid_size), 1)
    return 2.0 * math.pi / grid_size * (row_index * col_index % grid_size).astype(jnp.float32)


def line_matrices(shifts, grid_size):
    numbers = wave_numbers(lax.iota(jnp.int32, grid_size), grid_size)
    along = shifts[:, None] + numbers[None, :]
    phase = 0.5 * sub_time * (along * along)
    angles = table_angles(grid_size)
    cosine, sine = jnp.cos(angles), jnp.sin(angles)
    q_real, q_imag = jnp.cos(phase)[:, None, :], -jnp.sin(phase)[:, None, :]
    left_real = (cosine * q_real - sine * q_imag) / grid_size
    left_imag = (cosine * q_imag + sine * q_real) / grid_size
    both = jnp.stack([left_real, left_imag])
    by_cos = jnp.einsum("csam,mb->csab", both, cosine, precision=highest)
    by_sin = jnp.einsum("csam,mb->csab", both, sine, precision=highest)
    return by_cos[0] + by_sin[1], by_cos[1] - by_sin[0]


def real_form(real_part, imag_part):
    upper = jnp.stack([real_part, -imag_part], axis=-2)
    lower = jnp.stack([imag_part, real_part], axis=-2)
    return jnp.stack([upper, lower], axis=-4)


def spin(field, angle):
    cosine, sine = jnp.cos(angle), jnp.sin(angle)
    return jnp.stack(
        [field[0] * cosine + field[1] * sine, field[1] * cosine - field[0] * sine]
    )


def apply(form, matrix, field):
    return jnp.einsum(
        form, matrix, field, precision=lax.Precision.HIGHEST, preferred_element_type=jnp.float32
    )


def plain(orbitals, costate, potential, xc_kernel, vector_potential, kpoint_weight, occupation):
    grid_size = potential.shape[1]
    k_index = lax.axis_index("ka")
    fft_index = lax.axis_index("fft")
    planes = potential.shape[0]
    lattice_unit = 2.0 * math.pi / (grid_size * spacing)
    k_fraction = (k_index.astype(jnp.float32) + 0.5) / lax.axis_size("ka") - 0.5
    shifts = jnp.concatenate(
        [
            lattice_unit * k_fraction + vector_potential,
            jnp.array([lattice_unit * 0.25, -lattice_unit * 0.25], jnp.float32),
        ]
    )
    lines = real_form(*line_matrices(shifts, grid_size))
    back = jnp.transpose(lines, (0, 3, 4, 1, 2))

    def to_columns(field, split, concat):
        return lax.all_to_all(field, "fft", split_axis=split, concat_axis=concat, tiled=True)

    pot_rows = 0.5 * sub_time * potential
    pot_cols = to_columns(pot_rows, 1, 0)

    def propagate(field, step_index, sign):
        table = lines if sign > 0 else back
        order = range(SUB) if sign > 0 else range(SUB - 1, -1, -1)
        mat_y, mat_z = table[STEPS * SUB], table[STEPS * SUB + 1]
        in_rows = True
        field = spin(field, sign * pot_rows)
        for count, sub_index in enumerate(order):
            mat_x = table[step_index * SUB + sub_index]
            last = count == SUB - 1
            turn = sign * (1.0 if last else 2.0)
            field = apply("cadb,dkxyb->ckxya", mat_z, field)
            if in_rows:
                field = apply("cadb,dkxbz->ckxaz", mat_y, field)
                field = to_columns(field, 3, 2)
                field = apply("cadb,dkbyz->ckayz", mat_x, field)
                field = spin(field, turn * pot_cols)
            else:
                field = apply("cadb,dkbyz->ckayz", mat_x, field)
                field = to_columns(field, 2, 3)
                field = apply("cadb,dkxbz->ckxaz", mat_y, field)
                field = spin(field, turn * pot_rows)
            in_rows = not in_rows
        return field

    def parts_first(field):
        bands = field.shape[0] * field.shape[1]
        return jnp.moveaxis(field, 2, 0).reshape((2, bands) + field.shape[3:])

    angles = table_angles(grid_size)
    cas = (jnp.cos(angles) + jnp.sin(angles)) / math.sqrt(grid_size)
    numbers = wave_numbers(lax.iota(jnp.int32, grid_size), grid_size)
    numbers_local = wave_numbers(fft_index * planes + lax.iota(jnp.int32, planes), grid_size)
    g_squared = (
        (numbers * numbers)[:, None, None]
        + (numbers_local * numbers_local)[None, :, None]
        + (numbers * numbers)[None, None, :]
    )
    coulomb = jnp.where(
        g_squared > 0, 4.0 * math.pi / jnp.where(g_squared > 0, g_squared, 1.0), 0.0
    )
    orbital = parts_first(orbitals)
    history = [orbital]
    for step_index in range(STEPS):
        orbital = propagate(orbital, step_index, 1.0)
        history.append(orbital)
    occupied = occupation.astype(jnp.float32) / 100.0
    own_weight = lax.dynamic_slice_in_dim(kpoint_weight, k_index, 1)[0].astype(jnp.float32)
    weight = own_weight / jnp.sum(kpoint_weight).astype(jnp.float32)
    band_factor = 2.0 * weight * occupied
    adjoint = parts_first(costate)
    cross_pot = jnp.zeros_like(potential)
    for step_index in range(STEPS - 1, -1, -1):
        forward = history[step_index + 1]
        density = lax.psum(
            jnp.sum(band_factor[:, None, None, None] * jnp.sum(adjoint * forward, axis=0), axis=0),
            "ka",
        )
        hartree = apply("ab,xyb->xya", cas, density)
        hartree = apply("ab,xbz->xaz", cas, hartree)
        hartree = to_columns(hartree, 1, 0)
        hartree = apply("ab,byz->ayz", cas, hartree)
        hartree = apply("ab,byz->ayz", cas, hartree * coulomb)
        hartree = to_columns(hartree, 0, 1)
        hartree = apply("ab,xbz->xaz", cas, hartree)
        hartree = apply("ab,xyb->xya", cas, hartree)
        cross_pot = hartree + xc_kernel * density
        turned = jnp.stack([forward[1], -forward[0]])
        adjoint = propagate(adjoint + step_time * cross_pot * turned, step_index, -1.0)
    result = jnp.moveaxis(adjoint.reshape((2,) + orbitals.shape[:2] + adjoint.shape[2:]), 0, 2)
    return (result, cross_pot)


ROWS = 128
PLANES = 8
QUARTER = 4
AXES = ("ka", "fft")


def halves_of(value):
    high = value.astype(jnp.bfloat16)
    return high, (value - high.astype(jnp.float32)).astype(jnp.bfloat16)


def from_left(table, field):
    size = table.shape[1] // 2
    high, low = halves_of(field)
    return jnp.dot(
        jnp.concatenate([table[:, :size], table], axis=1),
        jnp.concatenate([high, low, high], axis=0),
        preferred_element_type=jnp.float32,
    )


def from_right(field, table):
    size = table.shape[0] // 2
    high, low = halves_of(field)
    return jnp.dot(
        jnp.concatenate([high, low, high], axis=1),
        jnp.concatenate([table[:size], table], axis=0),
        preferred_element_type=jnp.float32,
    )


def side_by_side(matrix, axis):
    return jnp.concatenate(halves_of(matrix), axis=axis)


def own_shift(count):
    side = lax.axis_index("fft") // (count // 2)
    return 0.5 * (jnp.full((ROWS, ROWS), side, jnp.int32).astype(jnp.float32) + 0.5) - 0.5


def circulant(shift, numbers, cosine, sine):
    along = shift + numbers
    phase = 0.5 * sub_time * (along * along)
    q_real, q_imag = jnp.cos(phase), -jnp.sin(phase)
    even = q_real * cosine + q_imag * sine
    odd = q_real * sine - q_imag * cosine
    spectrum = jnp.concatenate(
        [jnp.concatenate([even, odd], axis=1), jnp.concatenate([odd, -even], axis=1)], axis=0
    )
    upper = jnp.dot(
        jnp.concatenate([cosine, sine], axis=1),
        spectrum,
        precision=highest,
        preferred_element_type=jnp.float32,
    ) * (1.0 / ROWS)
    real_part, minus = upper[:, :ROWS], upper[:, ROWS:]
    real_turned, minus_turned = real_part.T, minus.T
    return upper, jnp.concatenate([real_turned, -minus_turned], axis=1)


def whole_matrix(upper):
    real_part, minus = upper[:, :ROWS], upper[:, ROWS:]
    return jnp.concatenate([upper, jnp.concatenate([-minus, real_part], axis=1)], axis=0)


def whole_left(table):
    return jnp.concatenate(
        [whole_matrix(table[:, : 2 * ROWS]), whole_matrix(table[:, 2 * ROWS :])], axis=1
    )


def table_kernel(unit, push_ref, lines_ref, *out_refs):
    numbers = wave_numbers(lax.broadcasted_iota(jnp.int32, (ROWS, ROWS), 0), ROWS)
    numbers = numbers + unit * own_shift(ROWS // PLANES)
    cosine, sine = lines_ref[:, :ROWS], lines_ref[:, ROWS:]
    pairs = (len(out_refs) + 1) // 2
    for line in range(2 * pairs):
        pair, which = divmod(line, 2)
        matrix, turned = circulant(push_ref[line], numbers, cosine, sine)
        if pair > 0:
            out_refs[pair - 1][which] = side_by_side(matrix, 1)
        out_refs[2 * pairs - 2 - pair][1 - which] = side_by_side(turned, 1)


def constant_circulant(shift, grid_size):
    grid_line = np.arange(grid_size)
    signed_line = np.where(grid_line < grid_size // 2, grid_line, grid_line - grid_size)
    along = shift + 2.0 * math.pi / (grid_size * spacing) * signed_line
    waves = np.exp(2j * np.pi / grid_size * (np.outer(grid_line, grid_line) % grid_size))
    line = (waves * np.exp(-0.5j * sub_time * along * along)) @ waves.conj() / grid_size
    whole = np.block([[line.real, -line.imag], [line.imag, line.real]])
    return whole, whole.T


def constant_table(matrix, axis):
    high = matrix.astype(jnp.bfloat16)
    low = (matrix - high.astype(np.float64)).astype(jnp.bfloat16)
    return jnp.asarray(np.concatenate([high, low], axis=axis))


def cos_sin(angle):
    square = angle * angle
    cosine = sine = 1.0
    for order in range(10, 0, -2):
        cosine = 1.0 - cosine * (square * (1.0 / (order * (order - 1))))
        sine = 1.0 - sine * (square * (1.0 / (order * (order + 1))))
    return cosine, sine * angle


def rotated(sign, real_part, imag_part, cosine, sine):
    if sign > 0:
        return real_part * cosine + imag_part * sine, imag_part * cosine - real_part * sine
    return real_part * cosine - imag_part * sine, imag_part * cosine + real_part * sine


def doubled(cosine, sine):
    return 1.0 - 2.0 * (sine * sine), 2.0 * sine * cosine


def place_of(block, blocks):
    core, rest = divmod(block, blocks // 2)
    return rest // 2 * 4 + core * 2 + rest % 2


def gathered(ref, *index):
    blocks = ref.shape[0]
    return jnp.concatenate(
        [ref[(place_of(block, blocks),) + index] for block in range(blocks)], axis=0
    )


def gather_planes(ref):
    return jnp.concatenate(
        [
            jnp.concatenate([gathered(ref, part, plane) for plane in range(PLANES)], axis=1)
            for part in range(2)
        ],
        axis=0,
    )


def natural(ref):
    return jnp.concatenate([ref[plane] for plane in range(PLANES)], axis=1)


def lane(value, plane):
    return value[:, plane * ROWS : (plane + 1) * ROWS]


def core_place(block, blocks):
    core, chip = divmod(block, blocks // 2)
    bits = (blocks // 2).bit_length() - 1
    return core, sum((chip >> bit & 1) << (bits - 1 - bit) for bit in range(bits))


def sources_of(blocks):
    half = blocks // 2
    return [
        (core * 2 + block // half) * half + core_place(block % half, blocks)[1]
        for block in range(blocks)
        for core in range(2)
    ]


def rows_to(out_ref, block, index, plane, piece):
    if not isinstance(out_ref, tuple):
        place = place_of(block, out_ref.shape[0])
        out_ref[(place,) + index + (pl.ds(plane, PLANES, stride=PLANES), slice(None))] = piece
        return
    sources = sources_of(out_ref[0].shape[0] // 2)
    for core in range(2):
        at = (sources[2 * block + core],) + index
        out_ref[0][at + (pl.ds(plane, QUARTER, stride=PLANES), slice(None))] = piece[
            core * QUARTER : (core + 1) * QUARTER
        ]


def turn_z(real_part, imag_part, table):
    rows = jnp.concatenate(
        [
            jnp.concatenate([lane(real_part, plane), lane(imag_part, plane)], axis=1)
            for plane in range(real_part.shape[1] // ROWS)
        ],
        axis=0,
    )
    return from_right(rows, table)


def scatter_planes(real_part, imag_part, table, out_ref):
    blocks = ROWS // PLANES
    turned = turn_z(real_part, imag_part, table)
    for plane in range(PLANES):
        for part in range(2):
            piece = turned[plane * ROWS : (plane + 1) * ROWS, part * ROWS : (part + 1) * ROWS]
            for block in range(blocks):
                rows_of = piece[block * PLANES : (block + 1) * PLANES]
                rows_to(out_ref, block, (part,), plane, rows_of)


def between(sign, field, cosine, sine, first, second, right, out_ref):
    field = from_left(whole_left(first), field)
    real_part, imag_part = rotated(sign, field[:ROWS], field[ROWS:], *doubled(cosine, sine))
    field = from_left(
        whole_left(second), jnp.concatenate([real_part, imag_part], axis=0)
    )
    scatter_planes(field[:ROWS], field[ROWS:], right, out_ref)


def mid_kernel(
    sign, field_ref, cosine_ref, sine_ref, first_ref, second_ref, right_ref, out_ref
):
    cosine, sine = natural(cosine_ref), natural(sine_ref)
    field = gather_planes(field_ref)
    between(
        sign, field, cosine, sine, first_ref[...], second_ref[...], right_ref[...], out_ref
    )


def gather_all(field_ref, part):
    return jnp.concatenate(
        [
            jnp.concatenate(
                [
                    field_ref[source, part, pl.ds(plane * QUARTER, QUARTER), :]
                    for source in sources_of(field_ref.shape[0] // 2)
                ],
                axis=0,
            )
            for plane in range(PLANES)
        ],
        axis=1,
    )


def first_mid_kernel(
    sign, unit, field_ref, push_ref, lines_ref, right_ref, out_ref, cosine_ref, sine_ref
):
    numbers = wave_numbers(lax.broadcasted_iota(jnp.int32, (ROWS, ROWS), 0), ROWS)
    numbers = numbers + unit * own_shift(ROWS // PLANES)
    first, second = (
        side_by_side(
            circulant(push_ref[line], numbers, lines_ref[:, :ROWS], lines_ref[:, ROWS:])[0], 1
        )
        for line in range(2)
    )
    pot = gather_all(field_ref, 2)
    for plane in range(PLANES):
        for block in range(ROWS // PLANES):
            rows_of = lane(pot, plane)[block * PLANES : (block + 1) * PLANES]
            rows_to(out_ref, block, (2,), plane, rows_of)
    cosine, sine = cos_sin(0.5 * sub_time * pot)
    store_natural(cosine_ref, cosine)
    store_natural(sine_ref, sine)
    field = jnp.concatenate([gather_all(field_ref, 0), gather_all(field_ref, 1)], axis=0)
    between(sign, field, cosine, sine, first, second, right_ref[...], out_ref)


def all_mid_kernel(
    sign, field_ref, cosine_ref, sine_ref, first_ref, second_ref, right_ref, out_ref
):
    cosine, sine = natural(cosine_ref), natural(sine_ref)
    field = jnp.concatenate([gather_all(field_ref, 0), gather_all(field_ref, 1)], axis=0)
    between(
        sign, field, cosine, sine, first_ref[...], second_ref[...], right_ref[...], out_ref
    )


def second_mid_kernel(
    sign, field_ref, first_ref, second_ref, right_ref, out_ref, cosine_ref, sine_ref
):
    pot = jnp.concatenate([gathered(field_ref, 2, plane) for plane in range(PLANES)], axis=1)
    cosine, sine = cos_sin(0.5 * sub_time * pot)
    store_natural(cosine_ref, cosine)
    store_natural(sine_ref, sine)
    field = gather_planes(field_ref)
    between(
        sign, field, cosine, sine, first_ref[...], second_ref[...], right_ref[...], out_ref
    )


def last_mid_kernel(
    sign, field_ref, cosine_ref, sine_ref, first_ref, second_ref, right_ref, out_ref
):
    cosine, sine = natural(cosine_ref), natural(sine_ref)
    field = gather_planes(field_ref)
    between(
        sign, field, cosine, sine, first_ref[...], second_ref[...], right_ref[...], (out_ref,)
    )


def store_natural(ref, value):
    for plane in range(PLANES):
        ref[plane] = lane(value, plane)


def density_factor(weight_ref, occupation_ref, k_index):
    def row(value):
        return jnp.full((1, ROWS), value, jnp.int32).astype(jnp.float32)

    total = row(weight_ref[0] + weight_ref[1])
    return 2.0 * (row(weight_ref[k_index]) / total) * (row(occupation_ref[0]) / 100.0)


def finish(sign, field_ref, cosine, sine, first_ref, real_ref, imag_ref):
    field = from_left(whole_left(first_ref[...]), gather_planes(field_ref))
    real_part, imag_part = rotated(sign, field[:ROWS], field[ROWS:], cosine, sine)
    store_natural(real_ref, real_part)
    store_natural(imag_ref, imag_part)
    return real_part, imag_part


def begin(sign, real_part, imag_part, cosine, sine, second, right, out_ref):
    real_part, imag_part = rotated(sign, real_part, imag_part, cosine, sine)
    field = from_left(second, jnp.concatenate([real_part, imag_part], axis=0))
    scatter_planes(field[:ROWS], field[ROWS:], right, out_ref)


def step_kernel(
    sign,
    field_ref,
    cosine_ref,
    sine_ref,
    first_ref,
    second_ref,
    right_ref,
    out_ref,
    real_ref,
    imag_ref,
):
    cosine, sine = natural(cosine_ref), natural(sine_ref)
    parts = finish(sign, field_ref, cosine, sine, first_ref, real_ref, imag_ref)
    begin(sign, *parts, cosine, sine, whole_left(second_ref[...]), right_ref[...], out_ref)


def plane_order(core):
    return [core * QUARTER + number for number in range(QUARTER)] + [
        (1 - core) * QUARTER + number for number in range(QUARTER)
    ]


def begin_some(sign, real_part, imag_part, cosine, sine, second, right, out_ref):
    real_part, imag_part = rotated(sign, real_part, imag_part, cosine, sine)
    field = from_left(second, jnp.concatenate([real_part, imag_part], axis=0))
    turned = turn_z(field[:ROWS], field[ROWS:], right)
    for number in range(QUARTER):
        for part in range(2):
            piece = turned[number * ROWS : (number + 1) * ROWS, part * ROWS : (part + 1) * ROWS]
            put_rows(out_ref, (part,), number, piece)


def put_rows(ref, index, number, piece):
    blocks = ROWS // PLANES
    for block in range(blocks):
        at = core_place(block, blocks) + index
        ref[at + (pl.ds(number, PLANES, stride=QUARTER), slice(None))] = piece[
            block * PLANES : (block + 1) * PLANES
        ]


def start_kernel(
    given, field_ref, pot_ref, second_ref, right_ref, out_ref, field, pot, second, right, sems
):
    start = plane_order(lax.axis_index("ka"))[given * QUARTER]
    copies = [
        pltpu.make_async_copy(source, target, sems.at[number])
        for number, (source, target) in enumerate(
            (
                (pot_ref.at[pl.ds(start, QUARTER)], pot),
                (field_ref.at[0, 0, :, pl.ds(start, QUARTER)], field),
                (second_ref, second),
                (right_ref, right),
            )
        )
    ]
    for copy in copies:
        copy.start()
    copies[0].wait()
    if out_ref.shape[2] > 2:
        for number in range(QUARTER):
            put_rows(out_ref, (2,), number, pot[number])
    planes = range(QUARTER)
    cosine, sine = cos_sin(
        0.5 * sub_time * jnp.concatenate([pot[plane] for plane in planes], axis=1)
    )
    for copy in copies[1:]:
        copy.wait()
    begin_some(
        1.0,
        jnp.concatenate([field[0, plane] for plane in planes], axis=1),
        jnp.concatenate([field[1, plane] for plane in planes], axis=1),
        cosine,
        sine,
        whole_left(second[...]),
        right[...],
        out_ref,
    )


def join_kernel(keep_ref, got_ref, out_ref):
    core = lax.axis_index("ka")
    parts = got_ref.shape[2]
    for to in range(2):
        out_ref[to, core] = keep_ref[to]
        out_ref[to, 1 - core, :, 0:parts] = got_ref[to]
        if keep_ref.shape[2] > parts:
            out_ref[to, 1 - core, :, parts] = keep_ref[to, :, parts]


def end_kernel(
    sign,
    field_ref,
    cosine_ref,
    sine_ref,
    first_ref,
    other_real_ref,
    other_imag_ref,
    weight_ref,
    occupation_ref,
    real_ref,
    imag_ref,
    density_ref,
):
    cosine, sine = natural(cosine_ref), natural(sine_ref)
    real_part, imag_part = finish(
        sign, field_ref, cosine, sine, first_ref, real_ref, imag_ref
    )
    side = lax.axis_index("fft") // (field_ref.shape[0] // 2)
    factor = density_factor(weight_ref, occupation_ref, side)
    for plane in range(PLANES):
        density_ref[plane] = factor * (
            lane(real_part, plane) * other_real_ref[plane]
            + lane(imag_part, plane) * other_imag_ref[plane]
        )


def finish_all(sign, field_ref, got_ref, pot_ref, first_ref):
    core = lax.axis_index("ka")
    order = plane_order(core)
    blocks = ROWS // PLANES

    def part_of(part):
        planes = []
        for number in range(PLANES):
            at = (part, pl.ds(number % QUARTER * PLANES, PLANES), slice(None))
            rows = [
                field_ref[(to, core, chip) + at] if number < QUARTER else got_ref[(to, chip) + at]
                for to, chip in (core_place(block, blocks) for block in range(blocks))
            ]
            planes.append(jnp.concatenate(rows, axis=0))
        return jnp.concatenate(planes, axis=1)

    cosine, sine = cos_sin(
        0.5 * sub_time * jnp.concatenate([pot_ref[plane] for plane in order], axis=1)
    )
    field = from_left(
        whole_left(first_ref[...]), jnp.concatenate([part_of(0), part_of(1)], axis=0)
    )
    return order, rotated(sign, field[:ROWS], field[ROWS:], cosine, sine)


def final_kernel(
    sign,
    field_ref,
    got_ref,
    pot_ref,
    first_ref,
    cross_ref,
    beside_ref,
    out_ref,
    cross_out_ref,
):
    blocks = ROWS // PLANES
    here = lax.axis_index("ka") == lax.axis_index("fft") // (blocks // 2)
    for plane in range(PLANES):
        cross_out_ref[plane] = jnp.where(here, cross_ref[plane], beside_ref[plane])
    order, (real_part, imag_part) = finish_all(sign, field_ref, got_ref, pot_ref, first_ref)
    for number, plane in enumerate(order):
        out_ref[0, 0, 0, plane] = lane(real_part, number)
        out_ref[0, 0, 1, plane] = lane(imag_part, number)


def end_all_kernel(
    sign,
    field_ref,
    got_ref,
    pot_ref,
    first_ref,
    other_ref,
    weight_ref,
    occupation_ref,
    real_ref,
    imag_ref,
    density_ref,
):
    order, (real_part, imag_part) = finish_all(sign, field_ref, got_ref, pot_ref, first_ref)
    factor = density_factor(weight_ref, occupation_ref, lax.axis_index("ka"))
    for number, plane in enumerate(order):
        real_ref[plane] = lane(real_part, number)
        imag_ref[plane] = lane(imag_part, number)
        density_ref[plane] = factor * (
            lane(real_part, number) * other_ref[0, 0, 0, plane]
            + lane(imag_part, number) * other_ref[0, 0, 1, plane]
        )


def density_all_kernel(
    own_ref, other_ref, left_ref, right_ref, density_ref, out_ref, whole_ref
):
    density = natural(own_ref) + natural(other_ref)
    store_natural(density_ref, density)
    spectrum = from_right(stack_planes(from_left(left_ref[...], density)), right_ref[...])
    for plane in range(PLANES):
        for block in range(ROWS // PLANES):
            start = plane * ROWS + block * PLANES
            whole_ref[block, pl.ds(plane, PLANES, stride=PLANES), :] = spectrum[
                start : start + PLANES
            ]
    size = QUARTER * PLANES
    start = pl.multiple_of(lax.axis_index("ka") * size, size)
    out_ref[...] = whole_ref[:, pl.ds(start, size), :]


def hartree_all_kernel(
    sign,
    given,
    field_ref,
    got_ref,
    density_ref,
    xc_ref,
    orbital_real_ref,
    orbital_imag_ref,
    adjoint_ref,
    pot_ref,
    cas_left_ref,
    cas_right_ref,
    second_ref,
    right_ref,
    out_ref,
    rows_ref,
):
    core = lax.axis_index("ka")
    order = plane_order(core)[given * QUARTER : (given + 1) * QUARTER]
    rows_ref[core] = field_ref[...]
    rows_ref[1 - core] = got_ref[...]

    def rows_of(plane):
        return jnp.concatenate(
            [
                rows_ref[number, block, pl.ds(plane, QUARTER, stride=PLANES), :]
                for block in range(field_ref.shape[0])
                for number in range(2)
            ],
            axis=0,
        )

    spectrum = jnp.concatenate(
        [
            jnp.where(core == given, rows_of(number), rows_of(QUARTER + number))
            for number in range(QUARTER)
        ],
        axis=1,
    )
    hartree = from_right(
        stack_planes(from_left(cas_left_ref[...], spectrum)), cas_right_ref[...]
    )
    real_parts, imag_parts = [], []
    for number, plane in enumerate(order):
        cross = (
            hartree[number * ROWS : (number + 1) * ROWS] + xc_ref[plane] * density_ref[plane]
        )
        real_parts.append(
            adjoint_ref[0, 0, 0, plane] + step_time * cross * orbital_imag_ref[plane]
        )
        imag_parts.append(
            adjoint_ref[0, 0, 1, plane] - step_time * cross * orbital_real_ref[plane]
        )
    cosine, sine = cos_sin(
        0.5 * sub_time * jnp.concatenate([pot_ref[plane] for plane in order], axis=1)
    )
    begin_some(
        sign,
        jnp.concatenate(real_parts, axis=1),
        jnp.concatenate(imag_parts, axis=1),
        cosine,
        sine,
        whole_left(second_ref[...]),
        right_ref[...],
        out_ref,
    )


def stack_planes(value):
    planes = value.shape[1] // ROWS
    return jnp.concatenate([lane(value, plane) for plane in range(planes)], axis=0)


def density_kernel(own_ref, other_ref, left_ref, right_ref, density_ref, out_ref):
    density = natural(own_ref) + natural(other_ref)
    store_natural(density_ref, density)
    spectrum = from_right(stack_planes(from_left(left_ref[...], density)), right_ref[...])
    for plane in range(PLANES):
        for block in range(ROWS // PLANES):
            start = plane * ROWS + block * PLANES
            rows_to(out_ref, block, (), plane, spectrum[start : start + PLANES])


def coulomb_kernel(unit, placed, field_ref, left_ref, out_ref):
    blocks, lines = field_ref.shape[:2]
    core, chip = lax.axis_index("ka"), lax.axis_index("fft")
    if placed:
        first = (core * (blocks // 2) + chip % (blocks // 2)) * PLANES
    else:
        first = chip * PLANES + core * QUARTER
    places = [place_of(block, blocks) if placed else block for block in range(blocks)]
    rows = jnp.concatenate(
        [
            jnp.concatenate([field_ref[place, line] for place in places], axis=0)
            for line in range(lines)
        ],
        axis=1,
    )
    rows = from_left(left_ref[...], rows)

    def squared(index):
        number = unit * jnp.where(index < ROWS // 2, index, index - ROWS).astype(jnp.float32)
        return number * number

    along = squared(lax.broadcasted_iota(jnp.int32, (ROWS, ROWS), 0)) + squared(
        lax.broadcasted_iota(jnp.int32, (ROWS, ROWS), 1)
    )
    parts = []
    for line in range(lines):
        square = along + squared(jnp.full((1, ROWS), first + line, jnp.int32))
        nonzero = square > 0
        inverse = jnp.where(nonzero, 4.0 * math.pi / jnp.where(nonzero, square, 1.0), 0.0)
        parts.append(lane(rows, line) * inverse)
    rows = from_left(left_ref[...], jnp.concatenate(parts, axis=1))
    for line in range(lines):
        for block, place in enumerate(places):
            out_ref[place, line] = lane(rows, line)[block * PLANES : (block + 1) * PLANES]


def hartree_kernel(
    sign,
    field_ref,
    density_ref,
    xc_ref,
    orbital_real_ref,
    orbital_imag_ref,
    adjoint_real_ref,
    adjoint_imag_ref,
    cosine_ref,
    sine_ref,
    cas_left_ref,
    cas_right_ref,
    second_ref,
    right_ref,
    out_ref,
    cross_ref,
):
    spectrum = jnp.concatenate(
        [gathered(field_ref, pl.ds(plane, PLANES, stride=PLANES)) for plane in range(PLANES)],
        axis=1,
    )
    hartree = from_right(
        stack_planes(from_left(cas_left_ref[...], spectrum)), cas_right_ref[...]
    )
    real_parts, imag_parts = [], []
    for plane in range(PLANES):
        cross = hartree[plane * ROWS : (plane + 1) * ROWS] + xc_ref[plane] * density_ref[plane]
        cross_ref[plane] = cross
        real_parts.append(adjoint_real_ref[plane] + step_time * cross * orbital_imag_ref[plane])
        imag_parts.append(adjoint_imag_ref[plane] - step_time * cross * orbital_real_ref[plane])
    begin(
        sign,
        jnp.concatenate(real_parts, axis=1),
        jnp.concatenate(imag_parts, axis=1),
        natural(cosine_ref),
        natural(sine_ref),
        whole_left(second_ref[...]),
        right_ref[...],
        out_ref,
    )


def run(kernel, outputs, *operands, space=pltpu.VMEM, scratch=(), grant=24):
    arrays, views = [], []
    for operand in operands:
        array, index = operand if isinstance(operand, tuple) else (operand, None)
        known = [number for number, other in enumerate(arrays) if other is array]
        if not known:
            arrays.append(array)
        views.append((known[0] if known else len(arrays) - 1, index))

    def body(*refs):
        seen = [
            refs[number] if index is None else refs[number].at[index] for number, index in views
        ]
        kernel(*seen, *refs[len(arrays) :])

    made = pl.pallas_call(
        body,
        out_shape=[
            jax.ShapeDtypeStruct(out, jnp.float32) if isinstance(out, tuple) else out
            for out in outputs
        ],
        in_specs=[
            pl.BlockSpec(memory_space=pltpu.SMEM if array.size < ROWS else space)
            for array in arrays
        ],
        out_specs=[pl.BlockSpec(memory_space=pltpu.VMEM) for _ in outputs],
        scratch_shapes=list(scratch),
        compiler_params=pltpu.CompilerParams(vmem_limit_bytes=grant * 2**20),
    )(*arrays)
    return made[0] if len(outputs) == 1 else made


def grouped(
    orbitals, costate, potential, xc_kernel, vector_potential, kpoint_weight, occupation
):
    grid_size = potential.shape[1]
    blocks = lax.axis_size("fft")
    half = blocks // 2
    core = lax.axis_index("ka")
    fft_index = lax.axis_index("fft")
    side = fft_index // half
    place = core * half + fft_index % half
    lattice_unit = 2.0 * math.pi / (grid_size * spacing)

    groups = []
    for h in range(2):
        devices = [c * blocks + h * half + j for c in range(2) for j in range(half)]
        group = [0] * blocks
        for block, device in enumerate(devices):
            group[place_of(block, blocks)] = device
        groups.append(group)
    everyone = [0] * (2 * blocks)
    for number, source in enumerate(sources_of(blocks)):
        everyone[source] = number % 2 * blocks + number // 2
    regroup = []
    for c in range(2):
        for f in range(blocks):
            h, j = f // half, f % half
            regroup.append((c * blocks + f, h * blocks + c * half + j))
    across = [
        (c * blocks + f, c * blocks + (f + half) % blocks) for c in range(2) for f in range(blocks)
    ]

    def exchange(array):
        return lax.all_to_all(array, AXES, 0, 0, axis_index_groups=groups, tiled=True)

    def exchange_whole(array):
        return lax.all_to_all(array, "fft", 0, 0, tiled=True)

    def exchange_all(array):
        return lax.all_to_all(
            array, AXES, 0, 0, axis_index_groups=[everyone], tiled=True
        )

    def other_core(array):
        return lax.ppermute(array, "ka", [(0, 1), (1, 0)])

    def joined(keep, give):
        return run(join_kernel, [(2,) + keep.shape], keep, other_core(give))

    def to_halves(sent):
        return exchange_all(sent.reshape((2 * blocks,) + sent.shape[3:]))

    def from_halves(sent):
        field = exchange_all(sent).reshape(2, 2, half, 2, PLANES * QUARTER, ROWS)
        zero = np.uint32(0)
        give = lax.dynamic_slice(
            field, (zero, other, zero, zero, zero, zero), (2, 1) + field.shape[2:]
        )
        return field, other_core(give.reshape((2,) + field.shape[2:]))

    def move(array, pairs):
        return lax.ppermute(array, AXES, pairs)

    block_shape = (blocks, 2, PLANES, PLANES, ROWS)
    sent_shape = (blocks, 2, PLANES * PLANES, ROWS)
    natural_shape = (2, PLANES, ROWS, ROWS)
    real_shape = (PLANES, ROWS, ROWS)

    def swap_field(array):
        return exchange(array.reshape(block_shape))

    grid_line = np.arange(grid_size)
    angles = 2.0 * np.pi / grid_size * (np.outer(grid_line, grid_line) % grid_size)
    line_pair = jnp.asarray(
        np.concatenate([np.cos(angles), np.sin(angles)], axis=1).astype(np.float32)
    )
    cas = (np.cos(angles) + np.sin(angles)) / math.sqrt(grid_size)
    cas_left, cas_right = constant_table(cas, 1), constant_table(cas, 0)
    line_y = constant_circulant(0.25 * lattice_unit, grid_size)
    line_z = constant_circulant(-0.25 * lattice_unit, grid_size)
    tables_y = {1.0: constant_table(line_y[0][:ROWS], 1), -1.0: constant_table(line_y[1][:ROWS], 1)}
    right_z = {1.0: constant_table(line_z[1], 0), -1.0: constant_table(line_z[0], 0)}

    count_x = STEPS * SUB

    def start(given, parts):
        return run(
            functools.partial(start_kernel, given),
            [(2, half, parts, PLANES * QUARTER, ROWS)],
            orbitals,
            potential,
            tables_y[1.0],
            right_z[1.0],
            space=pltpu.HBM,
            grant=56,
            scratch=[
                pltpu.VMEM((2, QUARTER, ROWS, ROWS), jnp.float32),
                pltpu.VMEM((QUARTER, ROWS, ROWS), jnp.float32),
                pltpu.VMEM(tables_y[1.0].shape, jnp.bfloat16),
                pltpu.VMEM(right_z[1.0].shape, jnp.bfloat16),
                pltpu.SemaphoreType.DMA((4,)),
            ],
        )

    give = start(1, 2)
    sent = joined(start(0, 3), give)
    sent, other = lax.optimization_barrier((sent, (1 - core).astype(jnp.uint32)))
    field = to_halves(sent)

    def table_y(sign):
        return tables_y[sign]

    def tables_of(sign, count):
        if count % 2 == 0:
            return table_y(sign), table_y(sign), right_z[sign]
        pair = tables_x[sign][count // 2]
        return (pair, 0), (pair, 1), right_z[sign]

    def middle(sign, field, count):
        waves = waves_rows if count % 2 == 0 else waves_cols
        return run(
            functools.partial(mid_kernel, sign),
            [sent_shape],
            field,
            *waves,
            *tables_of(sign, count),
        )

    sent, *waves_cols = run(
        functools.partial(first_mid_kernel, 1.0, lattice_unit),
        [(blocks, 3) + sent_shape[2:], real_shape, real_shape],
        field,
        vector_potential,
        line_pair,
        right_z[1.0],
    )
    sent, *waves_rows = run(
        functools.partial(second_mid_kernel, 1.0),
        [sent_shape, real_shape, real_shape],
        exchange(sent.reshape(blocks, 3, PLANES, PLANES, ROWS)),
        table_y(1.0),
        table_y(1.0),
        right_z[1.0],
    )
    sent, push, xc_rows = lax.optimization_barrier((sent, vector_potential, xc_kernel))
    xc_rows = move(xc_rows, regroup)
    field = swap_field(sent)
    made = run(
        functools.partial(table_kernel, lattice_unit),
        [jax.ShapeDtypeStruct((2, ROWS, 4 * ROWS), jnp.bfloat16)] * (count_x - 1),
        push,
        line_pair,
    )
    field, xc_rows, made = lax.optimization_barrier((field, xc_rows, made))
    tables_x = {1.0: [None, *made[: count_x // 2 - 1]], -1.0: made[count_x // 2 - 1 :]}
    sent = middle(1.0, field, 3)
    kept = []
    all_shape = (2 * blocks, 2, PLANES * QUARTER, ROWS)
    for count in range(4, count_x - 1):
        field = swap_field(sent)
        if count % SUB == 0:
            sent, *orbital = run(
                functools.partial(step_kernel, 1.0),
                [sent_shape, real_shape, real_shape],
                field,
                *waves_rows,
                *tables_of(1.0, count),
            )
            kept.append(orbital)
        else:
            sent = middle(1.0, field, count)
    sent = run(
        functools.partial(last_mid_kernel, 1.0),
        [all_shape],
        swap_field(sent),
        *waves_cols,
        *tables_of(1.0, count_x - 1),
    )
    *orbital, partial = run(
        functools.partial(end_all_kernel, 1.0),
        [real_shape] * 3,
        *from_halves(sent),
        potential,
        table_y(1.0),
        costate,
        kpoint_weight,
        occupation,
    )

    density, sent = run(
        density_all_kernel,
        [real_shape, (blocks, QUARTER * PLANES, ROWS)],
        partial,
        other_core(partial),
        cas_left,
        cas_right,
        scratch=[pltpu.VMEM((blocks, PLANES * PLANES, ROWS), jnp.float32)],
    )
    field = exchange_whole(sent.reshape(blocks, QUARTER, PLANES, ROWS))
    sent = run(
        functools.partial(coulomb_kernel, lattice_unit, False),
        [(blocks, QUARTER, PLANES, ROWS)],
        field,
        cas_left,
    )
    field = exchange_whole(sent)
    field = field.reshape(blocks, QUARTER * PLANES, ROWS)
    got = other_core(field)

    def restart(given):
        return run(
            functools.partial(hartree_all_kernel, -1.0, given),
            [(2, half, 2, PLANES * QUARTER, ROWS)],
            field,
            got,
            density,
            xc_kernel,
            *orbital,
            costate,
            potential,
            cas_left,
            cas_right,
            table_y(-1.0),
            right_z[-1.0],
            scratch=[pltpu.VMEM((2, blocks, QUARTER * PLANES, ROWS), jnp.float32)],
        )

    give = restart(1)
    sent = run(
        functools.partial(all_mid_kernel, -1.0),
        [sent_shape],
        to_halves(joined(restart(0), give)),
        *waves_cols,
        *tables_of(-1.0, 1),
    )
    for step_index in range(STEPS - 1, -1, -1):
        first = (STEPS - 1 - step_index) * SUB
        if step_index < STEPS - 1:
            density, sent = run(
                density_kernel,
                [real_shape, (blocks, PLANES * PLANES, ROWS)],
                partial,
                move(partial, across),
                cas_left,
                cas_right,
            )
            field = exchange(sent.reshape(blocks, PLANES, PLANES, ROWS))
            sent = run(
                functools.partial(coulomb_kernel, lattice_unit, True),
                [(blocks, PLANES, PLANES, ROWS)],
                field,
                cas_left,
            )
            field = exchange(sent).reshape(blocks, PLANES * PLANES, ROWS)
            sent, cross = run(
                functools.partial(hartree_kernel, -1.0),
                [sent_shape, real_shape],
                field,
                density,
                xc_rows,
                *kept[step_index],
                *adjoint,
                *waves_rows,
                cas_left,
                cas_right,
                table_y(-1.0),
                right_z[-1.0],
            )
            sent = middle(-1.0, swap_field(sent), first + 1)
        field = swap_field(sent)
        sent = middle(-1.0, field, first + 2)
        field = swap_field(sent)
        if step_index > 0:
            sent = middle(-1.0, field, first + SUB - 1)
            *adjoint, partial = run(
                functools.partial(end_kernel, -1.0),
                [real_shape] * 3,
                swap_field(sent),
                *waves_rows,
                table_y(-1.0),
                *kept[step_index - 1],
                kpoint_weight,
                occupation,
            )
    sent = run(
        functools.partial(last_mid_kernel, -1.0),
        [all_shape],
        field,
        *waves_cols,
        *tables_of(-1.0, count_x - 1),
    )
    field, got = from_halves(sent)
    field, cross = lax.optimization_barrier((field, cross))
    return run(
        functools.partial(final_kernel, -1.0),
        [orbitals.shape, real_shape],
        field,
        got,
        potential,
        table_y(-1.0),
        cross,
        other_core(cross),
    )


def solution(mesh):
    placed = (
        P("ka", None, None, "fft", None, None),
        P("ka", None, None, "fft", None, None),
        P("fft", None, None),
        P("fft", None, None),
        P(),
        P(),
        P(),
    )

    def local(*arguments):
        orbitals, potential = arguments[0], arguments[2]
        fits = (
            mesh.shape["ka"] == 2
            and mesh.shape["fft"] % 2 == 0
            and orbitals.shape[:2] == (1, 1)
            and potential.shape == (PLANES, ROWS, ROWS)
        )
        return grouped(*arguments) if fits else plain(*arguments)

    return jax.shard_map(
        local,
        mesh=mesh,
        in_specs=placed,
        out_specs=(P("ka", None, None, "fft", None, None), P("fft", None, None)),
        check_vma=False,
    )
```
